128 devices in a mesh: dp: 16 (over x, y_lo, core), tensor: 8 (over y_hi, z).
Axes of the slice: x: 4, y: 4 (y_hi: 2, y_lo: 2; y = y_hi * 2 + y_lo), z: 4, core: 2. Of those that a mesh axis runs over, the one named last changes fastest.
Arguments:
- tokens: bfloat16 [16384, 1024], P(('dp', 'tensor')), may hold values from -6 to 6
- input_proj: bfloat16 [3, 1024, 1024], P(None, 'dp', 'tensor'), may hold values from -0.25 to 0.25
- output_proj: bfloat16 [1024, 1024], P('tensor', 'dp'), may hold values from -0.75 to 0.75
- expand_proj: bfloat16 [1024, 4096], P('dp', 'tensor'), may hold values from -0.1875 to 0.1875
- contract_proj: bfloat16 [4096, 1024], P('tensor', 'dp'), may hold values from -0.09375 to 0.09375
- head_bias: bfloat16 [2, 8, 128], P(None, 'tensor', 'dp'), may hold values from -3 to 3
- hidden_bias: bfloat16 [8, 512], P('tensor', 'dp'), may hold values from -3 to 3
- norm_gains: bfloat16 [2, 1024], P(None, 'dp'), may hold values from 0.25 to 1.75
- offsets: bfloat16 [4, 1024], P(None, 'dp'), may hold values from -2 to 2
- cotangent: bfloat16 [16384, 1024], P(('dp', 'tensor')), may hold values from -24 to 24
Outputs:
- output: bfloat16 [16384, 1024], P(('dp', 'tensor'))
- grad_tokens: float32 [16384, 1024], P(('dp', 'tensor'))
- grad_input_proj: float32 [3, 1024, 1024], P(None, 'dp', 'tensor')
- grad_output_proj: float32 [1024, 1024], P('tensor', 'dp')
- grad_expand_proj: float32 [1024, 4096], P('dp', 'tensor')
- grad_contract_proj: float32 [4096, 1024], P('tensor', 'dp')
- grad_head_bias: float32 [2, 8, 128], P(None, 'tensor', 'dp')
- grad_hidden_bias: float32 [8, 512], P('tensor', 'dp')
- grad_norm_gains: float32 [2, 1024], P(None, 'dp')
- grad_offsets: float32 [4, 1024], P(None, 'dp')
The draws below stay inside these ranges and needn't reach their ends.
All inputs are finite; a program needn't handle non-finite values.
Results may differ from the reference program's by a relative error of at most 0.03.
Values may be sent and summed in bfloat16 or wider, within the bound.
A program may use at most 128 MiB of HBM per device.

```python
import jax
import jax.numpy as jnp
from jax import lax

D = 1024
H = 16
HD = 64
FF = 4096
SEQ_LEN = 1024
TOKENS = 16384
COL_DEV = 128
HID_DEV = 512
N_TENSOR = 8


def with_spikes(array, key, source, target, shards_of, factor):
    owner, partner = [(jnp.arange(array.shape[dim]) // (array.shape[dim] // shards_of)).reshape([-1 if axis == dim else 1 for axis in range(array.ndim)]) for dim in (source, target)]
    chosen = jax.random.permutation(key, shards_of)[partner]
    strong = (owner == chosen) | (owner == (partner + shards_of // 2) % shards_of)
    return jnp.where(strong, factor * array, array)


def block_scale(stream_key, shape, pieces, low, largest):
    gain, own = 1.0, jax.random.fold_in(stream_key, 6)
    for axis_at, parts in pieces:
        steps = jnp.exp(jax.random.uniform(jax.random.fold_in(own, axis_at), (parts,), jnp.float32, low / len(pieces), largest / len(pieces)))
        gain = gain * jnp.repeat(steps, shape[axis_at] // parts).reshape([-1 if axis == axis_at else 1 for axis in range(len(shape))])
    return gain


def normal_values(rng, extent, deviation, limit, pieces=(), held_as=jnp.bfloat16):
    loudness = block_scale(rng, extent, pieces, -0.22, 0.18) if pieces else 1.0
    drawn = jax.random.normal(rng, extent, jnp.float32) * deviation * loudness
    return jnp.minimum(jnp.maximum(drawn, -limit), limit).astype(held_as)


def noise_with(key, shape, scale, limit, shards, heavy, dtype=jnp.bfloat16):
    values = scale * jax.random.normal(key, shape, jnp.float32)
    if shards:
        values = values * block_scale(key, shape, shards, -0.22, 0.18)
    return jnp.clip(with_spikes(values, jax.random.fold_in(key, 3), *heavy), -limit, limit).astype(dtype)


def setup_inputs(seed: int = 0) -> dict:
    seeds = jax.random.split(jax.random.key(seed), 11)
    tokens = normal_values(seeds[0], (TOKENS, D), 1.0, 6.0, ((0, 128),))
    input_proj = normal_values(seeds[1], (3, D, D), (D // 2) ** -0.5, 0.25, ((1, 16), (2, 8)))
    output_proj = normal_values(seeds[2], (D, D), (D // 16) ** -0.5, 0.75, ((0, 8), (1, 16)))
    expand_proj = normal_values(seeds[3], (D, FF), D ** -0.5, 0.1875, ((0, 16), (1, 8)))
    contract_proj = normal_values(seeds[4], (FF, D), FF ** -0.5, 0.09375, ((0, 8), (1, 16)))
    head_bias = normal_values(seeds[5], (2, N_TENSOR, COL_DEV), 0.5, 3.0, ((1, 8), (2, 16)))
    hidden_bias = normal_values(seeds[6], (N_TENSOR, HID_DEV), 0.5, 3.0, ((0, 8), (1, 16)))
    norm_gains = jnp.clip(1.0 + 0.15 * jax.random.normal(seeds[7], (2, D), jnp.float32), 0.25, 1.75).astype(jnp.bfloat16)
    offsets = normal_values(seeds[8], (4, D), 0.3, 2.0, ((1, 16),))
    cotangent = noise_with(seeds[9], (TOKENS, D), 1.0, 24.0, ((0, 128),), (0, 1, 128, 5.5))
    return {"tokens": tokens, "input_proj": input_proj, "output_proj": output_proj, "expand_proj": expand_proj, "contract_proj": contract_proj, "head_bias": head_bias, "hidden_bias": hidden_bias, "norm_gains": norm_gains, "offsets": offsets, "cotangent": cotangent}


@jax.custom_vjp
def low(v):
    return lax.optimization_barrier(v.astype(jnp.bfloat16)).astype(jnp.float32)

@jax.custom_vjp
def low_back(v):
    return v

def low_keep(v):
    return (low(v), None)

def low_pass(kept, grad):
    return (grad,)

def back_keep(v):
    return (v, None)

def back_low(kept, grad):
    return (low(grad),)
low.defvjp(low_keep, low_pass)
low_back.defvjp(back_keep, back_low)
EPSILON = 1e-05
MASKED = -1000000000.0
GELU_COEF = 0.7978845608028654
CUBIC = 0.044715

def matmul(left, right):
    return jnp.dot(left, right, precision=lax.Precision.HIGHEST, preferred_element_type=jnp.float32)

def gelu_tanh(preact):
    return 0.5 * preact * (1.0 + jnp.tanh(GELU_COEF * (preact + CUBIC * preact * preact * preact)))

def layer_norm(row_values, norm_gain, offset):
    centre = lax.optimization_barrier(jnp.mean(row_values, axis=-1, keepdims=True))
    shifted = row_values - centre
    spread = lax.optimization_barrier(jnp.mean(shifted * shifted, axis=-1, keepdims=True))
    return shifted * lax.rsqrt(spread + EPSILON) * norm_gain + offset

def softmax_rows(scores):
    row_peak = lax.optimization_barrier(jnp.max(scores, axis=-1, keepdims=True))
    exponent = jnp.exp(scores - row_peak)
    return exponent / lax.optimization_barrier(jnp.sum(exponent, axis=-1, keepdims=True))

def sequence_block(params, sequence):
    input_proj, output_proj, expand_proj, contract_proj, head_bias, hidden_bias, norm_gains, offsets = params
    bias_rows = head_bias.reshape(2, D)
    first_norm = low(layer_norm(sequence, norm_gains[0], offsets[0]))
    queries = low(low_back(matmul(first_norm, input_proj[0]) + bias_rows[0]))
    key_rows = low(low_back(matmul(first_norm, input_proj[1])))
    values = low(low_back(matmul(first_norm, input_proj[2]) + bias_rows[1]))
    head_shape = (SEQ_LEN, H, HD)
    raw_scores = jnp.einsum('qhd,khd->hqk', queries.reshape(head_shape), key_rows.reshape(head_shape), precision=lax.Precision.HIGHEST)
    scores = low_back(HD ** (-0.5) * raw_scores)
    allowed = lax.broadcasted_iota(jnp.int32, (SEQ_LEN, SEQ_LEN), 0) >= lax.broadcasted_iota(jnp.int32, (SEQ_LEN, SEQ_LEN), 1)
    scores = jnp.where(allowed[None], scores, MASKED)
    attn_probs = low(softmax_rows(scores))
    mixed = jnp.einsum('hqk,khd->qhd', attn_probs, values.reshape(head_shape), precision=lax.Precision.HIGHEST)
    attended = low(low_back(mixed.reshape(SEQ_LEN, D)))
    branch = low_back(matmul(attended, output_proj) + offsets[1])
    resid = sequence + branch
    second_norm = low(layer_norm(resid, norm_gains[1], offsets[2]))
    preact = low_back(matmul(second_norm, expand_proj) + hidden_bias.reshape(FF))
    hidden = low(gelu_tanh(preact))
    return resid + low_back(matmul(hidden, contract_proj) + offsets[3])

def reference(tokens, input_proj, output_proj, expand_proj, contract_proj, head_bias, hidden_bias, norm_gains, offsets, cotangent):
    params = (input_proj.astype(jnp.float32), output_proj.astype(jnp.float32), expand_proj.astype(jnp.float32), contract_proj.astype(jnp.float32), head_bias.astype(jnp.float32), hidden_bias.astype(jnp.float32), norm_gains.astype(jnp.float32), offsets.astype(jnp.float32))
    token_vals = tokens.astype(jnp.float32)

    def forward(param_set, inputs):
        sequences = inputs.reshape(-1, SEQ_LEN, D)

        def step_one(carried, sequence):
            return (carried, jax.checkpoint(sequence_block)(param_set, sequence))
        _, outputs = lax.scan(step_one, jnp.zeros((), jnp.float32), sequences)
        return outputs.reshape(-1, D)
    output, pull_back = jax.vjp(forward, params, token_vals)
    grad_params, grad_tokens = pull_back(cotangent.astype(jnp.float32))
    return (output.astype(jnp.bfloat16), grad_tokens, grad_params[0], grad_params[1], grad_params[2], grad_params[3], grad_params[4], grad_params[5], grad_params[6], grad_params[7])
```

```python
import functools

import jax
import jax.numpy as jnp
from jax import lax
from jax.experimental import pallas as pl
from jax.experimental.pallas import tpu as pltpu
from jax.sharding import Mesh
from jax.sharding import PartitionSpec as P

F32, BF16 = jnp.float32, jnp.bfloat16
MESH = pl.DeviceIdType.MESH
DP = ("x", "yl", "c")
TENSOR = ("yh", "z")
EPSILON = 1e-05
MASKED = -1000000000.0
GELU_COEF = 0.7978845608028654
CUBIC = 0.044715
SCALE = 64 ** (-0.5)
N_SEMS = 340


def nn(a, b):
    return lax.dot_general(a, b, (((1,), (0,)), ((), ())), preferred_element_type=F32)


def nt(a, b):
    return lax.dot_general(a, b, (((1,), (1,)), ((), ())), preferred_element_type=F32)


def tn(a, b):
    return lax.dot_general(a, b, (((0,), (0,)), ((), ())), preferred_element_type=F32)


def rows(start, size, by=None):
    if isinstance(start, int):
        return pl.ds(start, size)
    return pl.ds(pl.multiple_of(start, by or size), size)


def norm_rows(v):
    shifted = v - jnp.mean(v, axis=-1, keepdims=True)
    inverse = lax.rsqrt(jnp.mean(shifted * shifted, axis=-1, keepdims=True) + EPSILON)
    return shifted * inverse, inverse


def norm_back(grad, normed, inverse, gain):
    scaled = grad * gain
    first = jnp.mean(scaled, axis=-1, keepdims=True)
    second = jnp.mean(scaled * normed, axis=-1, keepdims=True)
    return inverse * (scaled - first - normed * second)


class Links:
    def __init__(self, send_sems, recv_sems):
        self.send_sems, self.recv_sems = send_sems, recv_sems
        self.sent, self.received, self.open = 0, 0, []

    def slots(self, count):
        first = self.received
        self.received += count
        assert self.received <= N_SEMS
        return first

    def make(self, src, dst, recv, to):
        copy = pltpu.make_async_remote_copy(
            src_ref=src,
            dst_ref=dst,
            send_sem=self.send_sems.at[self.sent],
            recv_sem=self.recv_sems.at[recv],
            device_id=to,
            device_id_type=MESH,
        )
        self.sent += 1
        assert self.sent <= N_SEMS
        return copy

    def send(self, src, dst, recv, to):
        copy = self.make(src, dst, recv, to)
        copy.start()
        self.open.append((None, copy))

    def send_if(self, cond, src, dst, recv, to):
        copy = self.make(src, dst, recv, to)
        pl.when(cond)(copy.start)
        self.open.append((cond, copy))

    def local_if(self, cond, src, dst, recv):
        copy = pltpu.make_async_copy(src, dst, self.recv_sems.at[recv])
        pl.when(cond)(copy.start)

    def wait(self, recv, ref, to):
        pltpu.make_async_remote_copy(
            src_ref=ref,
            dst_ref=ref,
            send_sem=self.send_sems.at[0],
            recv_sem=self.recv_sems.at[recv],
            device_id=to,
            device_id_type=MESH,
        ).wait_recv()

    def drain(self):
        for cond, copy in self.open:
            if cond is None:
                copy.wait_send()
            else:
                pl.when(cond)(copy.wait_send)
        self.open = []


class Ring:
    def __init__(self, links, axis, pos):
        self.links, self.axis = links, axis
        self.pos = pos
        self.right, self.left, self.far = (lax.rem(pos + k, 4) for k in (1, 3, 2))
        self.to_right, self.to_left = {axis: self.right}, {axis: self.left}


class RingGather:
    def __init__(self, ring, buf, offset, half, partner=None, offset_partner=None):
        self.ring, self.buf, self.offset, self.half = ring, buf, offset, half
        self.partner, self.offset_partner = partner, offset_partner
        self.ids = ring.links.slots(6)
        if partner is not None:
            self.pids = ring.links.slots(8)

    def at(self, pos, part, offset=None):
        return self.buf.at[rows((offset or self.offset)(pos) + part * self.half, self.half)]

    def relay(self, pos, part, slot):
        if self.partner is not None:
            ref = self.at(pos, part)
            self.ring.links.send(ref, ref, self.pids + slot, self.partner)

    def start(self):
        r, s = self.ring, self.ring.links.send
        a, b = self.at(r.pos, 0), self.at(r.pos, 1)
        s(a, a, self.ids + 0, r.to_right)
        s(b, b, self.ids + 3, r.to_left)
        s(b, b, self.ids + 1, r.to_right)
        s(a, a, self.ids + 2, r.to_left)
        self.relay(r.pos, 0, 0)
        self.relay(r.pos, 1, 1)

    def forward(self):
        r, s, w = self.ring, self.ring.links.send, self.ring.links.wait
        ref = self.at(r.left, 0)
        w(self.ids + 0, ref, r.to_left)
        s(ref, ref, self.ids + 4, r.to_right)
        ref = self.at(r.right, 1)
        w(self.ids + 3, ref, r.to_right)
        s(ref, ref, self.ids + 5, r.to_left)
        self.relay(r.left, 0, 2)
        self.relay(r.right, 1, 5)

    def done(self):
        r, w = self.ring, self.ring.links.wait
        w(self.ids + 1, self.at(r.left, 1), r.to_left)
        self.relay(r.left, 1, 3)
        w(self.ids + 2, self.at(r.right, 0), r.to_right)
        self.relay(r.right, 0, 4)
        w(self.ids + 4, self.at(r.far, 0), r.to_left)
        self.relay(r.far, 0, 6)
        w(self.ids + 5, self.at(r.far, 1), r.to_right)
        self.relay(r.far, 1, 7)
        if self.partner is not None:
            order = ((r.pos, 0), (r.pos, 1), (r.left, 0), (r.left, 1))
            order += ((r.right, 0), (r.right, 1), (r.far, 0), (r.far, 1))
            for slot, (pos, part) in enumerate(order):
                w(self.pids + slot, self.at(pos, part, self.offset_partner), self.partner)


class RingSum:
    def __init__(self, ring, buf, offset, half, land):
        self.ring, self.buf, self.offset, self.half, self.land = ring, buf, offset, half, land
        self.ids = ring.links.slots(6)

    def at(self, pos, part, count=1):
        return self.buf.at[rows(self.offset(pos) + part * self.half, self.half * count, self.half)]

    def landing(self, slot):
        return self.land.at[pl.ds(slot * self.half, self.half)]

    def send(self, src, slot, to):
        self.ring.links.send(src, self.landing(slot), self.ids + slot, to)

    def wait(self, slot, to):
        self.ring.links.wait(self.ids + slot, self.landing(slot), to)

    def add(self, pos, part, slot):
        ref = self.at(pos, part)
        ref[...] = (ref[...].astype(F32) + self.landing(slot)[...].astype(F32)).astype(BF16)

    def send_far(self):
        r = self.ring
        self.send(self.at(r.far, 0), 0, r.to_right)
        self.send(self.at(r.far, 1), 1, r.to_left)

    def send_near(self):
        r = self.ring
        self.send(self.at(r.right, 1), 3, r.to_right)
        self.send(self.at(r.left, 0), 4, r.to_left)

    def middle(self):
        r = self.ring
        self.wait(0, r.to_left)
        self.add(r.right, 0, 0)
        self.send(self.at(r.right, 0), 2, r.to_right)
        self.wait(1, r.to_right)
        self.add(r.left, 1, 1)
        self.send(self.at(r.left, 1), 5, r.to_left)

    def total(self):
        r = self.ring
        self.wait(3, r.to_left)
        self.wait(4, r.to_right)
        self.wait(2, r.to_left)
        self.wait(5, r.to_right)
        own = self.at(r.pos, 0, 2)[...].astype(F32)
        left = self.land[pl.ds(2 * self.half, 2 * self.half)].astype(F32)
        right = self.land[pl.ds(4 * self.half, 2 * self.half)].astype(F32)
        return own + left + right


class GroupSum:
    def __init__(self, ring, c, buf, from_core, land):
        self.links, self.c, self.buf, self.from_core = ring.links, c, buf, from_core
        self.partner = {"c": 1 - c}
        self.order = (ring.far, ring.right, ring.left, ring.pos)
        self.ids = ring.links.slots(4)
        self.sum = RingSum(ring, buf, lambda p: c * 512 + p * 128, 64, land)

    def core_send(self):
        for k, pos in enumerate(self.order):
            src = self.buf.at[rows((1 - self.c) * 512 + pos * 128, 128)]
            dst = self.from_core.at[rows(pos * 128, 128)]
            self.links.send(src, dst, self.ids + k, self.partner)

    def core_add(self, k):
        got = self.from_core.at[rows(self.order[k] * 128, 128)]
        self.links.wait(self.ids + k, got, self.partner)
        ref = self.buf.at[rows(self.c * 512 + self.order[k] * 128, 128)]
        ref[...] = (ref[...].astype(F32) + got[...].astype(F32)).astype(BF16)

    def start(self):
        self.core_add(0)
        self.sum.send_far()
        self.core_add(1)
        self.core_add(2)
        self.sum.send_near()

    def middle(self):
        self.sum.middle()
        self.core_add(3)

    def total(self):
        return self.sum.total()


class WeightGather:
    def __init__(self, ring, me, buf, size, shard):
        self.ring, self.me, self.buf, self.size, self.shard = ring, me, buf, size, shard
        self.ids = ring.links.slots(4)
        self.gather = RingGather(ring, buf, lambda p: p * 4 * size, 2 * size)

    def start(self):
        x, yl, c, yh, z = self.me
        links = self.ring.links
        own = self.buf.at[rows((x * 4 + yl * 2 + c) * self.size, self.size)]
        slot = self.ids + yl * 2 + c
        for dl, dh in ((1, 0), (0, 1), (1, 1)):
            to = {"yl": lax.rem(yl + dl, 2), "yh": lax.rem(yh + dh, 2), "c": yh}
            links.send(self.shard, own, slot, to)
        links.local_if(c == yh, self.shard, own, slot)
        links.send_if(c != yh, self.shard, own, slot, {"c": yh})

    def start_x(self):
        x, yl, c, yh, z = self.me
        for k in range(4):
            ref = self.buf.at[rows((x * 4 + k) * self.size, self.size)]
            self.ring.links.wait(self.ids + k, ref, {"c": 1 - c})
        self.gather.start()


class WeightSum:
    def __init__(self, ring, me, buf, size, land, land_y):
        self.ring, self.me, self.buf, self.size = ring, me, buf, size
        self.land_y = land_y
        self.sum = RingSum(ring, buf, lambda p: p * 4 * size, 2 * size, land)
        self.ids = ring.links.slots(4)

    def start(self):
        self.sum.send_far()
        self.sum.send_near()

    def middle(self):
        self.sum.middle()

    def start_y(self):
        x, yl, c, yh, z = self.me
        links, size = self.ring.links, self.size
        total = self.sum.total()
        self.buf[rows(x * 4 * size, 4 * size)] = total.astype(BF16)
        slot = yh * 2 + yl
        dst = self.land_y.at[rows(slot * size, size)]
        for dl, dc in ((1, 0), (0, 1), (1, 1), (0, 0)):
            to_l, to_c = lax.rem(yl + dl, 2), lax.rem(c + dc, 2)
            src = self.buf.at[rows((x * 4 + to_l * 2 + to_c) * size, size)]
            if dl or dc:
                links.send(src, dst, self.ids + slot, {"yl": to_l, "c": to_c, "yh": c})
            else:
                links.local_if(c == yh, src, dst, self.ids + slot)
                links.send_if(c != yh, src, dst, self.ids + slot, {"yh": c})

    def finish(self):
        c = self.me[2]
        total = 0.0
        for k in range(4):
            ref = self.land_y.at[pl.ds(k * self.size, self.size)]
            self.ring.links.wait(self.ids + k, ref, {"c": 1 - c})
            total = total + ref[...].astype(F32)
        return total


def layer_kernel(
    tok_ref, cot_ref, wi_ref, wo_ref, we_ref, wc_ref, sm_ref,
    out_ref, gtok_ref, gwi_ref, gwo_ref, gwe_ref, gwc_ref, gsm_ref,
    xg, cotg, h1, h2, gbg, wi, wo, we, wc, sm, gi, go, ge, gc, gs,
    land_i, land_o, land_e, land_c, land_s, landy_i, landy_o, landy_e, landy_c, landy_s,
    part_b, part_o, part_2, part_1, core_b, core_o, core_2, core_1, near_b, near_o, near_2, near_1,
    qkv, gqkv, kvr, gkv_out, gkv_in, att, gatt, hid, gp, lse, dk_acc, dv_acc, dk0_acc, dv0_acc,
    resid, gres, vec, tens, hb_sum, send_sems, recv_sems,
):
    x, yl, c, yh, z = me = tuple(lax.axis_index(a) for a in ("x", "yl", "c", "yh", "z"))
    links = Links(send_sems, recv_sems)
    ring_z, ring_x = Ring(links, "z", z), Ring(links, "x", x)
    partner = {"c": 1 - c}

    def block(p):
        return c * 512 + p * 128

    def block_partner(p):
        return (1 - c) * 512 + p * 128

    barrier = pltpu.get_barrier_semaphore()
    peers = [{"x": ring_x.right}, {"x": ring_x.left}]
    for dh in range(2):
        for dz in range(4):
            if dh or dz:
                peers.append({"yh": lax.rem(yh + dh, 2), "z": lax.rem(z + dz, 4)})
    for dl in range(2):
        for dc in range(2):
            for dh in range(2):
                if dl or dc:
                    peers.append({"yl": lax.rem(yl + dl, 2), "c": lax.rem(c + dc, 2), "yh": lax.rem(yh + dh, 2)})
    for peer in peers:
        pl.semaphore_signal(barrier, inc=1, device_id=peer, device_id_type=MESH)
    own = rows(block(z), 128)
    xg[own] = tok_ref[...]
    cotg[own] = cot_ref[...]
    pl.semaphore_wait(barrier, len(peers))

    gather_x = RingGather(ring_z, xg, block, 64, partner, block_partner)
    gather_x.start()
    w_sm = WeightGather(ring_x, me, sm, 16, sm_ref)
    w_i = WeightGather(ring_x, me, wi, 64, wi_ref)
    w_o = WeightGather(ring_x, me, wo, 64, wo_ref)
    w_e = WeightGather(ring_x, me, we, 64, we_ref)
    w_c = WeightGather(ring_x, me, wc, 64, wc_ref)
    for w in (w_sm, w_i, w_o, w_e, w_c):
        w.start()
    w_sm.start_x()
    w_i.start_x()
    gather_x.forward()
    w_sm.gather.forward()
    w_i.gather.forward()
    gather_x.done()
    gather_c = RingGather(ring_z, cotg, block, 64, partner, block_partner)
    gather_c.start()
    w_sm.gather.done()

    tiles = [sm[pl.ds(16 * k, 16)].astype(F32) for k in range(16)]
    pairs = [tiles[2 * k] + tiles[2 * k + 1] for k in range(8)]
    vectors = jnp.concatenate(pairs, axis=1)
    gains, offs = vectors[0:2], vectors[2:6]
    fours = [pairs[2 * k] + pairs[2 * k + 1] for k in range(4)]
    hidden_bias = jnp.concatenate([f[6:7] for f in fours], axis=1)
    every = fours[0] + fours[1] + fours[2] + fours[3]
    qkv_bias = jnp.concatenate([every[7:8], jnp.zeros((1, 128), F32), every[8:9]], axis=1)
    gain1, gain2 = gains[0:1], gains[1:2]
    off0, off1, off2, off3 = (offs[k : k + 1] for k in range(4))

    w_i.gather.done()

    @pl.loop(0, 4)
    def _(i):
        r = rows(i * 256, 256)
        normed, _ = norm_rows(xg[r].astype(F32))
        low = (normed * gain1 + off0).astype(BF16)
        h1[r] = low
        qkv[r] = (nn(low, wi[...]) + qkv_bias).astype(BF16)

    kv_slot = links.slots(1)
    links.send_if(yh == 0, qkv.at[:, pl.ds(128, 256)], kvr, kv_slot, {"yh": 1})
    w_o.start_x()
    w_e.start_x()
    w_c.start_x()
    gather_c.forward()

    lane = lax.broadcasted_iota(jnp.int32, (1, 128), 1)
    head_lanes = [lane < 64, lane >= 64]

    def causal(scores, first):
        r = lax.broadcasted_iota(jnp.int32, scores.shape, 0) + first
        return jnp.where(r >= lax.broadcasted_iota(jnp.int32, scores.shape, 1), scores, MASKED)

    def masked(value, h):
        return jnp.where(head_lanes[h], value, jnp.zeros_like(value))

    def attend(remote):
        @pl.loop(0, 2)
        def _(s):
            for qb in range(2):
                nk = 256 * (qb + 1)
                r = rows(s * 512 + qb * 256, 256)
                keys = rows(s * 512, nk, 512)
                q, k, v = qkv[r, 0:128], qkv[keys, 128:256], qkv[keys, 256:384]
                outs = []
                for h in range(2):
                    qm = masked(q, h)
                    near = causal(nt(qm, k) * SCALE, qb * 256)
                    peak = jnp.max(near, axis=-1, keepdims=True)
                    if remote:
                        all_keys = rows(s * 512, 512)
                        far = nt(qm, kvr[all_keys, 0:128]) * SCALE
                        peak = jnp.maximum(peak, jnp.max(far, axis=-1, keepdims=True))
                        far = jnp.exp(far - peak)
                    near = jnp.exp(near - peak)
                    total = jnp.sum(near, axis=-1, keepdims=True)
                    if remote:
                        total = total + jnp.sum(far, axis=-1, keepdims=True)
                    inverse = 1.0 / total
                    o = nn((near * inverse).astype(BF16), v)
                    if remote:
                        o = o + nn((far * inverse).astype(BF16), kvr[all_keys, 128:256])
                    outs.append(o)
                    lse[h, r] = peak + jnp.log(total)
                att[r] = jnp.where(head_lanes[0], outs[0], outs[1]).astype(BF16)

    pl.when(yh == 0)(functools.partial(attend, False))

    @pl.when(yh == 1)
    def _():
        links.wait(kv_slot, kvr, {"yh": 0})
        attend(True)

    w_o.gather.forward()
    w_o.gather.done()

    def halves(body):
        def run(who):
            @pl.loop(0, 2)
            def _(i):
                body(rows(who * 512 + i * 256, 256))

        return run

    @halves
    def branch_tile(r):
        part_b[r] = nt(att[r], wo[...]).astype(BF16)

    sum_b = GroupSum(ring_z, c, part_b, core_b, near_b)
    branch_tile(1 - c)
    sum_b.core_send()
    branch_tile(c)
    gather_c.done()
    sum_b.start()
    w_e.gather.forward()
    w_c.gather.forward()
    sum_b.middle()
    x_own = tok_ref[...].astype(F32)
    resid[...] = x_own + sum_b.total() + off1
    normed2, inverse2 = norm_rows(resid[...])
    h2[own] = (normed2 * gain2 + off2).astype(BF16)
    gather_h = RingGather(ring_z, h2, block, 64, partner, block_partner)
    gather_h.start()
    w_e.gather.done()
    w_c.gather.done()
    gather_h.forward()
    gather_h.done()

    hb_sum[...] = jnp.zeros_like(hb_sum)

    @halves
    def mlp_tile(r):
        p = nn(h2[r], we[...]) + hidden_bias
        square = p * p
        t = jnp.tanh(GELU_COEF * (p + CUBIC * p * square))
        hid[r] = (0.5 * p * (1.0 + t)).astype(BF16)
        slope = 0.5 * (1.0 + t) + 0.5 * p * (1.0 - t * t) * (GELU_COEF * (1.0 + 3.0 * CUBIC * square))
        g = (nn(cotg[r], wc[...]) * slope).astype(BF16)
        gp[r] = g
        hb_sum[...] += jnp.sum(g.astype(F32), axis=0, keepdims=True)
        part_2[r] = nt(g, we[...]).astype(BF16)

    sum_2 = GroupSum(ring_z, c, part_2, core_2, near_2)
    mlp_tile(1 - c)
    sum_2.core_send()
    mlp_tile(c)
    sum_2.start()

    def weight_grad(out, left, right):
        @pl.loop(0, 4)
        def _(i):
            r = rows(i * 256, 256)
            out[r] = tn(left[:, r], right[...]).astype(BF16)

    g_e = WeightSum(ring_x, me, ge, 64, land_e, landy_e)
    g_c = WeightSum(ring_x, me, gc, 64, land_c, landy_c)
    weight_grad(ge, h2, gp)
    g_e.start()
    sum_2.middle()
    weight_grad(gc, cotg, hid)
    g_c.start()

    grad2 = sum_2.total()
    cot_own = cot_ref[...].astype(F32)
    gres[...] = cot_own + norm_back(grad2, normed2, inverse2, gain2)
    grad_branch = gres[...].astype(BF16)
    gbg[own] = grad_branch
    gather_b = RingGather(ring_z, gbg, block, 64, partner, block_partner)
    gather_b.start()
    vec[1:2] = jnp.sum(grad2 * normed2, axis=0, keepdims=True)
    vec[3:4] = jnp.sum(grad_branch.astype(F32), axis=0, keepdims=True)
    vec[4:5] = jnp.sum(grad2, axis=0, keepdims=True)
    vec[5:6] = jnp.sum(cot_own, axis=0, keepdims=True)
    g_e.middle()

    @halves
    def out_tile(r):
        part_o[r] = nt(hid[r], wc[...]).astype(BF16)

    sum_o = GroupSum(ring_z, c, part_o, core_o, near_o)
    gather_b.forward()
    out_tile(1 - c)
    sum_o.core_send()
    out_tile(c)
    gather_b.done()
    sum_o.start()

    @pl.loop(0, 4)
    def _(i):
        r = rows(i * 256, 256)
        gatt[r] = nn(gbg[r], wo[...]).astype(BF16)

    gkv_slot = links.slots(1)

    def attend_back(remote):
        @pl.loop(0, 2)
        def _(s):
            dk_acc[...] = jnp.zeros_like(dk_acc)
            dv_acc[...] = jnp.zeros_like(dv_acc)
            if remote:
                dk0_acc[...] = jnp.zeros_like(dk0_acc)
                dv0_acc[...] = jnp.zeros_like(dv0_acc)
            seq = rows(s * 512, 512)
            for qb in range(2):
                nk = 256 * (qb + 1)
                r = rows(s * 512 + qb * 256, 256)
                keys = rows(s * 512, nk, 512)
                q, k, v, g = qkv[r, 0:128], qkv[keys, 128:256], qkv[keys, 256:384], gatt[r]
                outs = []
                for h in range(2):
                    qm, gm, sums = masked(q, h), masked(g, h), lse[h, r]
                    near = jnp.exp(causal(nt(qm, k) * SCALE, qb * 256) - sums)
                    near_g = nt(gm, v)
                    dot = jnp.sum(near * near_g, axis=-1, keepdims=True)
                    if remote:
                        k0, v0 = kvr[seq, 0:128], kvr[seq, 128:256]
                        far = jnp.exp(nt(qm, k0) * SCALE - sums)
                        far_g = nt(gm, v0)
                        dot = dot + jnp.sum(far * far_g, axis=-1, keepdims=True)
                        far_s = (far * (far_g - dot)).astype(BF16)
                        dk0_acc[...] += tn(far_s, qm)
                        dv0_acc[...] += tn(far.astype(BF16), gm)
                    near_s = (near * (near_g - dot)).astype(BF16)
                    dk_acc[0:nk] += tn(near_s, qm)
                    dv_acc[0:nk] += tn(near.astype(BF16), gm)
                    o = nn(near_s, k)
                    if remote:
                        o = o + nn(far_s, k0)
                    outs.append(o)
                gqkv[r, 0:128] = (jnp.where(head_lanes[0], outs[0], outs[1]) * SCALE).astype(BF16)
            gqkv[seq, 128:256] = (dk_acc[...] * SCALE).astype(BF16)
            gqkv[seq, 256:384] = dv_acc[...].astype(BF16)
            if remote:
                gkv_out[seq, 0:128] = (dk0_acc[...] * SCALE).astype(BF16)
                gkv_out[seq, 128:256] = dv0_acc[...].astype(BF16)

    pl.when(yh == 0)(functools.partial(attend_back, False))
    pl.when(yh == 1)(functools.partial(attend_back, True))
    links.send_if(yh == 1, gkv_out, gkv_in, gkv_slot, {"yh": 0})
    sum_o.middle()
    g_c.middle()
    g_e.start_y()
    out_ref[...] = (resid[...] + sum_o.total() + off3).astype(BF16)
    weight_grad(go, gbg, att)
    g_o = WeightSum(ring_x, me, go, 64, land_o, landy_o)
    g_o.start()

    @pl.when(yh == 0)
    def _():
        links.wait(gkv_slot, gkv_in, {"yh": 1})
        for k in range(4):
            r = pl.ds(k * 256, 256)
            gqkv[r, 128:384] = (gqkv[r, 128:384].astype(F32) + gkv_in[r].astype(F32)).astype(BF16)

    @halves
    def grad1_tile(r):
        part_1[r] = nt(gqkv[r], wi[...]).astype(BF16)

    sum_1 = GroupSum(ring_z, c, part_1, core_1, near_1)
    grad1_tile(1 - c)
    sum_1.core_send()
    grad1_tile(c)
    sum_1.start()
    weight_grad(gi, h1, gqkv)
    g_i = WeightSum(ring_x, me, gi, 64, land_i, landy_i)
    g_i.start()
    g_c.start_y()
    g_o.middle()
    sum_1.middle()
    head_sums = jnp.sum(gqkv[...].astype(F32), axis=0, keepdims=True)
    normed1, inverse1 = norm_rows(x_own)
    grad1 = sum_1.total()
    vec[0:1] = jnp.sum(grad1 * normed1, axis=0, keepdims=True)
    vec[2:3] = jnp.sum(grad1, axis=0, keepdims=True)
    hb = hb_sum[...]
    vec[6:7] = jnp.concatenate([hb[:, 128 * (k // 2) : 128 * (k // 2) + 128] for k in range(8)], axis=1)
    vec[7:8] = jnp.concatenate([head_sums[:, 0:128]] * 8, axis=1)
    vec[8:9] = jnp.concatenate([head_sums[:, 256:384]] * 8, axis=1)
    vec[9:16] = jnp.zeros((7, 1024), F32)
    for k in range(16):
        gs[pl.ds(16 * k, 16)] = vec[:, 128 * (k // 2) : 128 * (k // 2) + 128].astype(BF16)
    g_s = WeightSum(ring_x, me, gs, 16, land_s, landy_s)
    g_s.start()
    gtok_ref[...] = gres[...] + norm_back(grad1, normed1, inverse1, gain1)
    g_s.middle()
    g_i.middle()
    g_s.start_y()
    g_o.start_y()
    g_i.start_y()
    tile = g_s.finish()
    slot = yh * 4 + z
    tens[rows(slot * 16, 16)] = tile
    mine = tens.at[rows(slot * 16, 16)]
    t_ids = links.slots(8)
    others = [(dh, dz) for dh in range(2) for dz in range(4) if dh or dz]
    for dh, dz in others:
        links.send(mine, mine, t_ids + slot, {"yh": lax.rem(yh + dh, 2), "z": lax.rem(z + dz, 4)})
    gwe_ref[...] = g_e.finish()
    gwc_ref[...] = g_c.finish()
    gwo_ref[...] = g_o.finish()
    gwi_ref[...] = g_i.finish()
    for dh, dz in others:
        theirs = lax.rem(yh + dh, 2) * 4 + lax.rem(z + dz, 4)
        ref = tens.at[rows(theirs * 16, 16)]
        links.wait(t_ids + theirs, ref, {"yh": lax.rem(yh + dh, 2), "z": lax.rem(z + dz, 4)})
    total = tens[0:16]
    for k in range(1, 8):
        total = total + tens[16 * k : 16 * k + 16]
    gsm_ref[0:6] = total[0:6]
    gsm_ref[6:16] = tile[6:16]
    links.drain()


def on_lanes(value, lane0, width):
    padded = jnp.zeros((value.shape[0], width), value.dtype)
    return lax.dynamic_update_slice(padded, value, (0, lane0))


def per_device(tokens, input_proj, output_proj, expand_proj, contract_proj, head_bias, hidden_bias, norm_gains, offsets, cotangent):
    c = lax.axis_index("c")
    dp = lax.axis_index("x") * 4 + lax.axis_index("yl") * 2 + c
    sm = jnp.concatenate(
        [
            on_lanes(jnp.concatenate([norm_gains, offsets], axis=0), c * 64, 128),
            on_lanes(hidden_bias, lax.rem(dp, 4) * 32, 128),
            on_lanes(head_bias[:, 0, :], dp * 8, 128),
            jnp.zeros((7, 128), BF16),
        ],
        axis=0,
    )
    wi = jnp.swapaxes(input_proj, 0, 1).reshape(64, 384)
    vmem = pl.BlockSpec(memory_space=pltpu.VMEM)
    shape = jax.ShapeDtypeStruct
    widths = (384, 128, 512, 512)

    def buf(r, n, t=BF16):
        return pltpu.VMEM((r, n), t)

    scratch = [buf(1024, 1024) for _ in range(5)]
    scratch += [buf(1024, n) for n in widths] + [buf(256, 128)]
    scratch += [buf(1024, n) for n in widths] + [buf(256, 128)]
    scratch += [buf(768, n) for n in widths] + [buf(192, 128)]
    scratch += [buf(256, n) for n in widths] + [buf(64, 128)]
    scratch += [buf(1024, 1024) for _ in range(4)] + [buf(512, 1024) for _ in range(4)]
    scratch += [buf(384, 1024) for _ in range(4)]
    scratch += [buf(1024, 384), buf(1024, 384), buf(1024, 256), buf(1024, 256), buf(1024, 256)]
    scratch += [buf(1024, 128), buf(1024, 128), buf(1024, 512), buf(1024, 512)]
    scratch += [pltpu.VMEM((2, 1024, 1), F32)] + [buf(512, 128, F32) for _ in range(4)]
    scratch += [buf(128, 1024, F32), buf(128, 1024, F32), buf(16, 1024, F32), buf(128, 128, F32)]
    scratch += [buf(1, 512, F32)]
    scratch += [pltpu.SemaphoreType.DMA((N_SEMS,)), pltpu.SemaphoreType.DMA((N_SEMS,))]
    out, gtok, gwi, gwo, gwe, gwc, gsm = pl.pallas_call(
        layer_kernel,
        out_shape=(
            shape((128, 1024), BF16),
            shape((128, 1024), F32),
            *(shape((64, n), F32) for n in widths),
            shape((16, 128), F32),
        ),
        in_specs=[vmem] * 7,
        out_specs=[vmem] * 7,
        scratch_shapes=scratch,
        compiler_params=pltpu.CompilerParams(
            collective_id=0, has_side_effects=True, vmem_limit_bytes=58 * 1024 * 1024
        ),
    )(tokens, cotangent, wi, output_proj.T, expand_proj, contract_proj.T, sm)
    grad_input = jnp.swapaxes(gwi.reshape(64, 3, 128), 0, 1)
    mine = lax.dynamic_slice(gsm, (0, c * 64), (6, 64))
    grad_hidden = lax.dynamic_slice(gsm, (6, lax.rem(dp, 4) * 32), (1, 32))
    grad_head = lax.dynamic_slice(gsm, (7, dp * 8), (2, 8))[:, None, :]
    return (out, gtok, grad_input, gwo.T, gwe, gwc.T, grad_head, grad_hidden, mine[0:2], mine[2:6])


def solution(mesh):
    split = Mesh(mesh.devices.reshape(4, 2, 2, 2, 4), ("x", "yl", "c", "yh", "z"))
    token_rows = P(DP + TENSOR, None)
    weights = (
        P(None, DP, TENSOR),
        P(TENSOR, DP),
        P(DP, TENSOR),
        P(TENSOR, DP),
        P(None, TENSOR, DP),
        P(TENSOR, DP),
        P(None, DP),
        P(None, DP),
    )
    return jax.shard_map(
        per_device,
        mesh=split,
        in_specs=(token_rows, *weights, token_rows),
        out_specs=(token_rows, token_rows, *weights),
        check_vma=False,
    )
```

```python
import functools

import jax
import jax.numpy as jnp
from jax import lax
from jax.experimental import pallas as pl
from jax.experimental.pallas import tpu as pltpu
from jax.sharding import Mesh
from jax.sharding import PartitionSpec as P

F32, BF16 = jnp.float32, jnp.bfloat16
MESH = pl.DeviceIdType.MESH
DP = ("x", "yl", "c")
TENSOR = ("yh", "z")
EPSILON = 1e-05
MASKED = -1000000000.0
GELU_COEF = 0.7978845608028654
CUBIC = 0.044715
SCALE = 64 ** (-0.5)
N_SEMS = 340


def nn(a, b):
    return lax.dot_general(a, b, (((1,), (0,)), ((), ())), preferred_element_type=F32)


def nt(a, b):
    return lax.dot_general(a, b, (((1,), (1,)), ((), ())), preferred_element_type=F32)


def tn(a, b):
    return lax.dot_general(a, b, (((0,), (0,)), ((), ())), preferred_element_type=F32)


def rows(start, size, by=None):
    if isinstance(start, int):
        return pl.ds(start, size)
    return pl.ds(pl.multiple_of(start, by or size), size)


def norm_rows(v):
    shifted = v - jnp.mean(v, axis=-1, keepdims=True)
    inverse = lax.rsqrt(jnp.mean(shifted * shifted, axis=-1, keepdims=True) + EPSILON)
    return shifted * inverse, inverse


def norm_back(grad, normed, inverse, gain):
    scaled = grad * gain
    first = jnp.mean(scaled, axis=-1, keepdims=True)
    second = jnp.mean(scaled * normed, axis=-1, keepdims=True)
    return inverse * (scaled - first - normed * second)


class Links:
    def __init__(self, send_sems, recv_sems):
        self.send_sems, self.recv_sems = send_sems, recv_sems
        self.sent, self.received, self.open = 0, 0, []

    def outgoing(self, count):
        first = self.sent
        self.sent += count
        assert self.sent <= N_SEMS
        return first

    def slots(self, count):
        first = self.received
        self.received += count
        assert self.received <= N_SEMS
        return first

    def make(self, src, dst, recv, to):
        copy = pltpu.make_async_remote_copy(
            src_ref=src,
            dst_ref=dst,
            send_sem=self.send_sems.at[self.sent],
            recv_sem=self.recv_sems.at[recv],
            device_id=to,
            device_id_type=MESH,
        )
        self.sent += 1
        assert self.sent <= N_SEMS
        return copy

    def send(self, src, dst, recv, to):
        copy = self.make(src, dst, recv, to)
        copy.start()
        self.open.append((None, copy))

    def send_if(self, cond, src, dst, recv, to):
        copy = self.make(src, dst, recv, to)
        pl.when(cond)(copy.start)
        self.open.append((cond, copy))

    def local_if(self, cond, src, dst, recv):
        copy = pltpu.make_async_copy(src, dst, self.recv_sems.at[recv])
        pl.when(cond)(copy.start)

    def wait(self, recv, ref, to):
        pltpu.make_async_remote_copy(
            src_ref=ref,
            dst_ref=ref,
            send_sem=self.send_sems.at[0],
            recv_sem=self.recv_sems.at[recv],
            device_id=to,
            device_id_type=MESH,
        ).wait_recv()

    def drain(self):
        for cond, copy in self.open:
            if cond is None:
                copy.wait_send()
            else:
                pl.when(cond)(copy.wait_send)
        self.open = []


class Ring:
    def __init__(self, links, axis, pos):
        self.links, self.axis = links, axis
        self.pos = pos
        self.right, self.left, self.far = (lax.rem(pos + k, 4) for k in (1, 3, 2))
        self.to_right, self.to_left = {axis: self.right}, {axis: self.left}


class RingGather:
    def __init__(self, ring, buf, offset, half, partner=None, offset_partner=None):
        self.ring, self.buf, self.offset, self.half = ring, buf, offset, half
        self.partner, self.offset_partner = partner, offset_partner
        self.ids = ring.links.slots(6)
        if partner is not None:
            self.pids = ring.links.slots(8)

    def at(self, pos, part, offset=None):
        return self.buf.at[rows((offset or self.offset)(pos) + part * self.half, self.half)]

    def relay(self, pos, part, slot):
        if self.partner is not None:
            ref = self.at(pos, part)
            self.ring.links.send(ref, ref, self.pids + slot, self.partner)

    def start(self):
        r, s = self.ring, self.ring.links.send
        a, b = self.at(r.pos, 0), self.at(r.pos, 1)
        s(a, a, self.ids + 0, r.to_right)
        s(b, b, self.ids + 3, r.to_left)
        s(b, b, self.ids + 1, r.to_right)
        s(a, a, self.ids + 2, r.to_left)
        self.relay(r.pos, 0, 0)
        self.relay(r.pos, 1, 1)

    def forward(self):
        r, s, w = self.ring, self.ring.links.send, self.ring.links.wait
        ref = self.at(r.left, 0)
        w(self.ids + 0, ref, r.to_left)
        s(ref, ref, self.ids + 4, r.to_right)
        ref = self.at(r.right, 1)
        w(self.ids + 3, ref, r.to_right)
        s(ref, ref, self.ids + 5, r.to_left)
        self.relay(r.left, 0, 2)
        self.relay(r.right, 1, 5)

    def done(self):
        r, w = self.ring, self.ring.links.wait
        w(self.ids + 1, self.at(r.left, 1), r.to_left)
        self.relay(r.left, 1, 3)
        w(self.ids + 2, self.at(r.right, 0), r.to_right)
        self.relay(r.right, 0, 4)
        w(self.ids + 4, self.at(r.far, 0), r.to_left)
        self.relay(r.far, 0, 6)
        w(self.ids + 5, self.at(r.far, 1), r.to_right)
        self.relay(r.far, 1, 7)
        if self.partner is not None:
            order = ((r.pos, 0), (r.pos, 1), (r.left, 0), (r.left, 1))
            order += ((r.right, 0), (r.right, 1), (r.far, 0), (r.far, 1))
            for slot, (pos, part) in enumerate(order):
                w(self.pids + slot, self.at(pos, part, self.offset_partner), self.partner)


class RingSum:
    def __init__(self, ring, buf, offset, half, land):
        self.ring, self.buf, self.offset, self.half, self.land = ring, buf, offset, half, land
        self.ids = ring.links.slots(6)

    def at(self, pos, part, count=1):
        return self.buf.at[rows(self.offset(pos) + part * self.half, self.half * count, self.half)]

    def landing(self, slot):
        return self.land.at[pl.ds(slot * self.half, self.half)]

    def send(self, src, slot, to):
        self.ring.links.send(src, self.landing(slot), self.ids + slot, to)

    def wait(self, slot, to):
        self.ring.links.wait(self.ids + slot, self.landing(slot), to)

    def add(self, pos, part, slot):
        ref = self.at(pos, part)
        ref[...] = (ref[...].astype(F32) + self.landing(slot)[...].astype(F32)).astype(BF16)

    def send_far(self):
        r = self.ring
        self.send(self.at(r.far, 0), 0, r.to_right)
        self.send(self.at(r.far, 1), 1, r.to_left)

    def send_near(self):
        r = self.ring
        self.send(self.at(r.right, 1), 3, r.to_right)
        self.send(self.at(r.left, 0), 4, r.to_left)

    def middle(self):
        r = self.ring
        self.wait(0, r.to_left)
        self.add(r.right, 0, 0)
        self.send(self.at(r.right, 0), 2, r.to_right)
        self.wait(1, r.to_right)
        self.add(r.left, 1, 1)
        self.send(self.at(r.left, 1), 5, r.to_left)

    def total(self):
        r = self.ring
        self.wait(3, r.to_left)
        self.wait(4, r.to_right)
        self.wait(2, r.to_left)
        self.wait(5, r.to_right)
        own = self.at(r.pos, 0, 2)[...].astype(F32)
        left = self.land[pl.ds(2 * self.half, 2 * self.half)].astype(F32)
        right = self.land[pl.ds(4 * self.half, 2 * self.half)].astype(F32)
        return own + left + right


class GroupSum:
    def __init__(self, ring, c, buf, from_core, land):
        self.links, self.c, self.buf, self.from_core = ring.links, c, buf, from_core
        self.partner = {"c": 1 - c}
        self.order = (ring.far, ring.right, ring.left, ring.pos)
        self.ids, self.out_ids = ring.links.slots(4), ring.links.outgoing(4)
        self.sum = RingSum(ring, buf, lambda p: c * 512 + p * 128, 64, land)

    def core_copy(self, pos):
        return pltpu.make_async_remote_copy(
            src_ref=self.buf.at[rows((1 - self.c) * 512 + pos * 128, 128)],
            dst_ref=self.from_core.at[rows(pos * 128, 128)],
            send_sem=self.links.send_sems.at[self.out_ids + pos],
            recv_sem=self.links.recv_sems.at[self.ids + pos],
            device_id=self.partner,
            device_id_type=MESH,
        )

    def run(self, body):
        first = self.order[0] // 2

        @pl.loop(0, 4)
        def _(i):
            tile = lax.rem(first + i, 2)
            body(rows(lax.rem(1 - self.c + i // 2, 2) * 512 + tile * 256, 256))

            @pl.when(i < 2)
            def _():
                self.core_copy(tile * 2).start()
                self.core_copy(tile * 2 + 1).start()

        for pos in range(4):
            self.links.open.append((None, self.core_copy(pos)))

    def core_add(self, k):
        got = self.from_core.at[rows(self.order[k] * 128, 128)]
        self.links.wait(self.ids + self.order[k], got, self.partner)
        ref = self.buf.at[rows(self.c * 512 + self.order[k] * 128, 128)]
        ref[...] = (ref[...].astype(F32) + got[...].astype(F32)).astype(BF16)

    def start(self):
        self.core_add(0)
        self.sum.send_far()
        self.core_add(1)
        self.core_add(2)
        self.sum.send_near()

    def middle(self):
        self.sum.middle()
        self.core_add(3)

    def total(self):
        return self.sum.total()


class WeightGather:
    def __init__(self, ring, me, buf, size, shard):
        self.ring, self.me, self.buf, self.size, self.shard = ring, me, buf, size, shard
        self.ids = ring.links.slots(4)
        self.gather = RingGather(ring, buf, lambda p: p * 4 * size, 2 * size)

    def start(self):
        x, yl, c, yh, z = self.me
        links = self.ring.links
        own = self.buf.at[rows((x * 4 + yl * 2 + c) * self.size, self.size)]
        slot = self.ids + yl * 2 + c
        for dl, dh in ((1, 0), (0, 1), (1, 1)):
            to = {"yl": lax.rem(yl + dl, 2), "yh": lax.rem(yh + dh, 2), "c": yh}
            links.send(self.shard, own, slot, to)
        links.local_if(c == yh, self.shard, own, slot)
        links.send_if(c != yh, self.shard, own, slot, {"c": yh})

    def start_x(self):
        x, yl, c, yh, z = self.me
        for k in range(4):
            ref = self.buf.at[rows((x * 4 + k) * self.size, self.size)]
            self.ring.links.wait(self.ids + k, ref, {"c": 1 - c})
        self.gather.start()


class WeightSum:
    def __init__(self, ring, me, buf, size, land, land_y):
        self.ring, self.me, self.buf, self.size = ring, me, buf, size
        self.land_y = land_y
        self.sum = RingSum(ring, buf, lambda p: p * 4 * size, 2 * size, land)
        self.ids = ring.links.slots(4)

    def start(self):
        self.sum.send_far()
        self.sum.send_near()

    def middle(self):
        self.sum.middle()

    def x_total(self):
        return self.sum.total()

    def start_y(self):
        x, yl, c, yh, z = self.me
        links, size = self.ring.links, self.size
        total = self.x_total()
        self.buf[rows(x * 4 * size, 4 * size)] = total.astype(BF16)
        slot = yh * 2 + yl
        dst = self.land_y.at[rows(slot * size, size)]
        for dl, dc in ((1, 0), (0, 1), (1, 1), (0, 0)):
            to_l, to_c = lax.rem(yl + dl, 2), lax.rem(c + dc, 2)
            src = self.buf.at[rows((x * 4 + to_l * 2 + to_c) * size, size)]
            if dl or dc:
                links.send(src, dst, self.ids + slot, {"yl": to_l, "c": to_c, "yh": c})
            else:
                links.local_if(c == yh, src, dst, self.ids + slot)
                links.send_if(c != yh, src, dst, self.ids + slot, {"yh": c})

    def finish(self):
        c = self.me[2]
        total = 0.0
        for k in range(4):
            ref = self.land_y.at[pl.ds(k * self.size, self.size)]
            self.ring.links.wait(self.ids + k, ref, {"c": 1 - c})
            total = total + ref[...].astype(F32)
        return total


class SmallSum(WeightSum):
    def __init__(self, ring, me, buf, size, land, land_y):
        self.ring, self.me, self.buf, self.size = ring, me, buf, size
        self.land, self.land_y = land, land_y
        self.x_ids = ring.links.slots(4)
        self.ids = ring.links.slots(4)

    def start(self):
        x = self.me[0]
        for d in (2, 1, 3):
            to = lax.rem(x + d, 4)
            src = self.buf.at[rows(to * 4 * self.size, 4 * self.size)]
            dst = self.land.at[pl.ds(d * 4 * self.size, 4 * self.size)]
            self.ring.links.send(src, dst, self.x_ids + d, {"x": to})

    def x_total(self):
        x = self.me[0]
        total = self.buf[rows(x * 4 * self.size, 4 * self.size)].astype(F32)
        for d in (1, 3, 2):
            ref = self.land.at[pl.ds(d * 4 * self.size, 4 * self.size)]
            self.ring.links.wait(self.x_ids + d, ref, {"x": lax.rem(x + 4 - d, 4)})
            total = total + ref[...].astype(F32)
        return total


def layer_kernel(
    tok_ref, cot_ref, wi_ref, wo_ref, we_ref, wc_ref, gain_ref, off_ref, hid_ref, head_ref,
    out_ref, gtok_ref, gwi_ref, gwo_ref, gwe_ref, gwc_ref, gsm_ref,
    xg, cotg, h1, h2, gbg, wi, wo, we, wc, sm, gi, go, ge, gc, gs,
    land_i, land_o, land_e, land_c, land_s, landy_i, landy_o, landy_e, landy_c, landy_s,
    part_b, part_o, part_2, part_1, core_b, core_o, core_2, core_1, near_b, near_o, near_2, near_1,
    qkv, gqkv, kvr, gkv_out, gkv_in, att, gatt, hid, gp, lse, dk_acc, dv_acc, dk0_acc, dv0_acc,
    resid, gres, vec, tens, hb_sum, wi_own, sm_own, sm_parts, top, low_sum, att_f, gq_f, delta, columns,
    vec_t, send_sems, recv_sems, local_sems,
):
    x, yl, c, yh, z = me = tuple(lax.axis_index(a) for a in ("x", "yl", "c", "yh", "z"))
    dp = x * 4 + yl * 2 + c
    links = Links(send_sems, recv_sems)
    ring_z, ring_x = Ring(links, "z", z), Ring(links, "x", x)
    partner = {"c": 1 - c}

    def block(p):
        return c * 512 + p * 128

    def block_partner(p):
        return (1 - c) * 512 + p * 128

    own = rows(block(z), 128)
    loads = [pltpu.make_async_copy(tok_ref, xg.at[own], local_sems.at[0])]
    loads.append(pltpu.make_async_copy(cot_ref, cotg.at[own], local_sems.at[1]))
    for k in range(3):
        loads.append(pltpu.make_async_copy(wi_ref.at[k], wi_own.at[:, pl.ds(128 * k, 128)], local_sems.at[2 + k]))
    for load in loads:
        load.start()

    barrier = pltpu.get_barrier_semaphore()
    peers = [{"x": ring_x.right}, {"x": ring_x.left}, {"x": ring_x.far}]
    for dh in range(2):
        for dz in range(4):
            if dh or dz:
                peers.append({"yh": lax.rem(yh + dh, 2), "z": lax.rem(z + dz, 4)})
    for dl in range(2):
        for dc in range(2):
            for dh in range(2):
                if dl or dc:
                    peers.append({"yl": lax.rem(yl + dl, 2), "c": lax.rem(c + dc, 2), "yh": lax.rem(yh + dh, 2)})
    for peer in peers:
        pl.semaphore_signal(barrier, inc=1, device_id=peer, device_id_type=MESH)
    sm_parts[...] = jnp.zeros_like(sm_parts)
    sm_parts[0:2, 0:64] = gain_ref[...].astype(F32)
    sm_parts[2:6, 0:64] = off_ref[...].astype(F32)
    sm_parts[22:23, 0:32] = hid_ref[...].astype(F32)
    sm_parts[39:40, 0:8] = head_ref[0].astype(F32)
    sm_parts[40:41, 0:8] = head_ref[1].astype(F32)
    placed = pltpu.roll(sm_parts[0:16], c * 64, 1) + pltpu.roll(sm_parts[16:32], lax.rem(dp, 4) * 32, 1)
    sm_own[...] = (placed + pltpu.roll(sm_parts[32:48], dp * 8, 1)).astype(BF16)
    for load in loads:
        load.wait()
    pl.semaphore_wait(barrier, len(peers))

    w_sm = WeightGather(ring_x, me, sm, 16, sm_own)
    w_i = WeightGather(ring_x, me, wi, 64, wi_own)
    w_o = WeightGather(ring_x, me, wo, 64, wo_ref)
    w_e = WeightGather(ring_x, me, we, 64, we_ref)
    w_c = WeightGather(ring_x, me, wc, 64, wc_ref)
    w_sm.start()
    w_i.start()
    gather_x = RingGather(ring_z, xg, block, 64, partner, block_partner)
    gather_x.start()
    w_o.start()
    w_sm.start_x()
    w_i.start_x()
    w_o.start_x()
    w_e.start()
    w_c.start()
    gather_x.forward()
    w_sm.gather.forward()
    w_i.gather.forward()
    gather_x.done()
    gather_c = RingGather(ring_z, cotg, block, 64, partner, block_partner)
    gather_c.start()
    w_sm.gather.done()

    tiles = [sm[pl.ds(16 * k, 16)].astype(F32) for k in range(16)]
    pairs = [tiles[2 * k] + tiles[2 * k + 1] for k in range(8)]
    vectors = jnp.concatenate(pairs, axis=1)
    gains, offs = vectors[0:2], vectors[2:6]
    fours = [pairs[2 * k] + pairs[2 * k + 1] for k in range(4)]
    hidden_bias = jnp.concatenate([f[6:7] for f in fours], axis=1)
    every = fours[0] + fours[1] + fours[2] + fours[3]
    qkv_bias = jnp.concatenate([every[7:8], jnp.zeros((1, 128), F32), every[8:9]], axis=1)
    gain1, gain2 = gains[0:1], gains[1:2]
    off0, off1, off2, off3 = (offs[k : k + 1] for k in range(4))

    @pl.loop(0, 4)
    def _(i):
        r = rows(i * 256, 256)
        normed, _ = norm_rows(xg[r].astype(F32))
        h1[r] = (normed * gain1 + off0).astype(BF16)

    w_i.gather.done()
    w_o.gather.forward()

    kv_slots = links.slots(2)
    kv_copies = []
    for s in range(2):
        part = pl.ds(s * 512, 512)
        kv_copies.append(links.make(qkv.at[part, pl.ds(128, 256)], kvr.at[part], kv_slots + s, {"yh": 1}))
        links.open.append((yh == 0, kv_copies[s]))

    @pl.loop(0, 4)
    def _(i):
        r = rows(i * 256, 256)
        qkv[r] = (nn(h1[r], wi[...]) + qkv_bias).astype(BF16)
        for s in range(2):
            pl.when((i == 2 * s + 1) & (yh == 0))(kv_copies[s].start)

    w_e.start_x()
    w_c.start_x()
    gather_c.forward()

    lane = lax.broadcasted_iota(jnp.int32, (1, 128), 1)
    head_lanes = [lane < 64, lane >= 64]

    def causal(scores, first):
        r = lax.broadcasted_iota(jnp.int32, scores.shape, 0) + first
        return jnp.where(r >= lax.broadcasted_iota(jnp.int32, scores.shape, 1), scores, MASKED)

    def masked(value, h):
        return jnp.where(head_lanes[h], value, jnp.zeros_like(value))

    def attend():
        @pl.loop(0, 2)
        def _(s):
            for qb in range(2):
                nk = 256 * (qb + 1)
                r = rows(s * 512 + qb * 256, 256)
                keys = rows(s * 512, nk, 512)
                q, k, v = qkv[r, 0:128], qkv[keys, 128:256], qkv[keys, 256:384]
                outs = []
                for h in range(2):
                    near = causal(nt(masked(q, h), k) * SCALE, qb * 256)
                    peak = jnp.max(near, axis=-1, keepdims=True)
                    near = jnp.exp(near - peak)
                    top[h, r] = peak
                    low_sum[h, r] = jnp.sum(near, axis=-1, keepdims=True)
                    outs.append(nn(near.astype(BF16), v))
                att_f[r] = jnp.where(head_lanes[0], outs[0], outs[1])

    def finish(remote):
        @pl.loop(0, 4)
        def _(i):
            r = rows(i * 256, 256)
            keys = rows((i // 2) * 512, 512)
            outs = []
            for h in range(2):
                peak, total, o = top[h, r], low_sum[h, r], att_f[r]
                if remote:
                    far = nt(masked(qkv[r, 0:128], h), kvr[keys, 0:128]) * SCALE
                    higher = jnp.maximum(peak, jnp.max(far, axis=-1, keepdims=True))
                    far = jnp.exp(far - higher)
                    shrink = jnp.exp(peak - higher)
                    total = total * shrink + jnp.sum(far, axis=-1, keepdims=True)
                    o = o * shrink + nn(far.astype(BF16), kvr[keys, 128:256])
                    peak = higher
                outs.append(o * (1.0 / total))
                lse[h, r] = peak + jnp.log(total)
            o = jnp.where(head_lanes[0], outs[0], outs[1])
            att_f[r] = o
            att[r] = o.astype(BF16)

    attend()
    w_o.gather.done()
    pl.when(yh == 0)(functools.partial(finish, False))

    @pl.when(yh == 1)
    def _():
        for s in range(2):
            links.wait(kv_slots + s, kvr.at[pl.ds(s * 512, 512)], {"yh": 0})
        finish(True)

    def branch_tile(r):
        part_b[r] = nt(att[r], wo[...]).astype(BF16)

    sum_b = GroupSum(ring_z, c, part_b, core_b, near_b)
    sum_b.run(branch_tile)
    gather_c.done()
    sum_b.start()
    w_e.gather.forward()
    w_c.gather.forward()
    sum_b.middle()
    x_own = xg[own].astype(F32)
    cot_own = cotg[own].astype(F32)
    resid[...] = x_own + sum_b.total() + off1
    normed2, inverse2 = norm_rows(resid[...])
    h2[own] = (normed2 * gain2 + off2).astype(BF16)
    gather_h = RingGather(ring_z, h2, block, 64, partner, block_partner)
    gather_h.start()
    w_e.gather.done()
    w_c.gather.done()
    vec_t[...] = jnp.transpose(vectors)
    gather_h.forward()
    gather_h.done()

    hb_sum[...] = jnp.zeros_like(hb_sum)

    def mlp_tile(r):
        p = nn(h2[r], we[...]) + hidden_bias
        square = p * p
        t = jnp.tanh(GELU_COEF * (p + CUBIC * p * square))
        hid[r] = (0.5 * p * (1.0 + t)).astype(BF16)
        slope = 0.5 * (1.0 + t) + 0.5 * p * (1.0 - t * t) * (GELU_COEF * (1.0 + 3.0 * CUBIC * square))
        g = (nn(cotg[r], wc[...]) * slope).astype(BF16)
        gp[r] = g
        hb_sum[...] += jnp.sum(g.astype(F32), axis=0, keepdims=True)
        part_2[r] = nt(g, we[...]).astype(BF16)

    sum_2 = GroupSum(ring_z, c, part_2, core_2, near_2)
    sum_2.run(mlp_tile)
    sum_2.start()

    def weight_grad(out, left, right):
        @pl.loop(0, 4)
        def _(i):
            r = rows(i * 256, 256)
            out[r] = tn(left[:, r], right[...]).astype(BF16)

    g_e = WeightSum(ring_x, me, ge, 64, land_e, landy_e)
    g_c = WeightSum(ring_x, me, gc, 64, land_c, landy_c)
    weight_grad(ge, h2, gp)
    g_e.start()
    sum_2.middle()
    weight_grad(gc, cotg, hid)
    g_c.start()

    grad2 = sum_2.total()
    gres[...] = cot_own + norm_back(grad2, normed2, inverse2, gain2)
    grad_branch = gres[...].astype(BF16)
    gbg[own] = grad_branch
    gather_b = RingGather(ring_z, gbg, block, 64, partner, block_partner)
    gather_b.start()
    vec[1:2] = jnp.sum(grad2 * normed2, axis=0, keepdims=True)
    vec[3:4] = jnp.sum(grad_branch.astype(F32), axis=0, keepdims=True)
    vec[4:5] = jnp.sum(grad2, axis=0, keepdims=True)
    vec[5:6] = jnp.sum(cot_own, axis=0, keepdims=True)
    g_e.middle()

    def out_tile(r):
        part_o[r] = nt(hid[r], wc[...]).astype(BF16)

    sum_o = GroupSum(ring_z, c, part_o, core_o, near_o)
    gather_b.forward()
    sum_o.run(out_tile)
    gather_b.done()
    sum_o.start()
    g_c.middle()

    @pl.loop(0, 4)
    def _(i):
        r = rows(i * 256, 256)
        g = nn(gbg[r], wo[...])
        low = g.astype(BF16)
        gatt[r] = low
        product = low.astype(F32) * att_f[r]
        for h in range(2):
            delta[h, r] = jnp.sum(masked(product, h), axis=-1, keepdims=True)

    gkv_slots = links.slots(2)
    gkv_copies = []
    for s in range(2):
        part = pl.ds(s * 512, 512)
        gkv_copies.append(links.make(gkv_out.at[part], gkv_in.at[part], gkv_slots + s, {"yh": 0}))
        links.open.append((yh == 1, gkv_copies[s]))

    def attend_far():
        @pl.loop(0, 2)
        def _(s):
            seq = rows(s * 512, 512)
            k, v = kvr[seq, 0:128], kvr[seq, 128:256]
            dk0_acc[...] = jnp.zeros_like(dk0_acc)
            dv0_acc[...] = jnp.zeros_like(dv0_acc)

            @pl.loop(0, 2)
            def _(qb):
                r = rows(s * 512 + qb * 256, 256)
                q, g = qkv[r, 0:128], gatt[r]
                outs = []
                for h in range(2):
                    qm, gm = masked(q, h), masked(g, h)
                    far = jnp.exp(nt(qm, k) * SCALE - lse[h, r])
                    far_s = (far * (nt(gm, v) - delta[h, r])).astype(BF16)
                    dk0_acc[...] += tn(far_s, qm)
                    dv0_acc[...] += tn(far.astype(BF16), gm)
                    outs.append(nn(far_s, k))
                gq_f[r] = jnp.where(head_lanes[0], outs[0], outs[1])

            gkv_out[seq, 0:128] = (dk0_acc[...] * SCALE).astype(BF16)
            gkv_out[seq, 128:256] = dv0_acc[...].astype(BF16)
            for k in range(2):
                pl.when(s == k)(gkv_copies[k].start)

    def attend_back():
        @pl.loop(0, 2)
        def _(s):
            dk_acc[...] = jnp.zeros_like(dk_acc)
            dv_acc[...] = jnp.zeros_like(dv_acc)
            seq = rows(s * 512, 512)
            for qb in range(2):
                nk = 256 * (qb + 1)
                r = rows(s * 512 + qb * 256, 256)
                keys = rows(s * 512, nk, 512)
                q, k, v, g = qkv[r, 0:128], qkv[keys, 128:256], qkv[keys, 256:384], gatt[r]
                outs = []
                for h in range(2):
                    qm, gm = masked(q, h), masked(g, h)
                    near = jnp.exp(causal(nt(qm, k) * SCALE, qb * 256) - lse[h, r])
                    near_s = (near * (nt(gm, v) - delta[h, r])).astype(BF16)
                    dk_acc[0:nk] += tn(near_s, qm)
                    dv_acc[0:nk] += tn(near.astype(BF16), gm)
                    outs.append(nn(near_s, k))
                total = gq_f[r] + jnp.where(head_lanes[0], outs[0], outs[1])
                gqkv[r, 0:128] = (total * SCALE).astype(BF16)
            gqkv[seq, 128:256] = (dk_acc[...] * SCALE).astype(BF16)
            gqkv[seq, 256:384] = dv_acc[...].astype(BF16)

    @pl.when(yh == 0)
    def _():
        gq_f[...] = jnp.zeros_like(gq_f)

    pl.when(yh == 1)(attend_far)
    g_e.start_y()
    weight_grad(go, gbg, att)
    g_o = WeightSum(ring_x, me, go, 64, land_o, landy_o)
    g_o.start()
    attend_back()
    sum_o.middle()
    g_o.middle()

    @pl.when(yh == 0)
    def _():
        for s in range(2):
            links.wait(gkv_slots + s, gkv_in.at[pl.ds(s * 512, 512)], {"yh": 1})

            @pl.loop(0, 2)
            def _(k):
                r = rows(s * 512 + k * 256, 256)
                gqkv[r, 128:384] = (gqkv[r, 128:384].astype(F32) + gkv_in[r].astype(F32)).astype(BF16)

    def grad1_tile(r):
        part_1[r] = nt(gqkv[r], wi[...]).astype(BF16)

    sum_1 = GroupSum(ring_z, c, part_1, core_1, near_1)
    sum_1.run(grad1_tile)
    sum_1.start()
    head_sums = jnp.sum(gqkv[...].astype(F32), axis=0, keepdims=True)

    @pl.loop(0, 4)
    def _(i):
        r = rows(i * 256, 256)
        g = tn(h1[:, r], gqkv[...])
        gi[r] = g.astype(BF16)
        weight = wi[r].astype(F32)
        off_grad = jnp.sum(weight * head_sums, axis=-1, keepdims=True)
        mixed = jnp.sum(weight * g, axis=-1, keepdims=True)
        gain_grad = (mixed - vec_t[r, 2:3] * off_grad) / vec_t[r, 0:1]
        columns[r] = jnp.where(lane == 0, gain_grad, jnp.where(lane == 2, off_grad, 0.0))

    g_i = WeightSum(ring_x, me, gi, 64, land_i, landy_i)
    g_i.start()
    turned = jnp.transpose(columns[...])
    vec[0:1] = turned[0:1]
    vec[2:3] = turned[2:3]
    hb = hb_sum[...]
    vec[6:7] = jnp.concatenate([hb[:, 128 * (k // 2) : 128 * (k // 2) + 128] for k in range(8)], axis=1)
    vec[7:8] = jnp.concatenate([head_sums[:, 0:128]] * 8, axis=1)
    vec[8:9] = jnp.concatenate([head_sums[:, 256:384]] * 8, axis=1)
    vec[9:16] = jnp.zeros((7, 1024), F32)
    for k in range(16):
        gs[pl.ds(16 * k, 16)] = vec[:, 128 * (k // 2) : 128 * (k // 2) + 128].astype(BF16)
    g_s = SmallSum(ring_x, me, gs, 16, land_s, landy_s)
    g_s.start()
    sum_1.middle()
    g_c.start_y()
    g_o.start_y()
    out_ref[...] = (resid[...] + sum_o.total() + off3).astype(BF16)
    g_s.start_y()
    g_i.middle()
    normed1, inverse1 = norm_rows(x_own)
    gtok_ref[...] = gres[...] + norm_back(sum_1.total(), normed1, inverse1, gain1)
    tile = g_s.finish()
    slot = yh * 4 + z
    tens[rows(slot * 16, 16)] = tile
    mine = tens.at[rows(slot * 16, 16)]
    t_ids = links.slots(8)
    others = [(dh, dz) for dh in range(2) for dz in range(4) if dh or dz]
    for dh, dz in others:
        links.send(mine, mine, t_ids + slot, {"yh": lax.rem(yh + dh, 2), "z": lax.rem(z + dz, 4)})
    g_i.start_y()
    gwe_ref[...] = g_e.finish()
    gwc_ref[...] = g_c.finish()
    gwo_ref[...] = g_o.finish()
    for dh, dz in others:
        theirs = lax.rem(yh + dh, 2) * 4 + lax.rem(z + dz, 4)
        ref = tens.at[rows(theirs * 16, 16)]
        links.wait(t_ids + theirs, ref, {"yh": lax.rem(yh + dh, 2), "z": lax.rem(z + dz, 4)})
    total = tens[0:16]
    for k in range(1, 8):
        total = total + tens[16 * k : 16 * k + 16]
    gsm_ref[0:6] = total[0:6]
    gsm_ref[6:16] = tile[6:16]
    gwi_ref[...] = g_i.finish()
    links.drain()


def final_kernel(
    out_k, gtok_k, gwi, gwo, gwe, gwc, gsm,
    out_ref, gtok_ref, gi_ref, go_ref, ge_ref, gc_ref, head_ref, hid_ref, gain_ref, off_ref,
):
    c = lax.axis_index("c")
    dp = lax.axis_index("x") * 4 + lax.axis_index("yl") * 2 + c
    out_ref[...] = out_k[...]
    gtok_ref[...] = gtok_k[...]
    for k in range(3):
        gi_ref[k] = gwi[:, 128 * k : 128 * k + 128]
    go_ref[...] = jnp.transpose(gwo[...])
    ge_ref[...] = gwe[...]
    gc_ref[...] = jnp.transpose(gwc[...])
    small = gsm[...]
    mine = pltpu.roll(small, lax.rem(128 - c * 64, 128), 1)
    gain_ref[...] = mine[0:2, 0:64]
    off_ref[...] = mine[2:6, 0:64]
    hid_ref[...] = pltpu.roll(small, lax.rem(128 - lax.rem(dp, 4) * 32, 128), 1)[6:7, 0:32]
    heads = pltpu.roll(small, lax.rem(128 - dp * 8, 128), 1)
    head_ref[0] = heads[7:8, 0:8]
    head_ref[1] = heads[8:9, 0:8]


def per_device(tokens, input_proj, output_proj, expand_proj, contract_proj, head_bias, hidden_bias, norm_gains, offsets, cotangent):
    vmem = pl.BlockSpec(memory_space=pltpu.VMEM)
    shape = jax.ShapeDtypeStruct
    widths = (384, 128, 512, 512)

    def buf(r, n, t=BF16):
        return pltpu.VMEM((r, n), t)

    scratch = [buf(1024, 1024) for _ in range(5)]
    scratch += [buf(1024, n) for n in widths] + [buf(256, 128)]
    scratch += [buf(1024, n) for n in widths] + [buf(256, 128)]
    scratch += [buf(768, n) for n in widths] + [buf(256, 128)]
    scratch += [buf(256, n) for n in widths] + [buf(64, 128)]
    scratch += [buf(1024, 1024) for _ in range(4)] + [buf(512, 1024) for _ in range(4)]
    scratch += [buf(384, 1024) for _ in range(4)]
    scratch += [buf(1024, 384), buf(1024, 384), buf(1024, 256), buf(1024, 256), buf(1024, 256)]
    scratch += [buf(1024, 128), buf(1024, 128), buf(1024, 512), buf(1024, 512)]
    scratch += [pltpu.VMEM((2, 1024, 1), F32)] + [buf(512, 128, F32) for _ in range(4)]
    scratch += [buf(128, 1024, F32), buf(128, 1024, F32), buf(16, 1024, F32), buf(128, 128, F32)]
    scratch += [buf(1, 512, F32), buf(64, 384), buf(16, 128), buf(48, 128, F32)]
    scratch += [pltpu.VMEM((2, 1024, 1), F32), pltpu.VMEM((2, 1024, 1), F32)]
    scratch += [buf(1024, 128, F32), buf(1024, 128, F32), pltpu.VMEM((2, 1024, 1), F32)]
    scratch += [buf(1024, 128, F32), buf(1024, 16, F32)]
    scratch += [pltpu.SemaphoreType.DMA((N_SEMS,)), pltpu.SemaphoreType.DMA((N_SEMS,))]
    scratch += [pltpu.SemaphoreType.DMA((8,))]
    out, gtok, gwi, gwo, gwe, gwc, gsm = pl.pallas_call(
        layer_kernel,
        out_shape=(
            shape((128, 1024), BF16),
            shape((128, 1024), F32),
            *(shape((64, n), F32) for n in widths),
            shape((16, 128), F32),
        ),
        in_specs=[pl.BlockSpec(memory_space=pl.ANY)] * 6 + [vmem] * 4,
        out_specs=[vmem] * 7,
        scratch_shapes=scratch,
        compiler_params=pltpu.CompilerParams(
            collective_id=0, has_side_effects=True, vmem_limit_bytes=58 * 1024 * 1024
        ),
    )(
        tokens, cotangent, input_proj, output_proj.T, expand_proj, contract_proj.T,
        norm_gains, offsets, hidden_bias, head_bias,
    )
    return pl.pallas_call(
        final_kernel,
        out_shape=(
            shape((128, 1024), BF16),
            shape((128, 1024), F32),
            shape((3, 64, 128), F32),
            shape((128, 64), F32),
            shape((64, 512), F32),
            shape((512, 64), F32),
            shape((2, 1, 8), F32),
            shape((1, 32), F32),
            shape((2, 64), F32),
            shape((4, 64), F32),
        ),
        in_specs=[vmem] * 7,
        out_specs=[vmem] * 10,
    )(out, gtok, gwi, gwo, gwe, gwc, gsm)


def solution(mesh):
    split = Mesh(mesh.devices.reshape(4, 2, 2, 2, 4), ("x", "yl", "c", "yh", "z"))
    token_rows = P(DP + TENSOR, None)
    weights = (
        P(None, DP, TENSOR),
        P(TENSOR, DP),
        P(DP, TENSOR),
        P(TENSOR, DP),
        P(None, TENSOR, DP),
        P(TENSOR, DP),
        P(None, DP),
        P(None, DP),
    )
    return jax.shard_map(
        per_device,
        mesh=split,
        in_specs=(token_rows, *weights, token_rows),
        out_specs=(token_rows, token_rows, *weights),
        check_vma=False,
    )
```

```python
import functools

import jax
import jax.numpy as jnp
from jax import lax
from jax.experimental import pallas as pl
from jax.experimental.pallas import tpu as pltpu
from jax.sharding import Mesh
from jax.sharding import PartitionSpec as P

F32, BF16 = jnp.float32, jnp.bfloat16
MESH = pl.DeviceIdType.MESH
DP = ("x", "yl", "c")
TENSOR = ("yh", "z")
EPSILON = 1e-05
MASKED = -1000000000.0
GELU_COEF = 0.7978845608028654
CUBIC = 0.044715
SCALE = 64 ** (-0.5)
N_SEMS = 340


def nn(a, b):
    return lax.dot_general(a, b, (((1,), (0,)), ((), ())), preferred_element_type=F32)


def nt(a, b):
    return lax.dot_general(a, b, (((1,), (1,)), ((), ())), preferred_element_type=F32)


def tn(a, b):
    return lax.dot_general(a, b, (((0,), (0,)), ((), ())), preferred_element_type=F32)


def rows(start, size, by=None):
    if isinstance(start, int):
        return pl.ds(start, size)
    return pl.ds(pl.multiple_of(start, by or size), size)


def norm_rows(v):
    shifted = v - jnp.mean(v, axis=-1, keepdims=True)
    inverse = lax.rsqrt(jnp.mean(shifted * shifted, axis=-1, keepdims=True) + EPSILON)
    return shifted * inverse, inverse


def norm_back(grad, normed, inverse, gain):
    scaled = grad * gain
    first = jnp.mean(scaled, axis=-1, keepdims=True)
    second = jnp.mean(scaled * normed, axis=-1, keepdims=True)
    return inverse * (scaled - first - normed * second)


class Links:
    def __init__(self, send_sems, recv_sems):
        self.send_sems, self.recv_sems = send_sems, recv_sems
        self.sent, self.received, self.open = 0, 0, []

    def outgoing(self, count):
        first = self.sent
        self.sent += count
        assert self.sent <= N_SEMS
        return first

    def slots(self, count):
        first = self.received
        self.received += count
        assert self.received <= N_SEMS
        return first

    def make(self, src, dst, recv, to):
        copy = pltpu.make_async_remote_copy(
            src_ref=src,
            dst_ref=dst,
            send_sem=self.send_sems.at[self.sent],
            recv_sem=self.recv_sems.at[recv],
            device_id=to,
            device_id_type=MESH,
        )
        self.sent += 1
        assert self.sent <= N_SEMS
        return copy

    def send(self, src, dst, recv, to, like=None):
        sem = self.sent
        copy = self.make(src, dst, recv, to)
        copy.start()
        self.open.append((None, copy) if like is None else (sem, like))

    def send_if(self, cond, src, dst, recv, to):
        copy = self.make(src, dst, recv, to)
        pl.when(cond)(copy.start)
        self.open.append((cond, copy))

    def local_if(self, cond, src, dst, recv):
        copy = pltpu.make_async_copy(src, dst, self.recv_sems.at[recv])
        pl.when(cond)(copy.start)

    def wait(self, recv, ref, to):
        pltpu.make_async_remote_copy(
            src_ref=ref,
            dst_ref=ref,
            send_sem=self.send_sems.at[0],
            recv_sem=self.recv_sems.at[recv],
            device_id=to,
            device_id_type=MESH,
        ).wait_recv()

    def drain(self):
        for cond, copy in self.open:
            if isinstance(cond, int):
                pltpu.make_async_remote_copy(
                    src_ref=copy,
                    dst_ref=copy,
                    send_sem=self.send_sems.at[cond],
                    recv_sem=self.recv_sems.at[0],
                    device_id={"c": 0},
                    device_id_type=MESH,
                ).wait_send()
            elif cond is None:
                copy.wait_send()
            else:
                pl.when(cond)(copy.wait_send)
        self.open = []


class Ring:
    def __init__(self, links, axis, pos):
        self.links, self.axis = links, axis
        self.pos = pos
        self.right, self.left, self.far = (lax.rem(pos + k, 4) for k in (1, 3, 2))
        self.to_right, self.to_left = {axis: self.right}, {axis: self.left}


class RingGather:
    def __init__(self, ring, buf, offset, half, partner=None, offset_partner=None):
        self.ring, self.buf, self.offset, self.half = ring, buf, offset, half
        self.partner, self.offset_partner = partner, offset_partner
        self.ids = ring.links.slots(6)
        if partner is not None:
            self.pids = ring.links.slots(8)

    def at(self, pos, part, offset=None):
        return self.buf.at[rows((offset or self.offset)(pos) + part * self.half, self.half)]

    def like(self):
        return self.buf.at[pl.ds(0, self.half)]

    def relay(self, pos, part, slot):
        if self.partner is not None:
            ref = self.at(pos, part)
            self.ring.links.send(ref, ref, self.pids + slot, self.partner, self.like())

    def start(self):
        r, s = self.ring, self.ring.links.send
        a, b = self.at(r.pos, 0), self.at(r.pos, 1)
        s(a, a, self.ids + 0, r.to_right)
        s(b, b, self.ids + 3, r.to_left)
        s(b, b, self.ids + 1, r.to_right)
        s(a, a, self.ids + 2, r.to_left)
        self.relay(r.pos, 0, 0)
        self.relay(r.pos, 1, 1)

    def forward(self):
        r, s, w = self.ring, self.ring.links.send, self.ring.links.wait
        ref = self.at(r.left, 0)
        w(self.ids + 0, ref, r.to_left)
        s(ref, ref, self.ids + 4, r.to_right)
        ref = self.at(r.right, 1)
        w(self.ids + 3, ref, r.to_right)
        s(ref, ref, self.ids + 5, r.to_left)
        self.relay(r.left, 0, 2)
        self.relay(r.right, 1, 5)

    def done(self):
        self.near()
        self.far()
        self.own()

    def near(self):
        r, w = self.ring, self.ring.links.wait
        w(self.ids + 1, self.at(r.left, 1), r.to_left)
        self.relay(r.left, 1, 3)
        w(self.ids + 2, self.at(r.right, 0), r.to_right)
        self.relay(r.right, 0, 4)
        self.relayed(2, ((r.left, 0), (r.left, 1), (r.right, 0), (r.right, 1)))

    def far(self):
        r, w = self.ring, self.ring.links.wait
        w(self.ids + 4, self.at(r.far, 0), r.to_left)
        self.relay(r.far, 0, 6)
        w(self.ids + 5, self.at(r.far, 1), r.to_right)
        self.relay(r.far, 1, 7)
        self.relayed(6, ((r.far, 0), (r.far, 1)))

    def own(self):
        r = self.ring
        self.relayed(0, ((r.pos, 0), (r.pos, 1)))

    def relayed(self, first, blocks):
        if self.partner is not None:
            for k, (pos, part) in enumerate(blocks):
                self.ring.links.wait(self.pids + first + k, self.at(pos, part, self.offset_partner), self.partner)


class ColumnGather(RingGather):
    def __init__(self, ring, c, buf, partner):
        super().__init__(ring, buf, c, buf.shape[0] // 2, partner, 1 - c)

    def at(self, pos, part, core=None):
        rank = (self.offset if core is None else core) * 4 + pos
        return self.buf.at[pl.ds(part * self.half, self.half), rows(rank * 128, 128)]

    def like(self):
        return self.buf.at[pl.ds(0, self.half), pl.ds(0, 128)]


class FirstGather(RingGather):
    def at(self, pos, part, offset=None):
        return self.buf.at[pos, pl.ds(part * self.half, self.half)]

    def like(self):
        return self.buf.at[0, pl.ds(0, self.half)]


class WeightGatherAlongX:
    def __init__(self, ring, me, buf, line):
        self.ring, self.me, self.buf, self.line = ring, me, buf, line
        self.gather = FirstGather(ring, line, None, line.shape[1] // 2)
        self.ids = ring.links.slots(4)

    def start_y(self):
        x, yl, c, yh, z = self.me
        links = self.ring.links
        self.gather.done()
        slot = yl * 2 + c
        dst = self.buf.at[:, slot]
        for dl, dh in ((1, 0), (0, 1), (1, 1)):
            to = {"yl": lax.rem(yl + dl, 2), "yh": lax.rem(yh + dh, 2), "c": yh}
            links.send(self.line, dst, self.ids + slot, to)
        links.local_if(c == yh, self.line, dst, self.ids + slot)
        links.send_if(c != yh, self.line, dst, self.ids + slot, {"c": yh})

    def done(self):
        for k in range(4):
            self.ring.links.wait(self.ids + k, self.buf.at[:, k], {"c": 1 - self.me[2]})


class Swap:
    def __init__(self, ring, c, size):
        self.ring, self.c, self.size = ring, c, size
        self.rank = c * 4 + ring.pos
        self.ids = ring.links.slots(8)
        self.others = [(dc, dz) for dz in (2, 1, 3, 0) for dc in (0, 1) if dc or dz]

    def peer(self, dc, dz):
        return lax.rem(self.c + dc, 2), lax.rem(self.ring.pos + dz, 4)

    def tile(self, buf, rank):
        return buf.at[rows(rank * self.size, self.size)]

    def start(self, src, dst):
        for dc, dz in self.others:
            to_c, to_z = self.peer(dc, dz)
            to = {"c": to_c, "z": to_z}
            self.ring.links.send(self.tile(src, to_c * 4 + to_z), self.tile(dst, self.rank), self.ids + self.rank, to)
        self.tile(dst, self.rank)[...] = self.tile(src, self.rank)[...]

    def done(self, dst):
        for dc, dz in self.others:
            of_c, of_z = self.peer(dc, dz)
            theirs = of_c * 4 + of_z
            self.ring.links.wait(self.ids + theirs, self.tile(dst, theirs), {"c": of_c, "z": of_z})


class RingSum:
    def __init__(self, ring, buf, offset, half, land):
        self.ring, self.buf, self.offset, self.half, self.land = ring, buf, offset, half, land
        self.ids = ring.links.slots(6)

    def at(self, pos, part, count=1):
        return self.buf.at[rows(self.offset(pos) + part * self.half, self.half * count, self.half)]

    def landing(self, slot):
        return self.land.at[pl.ds(slot * self.half, self.half)]

    def send(self, src, slot, to):
        like = self.buf.at[pl.ds(0, self.half)]
        self.ring.links.send(src, self.landing(slot), self.ids + slot, to, like)

    def wait(self, slot, to):
        self.ring.links.wait(self.ids + slot, self.landing(slot), to)

    def add(self, pos, part, slot):
        ref = self.at(pos, part)
        ref[...] = (ref[...].astype(F32) + self.landing(slot)[...].astype(F32)).astype(BF16)

    def send_far(self):
        r = self.ring
        self.send(self.at(r.far, 0), 0, r.to_right)
        self.send(self.at(r.far, 1), 1, r.to_left)

    def send_near(self):
        r = self.ring
        self.send(self.at(r.right, 1), 3, r.to_right)
        self.send(self.at(r.left, 0), 4, r.to_left)

    def middle(self):
        r = self.ring
        self.wait(0, r.to_left)
        self.add(r.right, 0, 0)
        self.send(self.at(r.right, 0), 2, r.to_right)
        self.wait(1, r.to_right)
        self.add(r.left, 1, 1)
        self.send(self.at(r.left, 1), 5, r.to_left)

    def total(self):
        r = self.ring
        self.wait(3, r.to_left)
        self.wait(4, r.to_right)
        self.wait(2, r.to_left)
        self.wait(5, r.to_right)
        own = self.at(r.pos, 0, 2)[...].astype(F32)
        left = self.land[pl.ds(2 * self.half, 2 * self.half)].astype(F32)
        right = self.land[pl.ds(4 * self.half, 2 * self.half)].astype(F32)
        return own + left + right


class GroupSum:
    def __init__(self, ring, c, buf, from_core, land):
        self.links, self.c, self.buf, self.from_core = ring.links, c, buf, from_core
        self.partner = {"c": 1 - c}
        self.order = (ring.far, ring.right, ring.left, ring.pos)
        self.ids, self.out_ids = ring.links.slots(4), ring.links.outgoing(4)
        self.sum = RingSum(ring, buf, lambda p: c * 512 + p * 128, 64, land)

    def core_copy(self, pos):
        return pltpu.make_async_remote_copy(
            src_ref=self.buf.at[rows((1 - self.c) * 512 + pos * 128, 128)],
            dst_ref=self.from_core.at[rows(pos * 128, 128)],
            send_sem=self.links.send_sems.at[self.out_ids + pos],
            recv_sem=self.links.recv_sems.at[self.ids + pos],
            device_id=self.partner,
            device_id_type=MESH,
        )

    def run(self, body):
        first = self.order[0] // 2

        @pl.loop(0, 4)
        def _(i):
            tile = lax.rem(first + i, 2)
            body(rows(lax.rem(1 - self.c + i // 2, 2) * 512 + tile * 256, 256))

            @pl.when(i < 2)
            def _():
                self.core_copy(tile * 2).start()
                self.core_copy(tile * 2 + 1).start()

        for pos in range(4):
            self.links.open.append((None, self.core_copy(pos)))

    def run_by_chip(self, body, gather):
        z = self.order[3]

        @pl.loop(0, 4)
        def _(i):
            pl.when(i == 0)(gather.own)
            pl.when(i == 1)(gather.near)

            @pl.when(i == 3)
            def _():
                gather.far()
                self.core_add(1)
                self.core_add(2)
                self.sum.send_near()

            pos = lax.rem(z + jnp.where(i == 2, 3, jnp.where(i == 3, 2, i)), 4)
            body(pos)
            self.core_copy(pos).start()

        for pos in range(4):
            self.links.open.append((None, self.core_copy(pos)))
        self.core_add(0)
        self.sum.send_far()

    def core_add(self, k):
        got = self.from_core.at[rows(self.order[k] * 128, 128)]
        self.links.wait(self.ids + self.order[k], got, self.partner)
        ref = self.buf.at[rows(self.c * 512 + self.order[k] * 128, 128)]
        ref[...] = (ref[...].astype(F32) + got[...].astype(F32)).astype(BF16)

    def start(self):
        self.core_add(0)
        self.sum.send_far()
        self.core_add(1)
        self.core_add(2)
        self.sum.send_near()

    def middle(self):
        self.sum.middle()
        self.core_add(3)

    def total(self):
        return self.sum.total()


class WeightGather:
    def __init__(self, ring, me, buf, size, shard):
        self.ring, self.me, self.buf, self.size, self.shard = ring, me, buf, size, shard
        self.ids = ring.links.slots(4)
        self.gather = RingGather(ring, buf, lambda p: p * 4 * size, 2 * size)

    def start(self):
        x, yl, c, yh, z = self.me
        links = self.ring.links
        own = self.buf.at[rows((x * 4 + yl * 2 + c) * self.size, self.size)]
        slot = self.ids + yl * 2 + c
        for dl, dh in ((1, 0), (0, 1), (1, 1)):
            to = {"yl": lax.rem(yl + dl, 2), "yh": lax.rem(yh + dh, 2), "c": yh}
            links.send(self.shard, own, slot, to)
        links.local_if(c == yh, self.shard, own, slot)
        links.send_if(c != yh, self.shard, own, slot, {"c": yh})

    def start_x(self):
        x, yl, c, yh, z = self.me
        for k in range(4):
            ref = self.buf.at[rows((x * 4 + k) * self.size, self.size)]
            self.ring.links.wait(self.ids + k, ref, {"c": 1 - c})
        self.gather.start()


class WeightSum:
    def __init__(self, ring, me, buf, size, land, land_y):
        self.ring, self.me, self.buf, self.size = ring, me, buf, size
        self.land_y = land_y
        self.sum = RingSum(ring, buf, lambda p: p * 4 * size, 2 * size, land)
        self.ids = ring.links.slots(4)

    def start(self):
        self.sum.send_far()
        self.sum.send_near()

    def middle(self):
        self.sum.middle()

    def x_total(self):
        return self.sum.total()

    def start_y(self):
        x, yl, c, yh, z = self.me
        links, size = self.ring.links, self.size
        total = self.x_total()
        self.buf[rows(x * 4 * size, 4 * size)] = total.astype(BF16)
        slot = yh * 2 + yl
        dst = self.land_y.at[rows(slot * size, size)]
        for dl, dc in ((1, 0), (0, 1), (1, 1), (0, 0)):
            to_l, to_c = lax.rem(yl + dl, 2), lax.rem(c + dc, 2)
            src = self.buf.at[rows((x * 4 + to_l * 2 + to_c) * size, size)]
            if dl or dc:
                links.send(src, dst, self.ids + slot, {"yl": to_l, "c": to_c, "yh": c})
            else:
                links.local_if(c == yh, src, dst, self.ids + slot)
                links.send_if(c != yh, src, dst, self.ids + slot, {"yh": c})

    def finish(self):
        c = self.me[2]
        total = 0.0
        for k in range(4):
            ref = self.land_y.at[pl.ds(k * self.size, self.size)]
            self.ring.links.wait(self.ids + k, ref, {"c": 1 - c})
            total = total + ref[...].astype(F32)
        return total


class SmallSum(WeightSum):
    def __init__(self, ring, me, buf, size, land, land_y):
        self.ring, self.me, self.buf, self.size = ring, me, buf, size
        self.land, self.land_y = land, land_y
        self.x_ids = ring.links.slots(4)
        self.ids = ring.links.slots(4)

    def start(self):
        x = self.me[0]
        for d in (2, 1, 3):
            to = lax.rem(x + d, 4)
            src = self.buf.at[rows(to * 4 * self.size, 4 * self.size)]
            dst = self.land.at[pl.ds(d * 4 * self.size, 4 * self.size)]
            self.ring.links.send(src, dst, self.x_ids + d, {"x": to})

    def x_total(self):
        x = self.me[0]
        total = self.buf[rows(x * 4 * self.size, 4 * self.size)].astype(F32)
        for d in (1, 3, 2):
            ref = self.land.at[pl.ds(d * 4 * self.size, 4 * self.size)]
            self.ring.links.wait(self.x_ids + d, ref, {"x": lax.rem(x + 4 - d, 4)})
            total = total + ref[...].astype(F32)
        return total


def layer_kernel(
    tok_ref, cot_ref, wi_ref, wo_ref, we_ref, wc_ref, gain_ref, off_ref, hid_ref, head_ref,
    out_ref, gtok_ref, gwi_ref, gwo_ref, gwe_ref, gwc_ref, gsm_ref,
    xg, cotg, h1, h2, gbg, wi, wo, we, wc, sm, gi, go, ge, gc, gs,
    land_i, land_o, land_e, land_c, land_s, landy_i, landy_o, landy_e, landy_c, landy_s,
    part_o, part_2, part_1, core_o, core_2, core_1, near_o, near_2, near_1, wo_all, att_in, gatt_out,
    qkv, gqkv, kvr, gkv_out, gkv_in, att, gatt, hid, gp, lse, dk_acc, dv_acc, dk0_acc, dv0_acc,
    resid, gres, vec, tens, hb_sum, wi_own, sm_own, sm_parts, top, low_sum, att_f, gq_f, delta, columns,
    vec_t, wq_all, wq_line, send_sems, recv_sems, local_sems,
):
    x, yl, c, yh, z = me = tuple(lax.axis_index(a) for a in ("x", "yl", "c", "yh", "z"))
    dp = x * 4 + yl * 2 + c
    links = Links(send_sems, recv_sems)
    ring_z, ring_x = Ring(links, "z", z), Ring(links, "x", x)
    partner = {"c": 1 - c}

    def block(p):
        return c * 512 + p * 128

    def block_partner(p):
        return (1 - c) * 512 + p * 128

    own = rows(block(z), 128)
    loads = [pltpu.make_async_copy(tok_ref, xg.at[own], local_sems.at[0])]
    loads.append(pltpu.make_async_copy(cot_ref, cotg.at[own], local_sems.at[1]))
    for k in range(3):
        loads.append(pltpu.make_async_copy(wi_ref.at[k], wi_own.at[:, pl.ds(128 * k, 128)], local_sems.at[2 + k]))
    for load in loads:
        load.start()

    barrier = pltpu.get_barrier_semaphore()
    peers = [{"x": ring_x.right}, {"x": ring_x.left}, {"x": ring_x.far}]
    for dh in range(2):
        for dz in range(4):
            if dh or dz:
                peers.append({"yh": lax.rem(yh + dh, 2), "z": lax.rem(z + dz, 4)})
    for dl in range(2):
        for dc in range(2):
            for dh in range(2):
                if dl or dc:
                    peers.append({"yl": lax.rem(yl + dl, 2), "c": lax.rem(c + dc, 2), "yh": lax.rem(yh + dh, 2)})
    for dz in (1, 2, 3):
        peers.append({"c": 1 - c, "z": lax.rem(z + dz, 4)})
    for peer in peers:
        pl.semaphore_signal(barrier, inc=1, device_id=peer, device_id_type=MESH)
    sm_parts[...] = jnp.zeros_like(sm_parts)
    sm_parts[0:2, 0:64] = gain_ref[...].astype(F32)
    sm_parts[2:6, 0:64] = off_ref[...].astype(F32)
    sm_parts[22:23, 0:32] = hid_ref[...].astype(F32)
    sm_parts[39:40, 0:8] = head_ref[0:1].astype(F32)
    sm_parts[40:41, 0:8] = head_ref[1:2].astype(F32)
    placed = pltpu.roll(sm_parts[0:16], c * 64, 1) + pltpu.roll(sm_parts[16:32], lax.rem(dp, 4) * 32, 1)
    sm_own[...] = (placed + pltpu.roll(sm_parts[32:48], dp * 8, 1)).astype(BF16)
    for load in loads:
        load.wait()
    pl.semaphore_wait(barrier, len(peers))

    w_sm = WeightGather(ring_x, me, sm, 16, sm_own)
    w_kv = WeightGather(ring_x, me, wi.at[:, pl.ds(128, 256)], 64, wi_own.at[:, pl.ds(128, 256)])
    w_q = WeightGatherAlongX(ring_x, me, wq_all, wq_line)
    w_o = WeightGather(ring_x, me, wo, 64, wo_ref)
    w_e = WeightGather(ring_x, me, we, 64, we_ref)
    w_c = WeightGather(ring_x, me, wc, 64, wc_ref)
    w_sm.start()
    w_kv.start()
    wq_line[x] = wi_own[:, 0:128]
    w_q.gather.start()
    gather_x = RingGather(ring_z, xg, block, 64, partner, block_partner)
    gather_x.start()
    w_o.start()
    w_sm.start_x()
    w_e.start()
    w_c.start()
    w_kv.start_x()
    w_q.gather.forward()
    w_o.start_x()
    gather_x.forward()
    w_q.start_y()
    w_sm.gather.forward()
    w_kv.gather.forward()
    gather_x.done()
    gather_c = RingGather(ring_z, cotg, block, 64, partner, block_partner)
    gather_c.start()
    w_sm.gather.done()

    tiles = [sm[pl.ds(16 * k, 16)].astype(F32) for k in range(16)]
    pairs = [tiles[2 * k] + tiles[2 * k + 1] for k in range(8)]
    vectors = jnp.concatenate(pairs, axis=1)
    gains, offs = vectors[0:2], vectors[2:6]
    fours = [pairs[2 * k] + pairs[2 * k + 1] for k in range(4)]
    hidden_bias = jnp.concatenate([f[6:7] for f in fours], axis=1)
    every = fours[0] + fours[1] + fours[2] + fours[3]
    qkv_bias = jnp.concatenate([every[7:8], jnp.zeros((1, 128), F32), every[8:9]], axis=1)
    gain1, gain2 = gains[0:1], gains[1:2]
    off0, off1, off2, off3 = (offs[k : k + 1] for k in range(4))

    @pl.loop(0, 4)
    def _(i):
        r = rows(i * 256, 256)
        normed, _ = norm_rows(xg[r].astype(F32))
        h1[r] = (normed * gain1 + off0).astype(BF16)

    w_kv.gather.done()
    w_o.gather.forward()

    kv_slots = links.slots(2)
    kv_copies = []
    for s in range(2):
        part = pl.ds(s * 512, 512)
        kv_copies.append(links.make(qkv.at[part, pl.ds(128, 256)], kvr.at[part], kv_slots + s, {"yh": 1}))
        links.open.append((yh == 0, kv_copies[s]))

    @pl.loop(0, 4)
    def _(i):
        r = rows(i * 256, 256)
        qkv[r, 128:384] = (nn(h1[r], wi[:, 128:384]) + qkv_bias[:, 128:384]).astype(BF16)
        for s in range(2):
            pl.when((i == 2 * s + 1) & (yh == 0))(kv_copies[s].start)

    w_q.done()
    wi[:, 0:128] = wq_all[...].reshape(1024, 128)

    @pl.loop(0, 4)
    def _(i):
        r = rows(i * 256, 256)
        qkv[r, 0:128] = (nn(h1[r], wi[:, 0:128]) + qkv_bias[:, 0:128]).astype(BF16)

    w_o.gather.done()
    w_e.start_x()
    w_c.start_x()
    rank = c * 4 + z
    wo_all[:, rows(rank * 128, 128)] = wo[...]
    gather_o = ColumnGather(ring_z, c, wo_all, partner)
    gather_c.forward()
    gather_o.start()

    lane = lax.broadcasted_iota(jnp.int32, (1, 128), 1)
    head_lanes = [lane < 64, lane >= 64]

    def causal(scores, first):
        r = lax.broadcasted_iota(jnp.int32, scores.shape, 0) + first
        return jnp.where(r >= lax.broadcasted_iota(jnp.int32, scores.shape, 1), scores, MASKED)

    def masked(value, h):
        return jnp.where(head_lanes[h], value, jnp.zeros_like(value))

    def attend():
        @pl.loop(0, 2)
        def _(s):
            for qb in range(2):
                nk = 256 * (qb + 1)
                r = rows(s * 512 + qb * 256, 256)
                keys = rows(s * 512, nk, 512)
                q, k, v = qkv[r, 0:128], qkv[keys, 128:256], qkv[keys, 256:384]
                outs = []
                for h in range(2):
                    near = causal(nt(masked(q, h), k) * SCALE, qb * 256)
                    peak = jnp.max(near, axis=-1, keepdims=True)
                    near = jnp.exp(near - peak)
                    top[h, r] = peak
                    low_sum[h, r] = jnp.sum(near, axis=-1, keepdims=True)
                    outs.append(nn(near.astype(BF16), v))
                att_f[r] = jnp.where(head_lanes[0], outs[0], outs[1])

    def finish(remote):
        @pl.loop(0, 4)
        def _(i):
            r = rows(i * 256, 256)
            keys = rows((i // 2) * 512, 512)
            outs = []
            for h in range(2):
                peak, total, o = top[h, r], low_sum[h, r], att_f[r]
                if remote:
                    far = nt(masked(qkv[r, 0:128], h), kvr[keys, 0:128]) * SCALE
                    higher = jnp.maximum(peak, jnp.max(far, axis=-1, keepdims=True))
                    far = jnp.exp(far - higher)
                    shrink = jnp.exp(peak - higher)
                    total = total * shrink + jnp.sum(far, axis=-1, keepdims=True)
                    o = o * shrink + nn(far.astype(BF16), kvr[keys, 128:256])
                    peak = higher
                outs.append(o * (1.0 / total))
                lse[h, r] = peak + jnp.log(total)
            o = jnp.where(head_lanes[0], outs[0], outs[1])
            att_f[r] = o
            att[r] = o.astype(BF16)

    attend()
    gather_o.forward()
    gather_c.done()
    pl.when(yh == 0)(functools.partial(finish, False))

    @pl.when(yh == 1)
    def _():
        for s in range(2):
            links.wait(kv_slots + s, kvr.at[pl.ds(s * 512, 512)], {"yh": 0})
        finish(True)

    swap_a = Swap(ring_z, c, 128)
    swap_a.start(att, att_in)
    x_own = xg[own].astype(F32)
    cot_own = cotg[own].astype(F32)
    w_e.gather.forward()
    w_c.gather.forward()
    gather_o.done()
    swap_a.done(att_in)
    joined = jnp.concatenate([att_in[128 * k : 128 * k + 128] for k in range(8)], axis=1)
    resid[...] = x_own + nt(joined, wo_all[...]) + off1
    normed2, inverse2 = norm_rows(resid[...])
    h2[own] = (normed2 * gain2 + off2).astype(BF16)
    gather_h = RingGather(ring_z, h2, block, 64, partner, block_partner)
    gather_h.start()
    w_e.gather.done()
    w_c.gather.done()
    vec_t[...] = jnp.transpose(vectors)
    gather_h.forward()

    hb_sum[...] = jnp.zeros_like(hb_sum)

    def mlp_tile(pos):
        near_rows, next_rows = rows(pos * 128, 128), rows(512 + pos * 128, 128)

        def load(ref):
            return jnp.concatenate([ref[near_rows], ref[next_rows]], axis=0)

        def store(ref, value):
            ref[near_rows] = value[0:128]
            ref[next_rows] = value[128:256]

        p = nn(load(h2), we[...]) + hidden_bias
        square = p * p
        t = jnp.tanh(GELU_COEF * (p + CUBIC * p * square))
        store(hid, (0.5 * p * (1.0 + t)).astype(BF16))
        slope = 0.5 * (1.0 + t) + 0.5 * p * (1.0 - t * t) * (GELU_COEF * (1.0 + 3.0 * CUBIC * square))
        g = (nn(load(cotg), wc[...]) * slope).astype(BF16)
        store(gp, g)
        hb_sum[...] += jnp.sum(g.astype(F32), axis=0, keepdims=True)
        store(part_2, nt(g, we[...]).astype(BF16))

    sum_2 = GroupSum(ring_z, c, part_2, core_2, near_2)
    sum_2.run_by_chip(mlp_tile, gather_h)

    def weight_grad(out, left, right):
        @pl.loop(0, 4)
        def _(i):
            r = rows(i * 256, 256)
            out[r] = tn(left[:, r], right[...]).astype(BF16)

    g_e = WeightSum(ring_x, me, ge, 64, land_e, landy_e)
    g_c = WeightSum(ring_x, me, gc, 64, land_c, landy_c)
    weight_grad(ge, h2, gp)
    g_e.start()
    sum_2.middle()
    weight_grad(gc, cotg, hid)
    g_c.start()

    grad2 = sum_2.total()
    gres[...] = cot_own + norm_back(grad2, normed2, inverse2, gain2)
    grad_branch = gres[...].astype(BF16)
    gbg[own] = grad_branch
    for k in range(4):
        g = nn(grad_branch, wo_all[:, 256 * k : 256 * k + 256]).astype(BF16)
        gatt_out[256 * k : 256 * k + 128] = g[:, 0:128]
        gatt_out[256 * k + 128 : 256 * k + 256] = g[:, 128:256]
    swap_g = Swap(ring_z, c, 128)
    swap_g.start(gatt_out, gatt)
    gather_b = RingGather(ring_z, gbg, block, 64, partner, block_partner)
    gather_b.start()
    vec[1:2] = jnp.sum(grad2 * normed2, axis=0, keepdims=True)
    vec[3:4] = jnp.sum(grad_branch.astype(F32), axis=0, keepdims=True)
    vec[4:5] = jnp.sum(grad2, axis=0, keepdims=True)
    vec[5:6] = jnp.sum(cot_own, axis=0, keepdims=True)

    def out_tile(r):
        part_o[r] = nt(hid[r], wc[...]).astype(BF16)

    sum_o = GroupSum(ring_z, c, part_o, core_o, near_o)
    sum_o.run(out_tile)
    g_e.middle()
    swap_g.done(gatt)

    @pl.loop(0, 4)
    def _(i):
        r = rows(i * 256, 256)
        product = gatt[r].astype(F32) * att_f[r]
        for h in range(2):
            delta[h, r] = jnp.sum(masked(product, h), axis=-1, keepdims=True)

    gather_b.forward()
    g_c.middle()
    gkv_slots = links.slots(2)
    gkv_copies = []
    for s in range(2):
        part = pl.ds(s * 512, 512)
        gkv_copies.append(links.make(gkv_out.at[part], gkv_in.at[part], gkv_slots + s, {"yh": 0}))
        links.open.append((yh == 1, gkv_copies[s]))

    def attend_far():
        @pl.loop(0, 2)
        def _(s):
            seq = rows(s * 512, 512)
            k, v = kvr[seq, 0:128], kvr[seq, 128:256]
            dk0_acc[...] = jnp.zeros_like(dk0_acc)
            dv0_acc[...] = jnp.zeros_like(dv0_acc)

            @pl.loop(0, 2)
            def _(qb):
                r = rows(s * 512 + qb * 256, 256)
                q, g = qkv[r, 0:128], gatt[r]
                outs = []
                for h in range(2):
                    qm, gm = masked(q, h), masked(g, h)
                    far = jnp.exp(nt(qm, k) * SCALE - lse[h, r])
                    far_s = (far * (nt(gm, v) - delta[h, r])).astype(BF16)
                    dk0_acc[...] += tn(far_s, qm)
                    dv0_acc[...] += tn(far.astype(BF16), gm)
                    outs.append(nn(far_s, k))
                gq_f[r] = jnp.where(head_lanes[0], outs[0], outs[1])

            gkv_out[seq, 0:128] = (dk0_acc[...] * SCALE).astype(BF16)
            gkv_out[seq, 128:256] = dv0_acc[...].astype(BF16)
            for k in range(2):
                pl.when(s == k)(gkv_copies[k].start)

    def attend_back():
        @pl.loop(0, 2)
        def _(s):
            dk_acc[...] = jnp.zeros_like(dk_acc)
            dv_acc[...] = jnp.zeros_like(dv_acc)
            seq = rows(s * 512, 512)
            for qb in range(2):
                nk = 256 * (qb + 1)
                r = rows(s * 512 + qb * 256, 256)
                keys = rows(s * 512, nk, 512)
                q, k, v, g = qkv[r, 0:128], qkv[keys, 128:256], qkv[keys, 256:384], gatt[r]
                outs = []
                for h in range(2):
                    qm, gm = masked(q, h), masked(g, h)
                    near = jnp.exp(causal(nt(qm, k) * SCALE, qb * 256) - lse[h, r])
                    near_s = (near * (nt(gm, v) - delta[h, r])).astype(BF16)
                    dk_acc[0:nk] += tn(near_s, qm)
                    dv_acc[0:nk] += tn(near.astype(BF16), gm)
                    outs.append(nn(near_s, k))
                total = gq_f[r] + jnp.where(head_lanes[0], outs[0], outs[1])
                gqkv[r, 0:128] = (total * SCALE).astype(BF16)
            gqkv[seq, 128:256] = (dk_acc[...] * SCALE).astype(BF16)
            gqkv[seq, 256:384] = dv_acc[...].astype(BF16)

    @pl.when(yh == 0)
    def _():
        gq_f[...] = jnp.zeros_like(gq_f)

    pl.when(yh == 1)(attend_far)
    g_e.start_y()
    sum_o.start()
    gather_b.done()
    attend_back()
    sum_o.middle()
    weight_grad(go, gbg, att)
    g_o = WeightSum(ring_x, me, go, 64, land_o, landy_o)
    g_o.start()

    @pl.when(yh == 0)
    def _():
        for s in range(2):
            links.wait(gkv_slots + s, gkv_in.at[pl.ds(s * 512, 512)], {"yh": 1})

            @pl.loop(0, 2)
            def _(k):
                r = rows(s * 512 + k * 256, 256)
                gqkv[r, 128:384] = (gqkv[r, 128:384].astype(F32) + gkv_in[r].astype(F32)).astype(BF16)

    def grad1_tile(r):
        part_1[r] = nt(gqkv[r], wi[...]).astype(BF16)

    sum_1 = GroupSum(ring_z, c, part_1, core_1, near_1)
    sum_1.run(grad1_tile)
    sum_1.start()
    head_sums = jnp.sum(gqkv[...].astype(F32), axis=0, keepdims=True)

    @pl.loop(0, 4)
    def _(i):
        r = rows(i * 256, 256)
        g = tn(h1[:, r], gqkv[...])
        gi[r] = g.astype(BF16)
        weight = wi[r].astype(F32)
        off_grad = jnp.sum(weight * head_sums, axis=-1, keepdims=True)
        mixed = jnp.sum(weight * g, axis=-1, keepdims=True)
        gain_grad = (mixed - vec_t[r, 2:3] * off_grad) / vec_t[r, 0:1]
        columns[r] = jnp.where(lane == 0, gain_grad, jnp.where(lane == 2, off_grad, 0.0))

    g_i = WeightSum(ring_x, me, gi, 64, land_i, landy_i)
    g_i.start()
    turned = jnp.transpose(columns[...])
    vec[0:1] = turned[0:1]
    vec[2:3] = turned[2:3]
    hb = hb_sum[...]
    vec[6:7] = jnp.concatenate([hb[:, 128 * (k // 2) : 128 * (k // 2) + 128] for k in range(8)], axis=1)
    vec[7:8] = jnp.concatenate([head_sums[:, 0:128]] * 8, axis=1)
    vec[8:9] = jnp.concatenate([head_sums[:, 256:384]] * 8, axis=1)
    vec[9:16] = jnp.zeros((7, 1024), F32)
    for k in range(16):
        gs[pl.ds(16 * k, 16)] = vec[:, 128 * (k // 2) : 128 * (k // 2) + 128].astype(BF16)
    g_s = SmallSum(ring_x, me, gs, 16, land_s, landy_s)
    g_s.start()
    sum_1.middle()
    g_o.middle()
    g_c.start_y()
    out_ref[...] = (resid[...] + sum_o.total() + off3).astype(BF16)
    g_s.start_y()
    g_o.start_y()
    g_i.middle()
    normed1, inverse1 = norm_rows(x_own)
    gtok_ref[...] = gres[...] + norm_back(sum_1.total(), normed1, inverse1, gain1)
    tile = g_s.finish()
    slot = yh * 4 + z
    tens[rows(slot * 16, 16)] = tile
    mine = tens.at[rows(slot * 16, 16)]
    t_ids = links.slots(8)
    others = [(dh, dz) for dh in range(2) for dz in range(4) if dh or dz]
    for dh, dz in others:
        links.send(mine, mine, t_ids + slot, {"yh": lax.rem(yh + dh, 2), "z": lax.rem(z + dz, 4)})
    g_i.start_y()
    gwe_ref[...] = g_e.finish()
    gwc_ref[...] = g_c.finish()
    gwo_ref[...] = g_o.finish()
    for dh, dz in others:
        theirs = lax.rem(yh + dh, 2) * 4 + lax.rem(z + dz, 4)
        ref = tens.at[rows(theirs * 16, 16)]
        links.wait(t_ids + theirs, ref, {"yh": lax.rem(yh + dh, 2), "z": lax.rem(z + dz, 4)})
    total = tens[0:16]
    for k in range(1, 8):
        total = total + tens[16 * k : 16 * k + 16]
    gsm_ref[0:6] = total[0:6]
    gsm_ref[6:16] = tile[6:16]
    gwi_ref[...] = g_i.finish()
    links.drain()


def final_kernel(
    out_k, gtok_k, gwi, gwo, gwe, gwc, gsm,
    out_ref, gtok_ref, gi_ref, go_ref, ge_ref, gc_ref, head_ref, hid_ref, gain_ref, off_ref,
):
    c = lax.axis_index("c")
    dp = lax.axis_index("x") * 4 + lax.axis_index("yl") * 2 + c
    out_ref[...] = out_k[...]
    gtok_ref[...] = gtok_k[...]
    for k in range(3):
        gi_ref[k] = gwi[:, 128 * k : 128 * k + 128]
    go_ref[...] = gwo[...]
    ge_ref[...] = gwe[...]
    gc_ref[...] = gwc[...]
    small = gsm[...]
    mine = pltpu.roll(small, lax.rem(128 - c * 64, 128), 1)
    gain_ref[...] = mine[0:2, 0:64]
    off_ref[...] = mine[2:6, 0:64]
    hid_ref[...] = pltpu.roll(small, lax.rem(128 - lax.rem(dp, 4) * 32, 128), 1)[6:7, 0:32]
    heads = pltpu.roll(small, lax.rem(128 - dp * 8, 128), 1)
    head_ref[0] = heads[7:8, 0:8]
    head_ref[1] = heads[8:9, 0:8]


def per_device(tokens, input_proj, output_proj, expand_proj, contract_proj, head_bias, hidden_bias, norm_gains, offsets, cotangent):
    vmem = pl.BlockSpec(memory_space=pltpu.VMEM)
    shape = jax.ShapeDtypeStruct
    widths = (384, 128, 512, 512)

    def buf(r, n, t=BF16):
        return pltpu.VMEM((r, n), t)

    scratch = [buf(1024, 1024) for _ in range(5)]
    scratch += [buf(1024, n) for n in widths] + [buf(256, 128)]
    scratch += [buf(1024, n) for n in widths] + [buf(256, 128)]
    scratch += [buf(768, n) for n in widths] + [buf(256, 128)]
    scratch += [buf(256, n) for n in widths] + [buf(64, 128)]
    scratch += [buf(1024, 1024) for _ in range(3)] + [buf(512, 1024) for _ in range(3)]
    scratch += [buf(384, 1024) for _ in range(3)]
    scratch += [buf(1024, 1024), buf(1024, 128), buf(1024, 128)]
    scratch += [buf(1024, 384), buf(1024, 384), buf(1024, 256), buf(1024, 256), buf(1024, 256)]
    scratch += [buf(1024, 128), buf(1024, 128), buf(1024, 512), buf(1024, 512)]
    scratch += [pltpu.VMEM((2, 1024, 1), F32)] + [buf(512, 128, F32) for _ in range(4)]
    scratch += [buf(128, 1024, F32), buf(128, 1024, F32), buf(16, 1024, F32), buf(128, 128, F32)]
    scratch += [buf(1, 512, F32), buf(64, 384), buf(16, 128), buf(48, 128, F32)]
    scratch += [pltpu.VMEM((2, 1024, 1), F32), pltpu.VMEM((2, 1024, 1), F32)]
    scratch += [buf(1024, 128, F32), buf(1024, 128, F32), pltpu.VMEM((2, 1024, 1), F32)]
    scratch += [buf(1024, 128, F32), buf(1024, 16, F32)]
    scratch += [pltpu.VMEM((4, 4, 64, 128), BF16), pltpu.VMEM((4, 64, 128), BF16)]
    scratch += [pltpu.SemaphoreType.DMA((N_SEMS,)), pltpu.SemaphoreType.DMA((N_SEMS,))]
    scratch += [pltpu.SemaphoreType.DMA((8,))]
    out, gtok, gwi, gwo, gwe, gwc, gsm = pl.pallas_call(
        layer_kernel,
        out_shape=(
            shape((128, 1024), BF16),
            shape((128, 1024), F32),
            *(shape((64, n), F32) for n in widths),
            shape((16, 128), F32),
        ),
        in_specs=[pl.BlockSpec(memory_space=pl.ANY)] * 6 + [vmem] * 4,
        out_specs=[vmem] * 7,
        scratch_shapes=scratch,
        compiler_params=pltpu.CompilerParams(
            collective_id=0, has_side_effects=True, vmem_limit_bytes=58 * 1024 * 1024
        ),
    )(
        tokens, cotangent, input_proj, output_proj.T, expand_proj, contract_proj.T,
        norm_gains, offsets, hidden_bias, head_bias.reshape(2, 8),
    )
    outs = pl.pallas_call(
        final_kernel,
        out_shape=(
            shape((128, 1024), BF16),
            shape((128, 1024), F32),
            shape((3, 64, 128), F32),
            shape((64, 128), F32),
            shape((64, 512), F32),
            shape((64, 512), F32),
            shape((2, 1, 8), F32),
            shape((1, 32), F32),
            shape((2, 64), F32),
            shape((4, 64), F32),
        ),
        in_specs=[vmem] * 7,
        out_specs=[vmem] * 10,
    )(out, gtok, gwi, gwo, gwe, gwc, gsm)
    return (*outs[:3], outs[3].T, outs[4], outs[5].T, *outs[6:])


def solution(mesh):
    split = Mesh(mesh.devices.reshape(4, 2, 2, 2, 4), ("x", "yl", "c", "yh", "z"))
    token_rows = P(DP + TENSOR, None)
    weights = (
        P(None, DP, TENSOR),
        P(TENSOR, DP),
        P(DP, TENSOR),
        P(TENSOR, DP),
        P(None, TENSOR, DP),
        P(TENSOR, DP),
        P(None, DP),
        P(None, DP),
    )
    return jax.shard_map(
        per_device,
        mesh=split,
        in_specs=(token_rows, *weights, token_rows),
        out_specs=(token_rows, token_rows, *weights),
        check_vma=False,
    )
```

```python
import functools

import jax
import jax.numpy as jnp
from jax import lax
from jax.experimental import pallas as pl
from jax.experimental.pallas import tpu as pltpu
from jax.sharding import Mesh
from jax.sharding import PartitionSpec as P

F32, BF16 = jnp.float32, jnp.bfloat16
MESH = pl.DeviceIdType.MESH
DP = ("x", "yl", "c")
TENSOR = ("yh", "z")
EPSILON = 1e-05
MASKED = -1000000000.0
GELU_COEF = 0.7978845608028654
CUBIC = 0.044715
SCALE = 64 ** (-0.5)
SENDS = 140
RECEIVES = 236


def nn(a, b):
    return lax.dot_general(a, b, (((1,), (0,)), ((), ())), preferred_element_type=F32)


def nt(a, b):
    return lax.dot_general(a, b, (((1,), (1,)), ((), ())), preferred_element_type=F32)


def tn(a, b):
    return lax.dot_general(a, b, (((0,), (0,)), ((), ())), preferred_element_type=F32)


def rows(start, size, by=None):
    if isinstance(start, int):
        return pl.ds(start, size)
    return pl.ds(pl.multiple_of(start, by or size), size)


def norm_rows(v):
    shifted = v - jnp.mean(v, axis=-1, keepdims=True)
    inverse = lax.rsqrt(jnp.mean(shifted * shifted, axis=-1, keepdims=True) + EPSILON)
    return shifted * inverse, inverse


def norm_back(grad, normed, inverse, gain):
    scaled = grad * gain
    first = jnp.mean(scaled, axis=-1, keepdims=True)
    second = jnp.mean(scaled * normed, axis=-1, keepdims=True)
    return inverse * (scaled - first - normed * second)


class Links:
    def __init__(self, send_sems, recv_sems):
        self.send_sems, self.recv_sems = send_sems, recv_sems
        self.sent, self.received, self.open, self.free, self.mark = 0, 0, [], [], 0

    def outgoing(self, count):
        first = self.sent
        self.sent += count
        assert self.sent <= SENDS, self.sent
        return first

    def slots(self, count):
        first = self.received
        self.received += count
        assert self.received <= RECEIVES, self.received
        return first

    def make(self, src, dst, recv, to):
        self.last = self.free.pop(0) if self.free else self.outgoing(1)
        return pltpu.make_async_remote_copy(
            src_ref=src,
            dst_ref=dst,
            send_sem=self.send_sems.at[self.last],
            recv_sem=self.recv_sems.at[recv],
            device_id=to,
            device_id_type=MESH,
        )

    def keep(self, copy, cond=None):
        self.open.append((self.last, cond, copy))

    def send(self, src, dst, recv, to, like=None):
        copy = self.make(src, dst, recv, to)
        copy.start()
        if like is not None:
            copy = like
        self.keep(copy)

    def send_if(self, cond, src, dst, recv, to):
        copy = self.make(src, dst, recv, to)
        pl.when(cond)(copy.start)
        self.keep(copy, cond)

    def local_if(self, cond, src, dst, recv):
        copy = pltpu.make_async_copy(src, dst, self.recv_sems.at[recv])
        pl.when(cond)(copy.start)

    def wait(self, recv, ref, to):
        pltpu.make_async_remote_copy(
            src_ref=ref,
            dst_ref=ref,
            send_sem=self.send_sems.at[0],
            recv_sem=self.recv_sems.at[recv],
            device_id=to,
            device_id_type=MESH,
        ).wait_recv()

    def drain(self, count):
        for sem, cond, copy in self.open[:count]:
            if not hasattr(copy, "wait_send"):
                copy = pltpu.make_async_remote_copy(
                    src_ref=copy,
                    dst_ref=copy,
                    send_sem=self.send_sems.at[sem],
                    recv_sem=self.recv_sems.at[0],
                    device_id={"c": 0},
                    device_id_type=MESH,
                )
            if cond is None:
                copy.wait_send()
            else:
                pl.when(cond)(copy.wait_send)
            if sem is not None:
                self.free.append(sem)
        self.open = self.open[count:]

    def settle(self):
        self.drain(self.mark)
        self.mark = len(self.open)


class Ring:
    def __init__(self, links, axis, pos):
        self.links, self.axis = links, axis
        self.pos = pos
        self.right, self.left, self.far = (lax.rem(pos + k, 4) for k in (1, 3, 2))
        self.to_right, self.to_left = {axis: self.right}, {axis: self.left}


class RingGather:
    def __init__(self, ring, buf, offset, half, partner=None, offset_partner=None):
        self.ring, self.buf, self.offset, self.half = ring, buf, offset, half
        self.partner, self.offset_partner = partner, offset_partner
        self.ids = ring.links.slots(6)
        if partner is not None:
            self.pids = ring.links.slots(8)

    def at(self, pos, part, offset=None):
        return self.buf.at[rows((offset or self.offset)(pos) + part * self.half, self.half)]

    def like(self):
        return self.buf.at[pl.ds(0, self.half)]

    def relay(self, pos, part, slot):
        if self.partner is not None:
            ref = self.at(pos, part)
            self.ring.links.send(ref, ref, self.pids + slot, self.partner, self.like())

    def start(self):
        r, s = self.ring, self.ring.links.send
        a, b = self.at(r.pos, 0), self.at(r.pos, 1)
        s(a, a, self.ids + 0, r.to_right)
        s(b, b, self.ids + 3, r.to_left)
        s(b, b, self.ids + 1, r.to_right)
        s(a, a, self.ids + 2, r.to_left)
        self.relay(r.pos, 0, 0)
        self.relay(r.pos, 1, 1)

    def forward(self):
        r, s, w = self.ring, self.ring.links.send, self.ring.links.wait
        ref = self.at(r.left, 0)
        w(self.ids + 0, ref, r.to_left)
        s(ref, ref, self.ids + 4, r.to_right)
        ref = self.at(r.right, 1)
        w(self.ids + 3, ref, r.to_right)
        s(ref, ref, self.ids + 5, r.to_left)
        self.relay(r.left, 0, 2)
        self.relay(r.right, 1, 5)

    def done(self):
        self.near()
        self.far()
        self.own()

    def near(self):
        r, w = self.ring, self.ring.links.wait
        w(self.ids + 1, self.at(r.left, 1), r.to_left)
        self.relay(r.left, 1, 3)
        w(self.ids + 2, self.at(r.right, 0), r.to_right)
        self.relay(r.right, 0, 4)
        self.relayed(2, ((r.left, 0), (r.left, 1), (r.right, 0), (r.right, 1)))

    def far(self):
        r, w = self.ring, self.ring.links.wait
        w(self.ids + 4, self.at(r.far, 0), r.to_left)
        self.relay(r.far, 0, 6)
        w(self.ids + 5, self.at(r.far, 1), r.to_right)
        self.relay(r.far, 1, 7)
        self.relayed(6, ((r.far, 0), (r.far, 1)))

    def own(self):
        r = self.ring
        self.relayed(0, ((r.pos, 0), (r.pos, 1)))

    def relayed(self, first, blocks):
        if self.partner is not None:
            for k, (pos, part) in enumerate(blocks):
                self.ring.links.wait(self.pids + first + k, self.at(pos, part, self.offset_partner), self.partner)


class ColumnGather(RingGather):
    def __init__(self, ring, c, buf, partner):
        super().__init__(ring, buf, c, buf.shape[0] // 2, partner, 1 - c)

    def at(self, pos, part, core=None):
        rank = (self.offset if core is None else core) * 4 + pos
        return self.buf.at[pl.ds(part * self.half, self.half), rows(rank * 128, 128)]

    def like(self):
        return self.buf.at[pl.ds(0, self.half), pl.ds(0, 128)]


class FirstGather(RingGather):
    def at(self, pos, part, offset=None):
        return self.buf.at[pos, pl.ds(part * self.half, self.half)]

    def like(self):
        return self.buf.at[0, pl.ds(0, self.half)]


class WeightGatherAlongX:
    def __init__(self, ring, me, buf, line):
        self.ring, self.me, self.buf, self.line = ring, me, buf, line
        self.gather = FirstGather(ring, line, None, line.shape[1] // 2)
        self.ids = ring.links.slots(4)

    def start_y(self):
        x, yl, c, yh, z = self.me
        links = self.ring.links
        self.gather.done()
        slot = yl * 2 + c
        dst = self.buf.at[:, slot]
        for dl, dh in ((1, 0), (0, 1), (1, 1)):
            to = {"yl": lax.rem(yl + dl, 2), "yh": lax.rem(yh + dh, 2), "c": yh}
            links.send(self.line, dst, self.ids + slot, to)
        links.local_if(c == yh, self.line, dst, self.ids + slot)
        links.send_if(c != yh, self.line, dst, self.ids + slot, {"c": yh})

    def done(self):
        for k in range(4):
            self.ring.links.wait(self.ids + k, self.buf.at[:, k], {"c": 1 - self.me[2]})


class Swap:
    def __init__(self, ring, c, size):
        self.ring, self.c, self.size = ring, c, size
        self.rank = c * 4 + ring.pos
        self.ids = ring.links.slots(8)
        self.others = [(dc, dz) for dz in (2, 1, 3, 0) for dc in (0, 1) if dc or dz]

    def peer(self, dc, dz):
        return lax.rem(self.c + dc, 2), lax.rem(self.ring.pos + dz, 4)

    def tile(self, buf, rank):
        return buf.at[rows(rank * self.size, self.size)]

    def start(self, src, dst):
        for dc, dz in self.others:
            to_c, to_z = self.peer(dc, dz)
            to = {"c": to_c, "z": to_z}
            self.ring.links.send(self.tile(src, to_c * 4 + to_z), self.tile(dst, self.rank), self.ids + self.rank, to)
        self.tile(dst, self.rank)[...] = self.tile(src, self.rank)[...]

    def done(self, dst):
        for dc, dz in self.others:
            of_c, of_z = self.peer(dc, dz)
            theirs = of_c * 4 + of_z
            self.ring.links.wait(self.ids + theirs, self.tile(dst, theirs), {"c": of_c, "z": of_z})


class RingSum:
    def __init__(self, ring, buf, offset, half, land):
        self.ring, self.buf, self.offset, self.half, self.land = ring, buf, offset, half, land
        self.ids = ring.links.slots(6)

    def at(self, pos, part, count=1):
        return self.buf.at[rows(self.offset(pos) + part * self.half, self.half * count, self.half)]

    def landing(self, slot):
        return self.land.at[pl.ds(slot * self.half, self.half)]

    def send(self, src, slot, to):
        like = self.buf.at[pl.ds(0, self.half)]
        self.ring.links.send(src, self.landing(slot), self.ids + slot, to, like)

    def wait(self, slot, to):
        self.ring.links.wait(self.ids + slot, self.landing(slot), to)

    def add(self, pos, part, slot):
        ref = self.at(pos, part)
        ref[...] = (ref[...].astype(F32) + self.landing(slot)[...].astype(F32)).astype(BF16)

    def send_far(self):
        r = self.ring
        self.send(self.at(r.far, 0), 0, r.to_right)
        self.send(self.at(r.far, 1), 1, r.to_left)

    def send_near(self):
        r = self.ring
        self.send(self.at(r.right, 1), 3, r.to_right)
        self.send(self.at(r.left, 0), 4, r.to_left)

    def middle(self):
        r = self.ring
        self.wait(0, r.to_left)
        self.add(r.right, 0, 0)
        self.send(self.at(r.right, 0), 2, r.to_right)
        self.wait(1, r.to_right)
        self.add(r.left, 1, 1)
        self.send(self.at(r.left, 1), 5, r.to_left)

    def total(self):
        r = self.ring
        self.wait(3, r.to_left)
        self.wait(4, r.to_right)
        self.wait(2, r.to_left)
        self.wait(5, r.to_right)
        own = self.at(r.pos, 0, 2)[...].astype(F32)
        left = self.land[pl.ds(2 * self.half, 2 * self.half)].astype(F32)
        right = self.land[pl.ds(4 * self.half, 2 * self.half)].astype(F32)
        return own + left + right


class GroupSum:
    def __init__(self, ring, c, buf, from_core, land):
        self.links, self.c, self.buf, self.from_core = ring.links, c, buf, from_core
        self.partner = {"c": 1 - c}
        self.order = (ring.far, ring.right, ring.left, ring.pos)
        self.ids, self.out_ids = ring.links.slots(4), ring.links.outgoing(4)
        self.sum = RingSum(ring, buf, lambda p: c * 512 + p * 128, 64, land)

    def core_copy(self, pos):
        return pltpu.make_async_remote_copy(
            src_ref=self.buf.at[rows((1 - self.c) * 512 + pos * 128, 128)],
            dst_ref=self.from_core.at[rows(pos * 128, 128)],
            send_sem=self.links.send_sems.at[self.out_ids + pos],
            recv_sem=self.links.recv_sems.at[self.ids + pos],
            device_id=self.partner,
            device_id_type=MESH,
        )

    def run(self, body):
        first = self.order[0] // 2

        @pl.loop(0, 4)
        def _(i):
            tile = lax.rem(first + i, 2)
            body(rows(lax.rem(1 - self.c + i // 2, 2) * 512 + tile * 256, 256))

            @pl.when(i < 2)
            def _():
                self.core_copy(tile * 2).start()
                self.core_copy(tile * 2 + 1).start()

        for pos in range(4):
            self.links.open.append((None, None, self.core_copy(pos)))

    def run_by_chip(self, body, gather):
        z = self.order[3]

        @pl.loop(0, 4)
        def _(i):
            pl.when(i == 0)(gather.own)
            pl.when(i == 1)(gather.near)

            @pl.when(i == 3)
            def _():
                gather.far()
                self.core_add(1)
                self.core_add(2)
                self.sum.send_near()

            pos = lax.rem(z + jnp.where(i == 2, 3, jnp.where(i == 3, 2, i)), 4)
            body(pos)
            self.core_copy(pos).start()

        for pos in range(4):
            self.links.open.append((None, None, self.core_copy(pos)))
        self.core_add(0)
        self.sum.send_far()

    def core_add(self, k):
        got = self.from_core.at[rows(self.order[k] * 128, 128)]
        self.links.wait(self.ids + self.order[k], got, self.partner)
        ref = self.buf.at[rows(self.c * 512 + self.order[k] * 128, 128)]
        ref[...] = (ref[...].astype(F32) + got[...].astype(F32)).astype(BF16)

    def start(self):
        self.core_add(0)
        self.sum.send_far()
        self.core_add(1)
        self.core_add(2)
        self.sum.send_near()

    def middle(self):
        self.sum.middle()
        self.core_add(3)

    def total(self):
        return self.sum.total()


class WeightGather:
    def __init__(self, ring, me, buf, size, shard):
        self.ring, self.me, self.buf, self.size, self.shard = ring, me, buf, size, shard
        self.ids = ring.links.slots(4)
        self.gather = RingGather(ring, buf, lambda p: p * 4 * size, 2 * size)

    def start(self):
        x, yl, c, yh, z = self.me
        links = self.ring.links
        own = self.buf.at[rows((x * 4 + yl * 2 + c) * self.size, self.size)]
        slot = self.ids + yl * 2 + c
        for dl, dh in ((1, 0), (0, 1), (1, 1)):
            to = {"yl": lax.rem(yl + dl, 2), "yh": lax.rem(yh + dh, 2), "c": yh}
            links.send(self.shard, own, slot, to)
        links.local_if(c == yh, self.shard, own, slot)
        links.send_if(c != yh, self.shard, own, slot, {"c": yh})

    def start_x(self):
        x, yl, c, yh, z = self.me
        for k in range(4):
            ref = self.buf.at[rows((x * 4 + k) * self.size, self.size)]
            self.ring.links.wait(self.ids + k, ref, {"c": 1 - c})
        self.gather.start()


class WeightSum:
    def __init__(self, ring, me, buf, size, land, land_y):
        self.ring, self.me, self.buf, self.size = ring, me, buf, size
        self.land_y = land_y
        self.sum = RingSum(ring, buf, lambda p: p * 4 * size, 2 * size, land)
        self.ids = ring.links.slots(4)

    def start(self):
        self.sum.send_far()
        self.sum.send_near()

    def middle(self):
        self.sum.middle()

    def x_total(self):
        return self.sum.total()

    def start_y(self):
        x, yl, c, yh, z = self.me
        links, size = self.ring.links, self.size
        total = self.x_total()
        self.buf[rows(x * 4 * size, 4 * size)] = total.astype(BF16)
        slot = yh * 2 + yl
        dst = self.land_y.at[rows(slot * size, size)]
        for dl, dc in ((1, 0), (0, 1), (1, 1), (0, 0)):
            to_l, to_c = lax.rem(yl + dl, 2), lax.rem(c + dc, 2)
            src = self.buf.at[rows((x * 4 + to_l * 2 + to_c) * size, size)]
            if dl or dc:
                links.send(src, dst, self.ids + slot, {"yl": to_l, "c": to_c, "yh": c})
            else:
                links.local_if(c == yh, src, dst, self.ids + slot)
                links.send_if(c != yh, src, dst, self.ids + slot, {"yh": c})

    def finish(self):
        c = self.me[2]
        total = 0.0
        for k in range(4):
            ref = self.land_y.at[pl.ds(k * self.size, self.size)]
            self.ring.links.wait(self.ids + k, ref, {"c": 1 - c})
            total = total + ref[...].astype(F32)
        return total


class SmallSum(WeightSum):
    def __init__(self, ring, me, buf, size, land, land_y):
        self.ring, self.me, self.buf, self.size = ring, me, buf, size
        self.land, self.land_y = land, land_y
        self.x_ids = ring.links.slots(4)
        self.ids = ring.links.slots(4)

    def start(self):
        x = self.me[0]
        for d in (2, 1, 3):
            to = lax.rem(x + d, 4)
            src = self.buf.at[rows(to * 4 * self.size, 4 * self.size)]
            dst = self.land.at[pl.ds(d * 4 * self.size, 4 * self.size)]
            self.ring.links.send(src, dst, self.x_ids + d, {"x": to})

    def x_total(self):
        x = self.me[0]
        total = self.buf[rows(x * 4 * self.size, 4 * self.size)].astype(F32)
        for d in (1, 3, 2):
            ref = self.land.at[pl.ds(d * 4 * self.size, 4 * self.size)]
            self.ring.links.wait(self.x_ids + d, ref, {"x": lax.rem(x + 4 - d, 4)})
            total = total + ref[...].astype(F32)
        return total


def layer_kernel(
    tok_ref, cot_ref, wi_ref, wo_ref, we_ref, wc_ref, gain_ref, off_ref, hid_ref, head_ref,
    out_ref, gtok_ref, gwi_ref, gwo_ref, gwe_ref, gwc_ref, gsm_ref,
    xg, cotg, h1, h2, gbg, wi, wo, we, wc, sm, gi, go, ge, gc, gs,
    land_i, land_o, land_e, land_c, land_s, landy_i, landy_o, landy_e, landy_c, landy_s,
    part_o, part_2, part_1, core_o, core_2, core_1, near_o, near_2, near_1, wo_all, att_in, gatt_out,
    qkv, gqkv, kvr, gkv_out, gkv_in, att, gatt, hid, gp, lse, dk_acc, dv_acc, dk0_acc, dv0_acc,
    resid, gres, vec, tens, hb_sum, wi_own, sm_own, sm_parts, top, low_sum, att_f, gq_f, delta, columns,
    vec_t, wq_all, wq_line, send_sems, recv_sems, local_sems,
):
    x, yl, c, yh, z = me = tuple(lax.axis_index(a) for a in ("x", "yl", "c", "yh", "z"))
    dp = x * 4 + yl * 2 + c
    links = Links(send_sems, recv_sems)
    ring_z, ring_x = Ring(links, "z", z), Ring(links, "x", x)
    partner = {"c": 1 - c}

    def block(p):
        return c * 512 + p * 128

    def block_partner(p):
        return (1 - c) * 512 + p * 128

    own = rows(block(z), 128)
    loads = [pltpu.make_async_copy(tok_ref, xg.at[own], local_sems.at[0])]
    loads.append(pltpu.make_async_copy(cot_ref, cotg.at[own], local_sems.at[1]))
    for k in range(3):
        loads.append(pltpu.make_async_copy(wi_ref.at[k], wi_own.at[:, pl.ds(128 * k, 128)], local_sems.at[2 + k]))
    for load in loads:
        load.start()

    barrier = pltpu.get_barrier_semaphore()
    peers = [{"x": ring_x.right}, {"x": ring_x.left}, {"z": ring_z.right}, {"z": ring_z.left}]
    for dl in range(2):
        for dc in range(2):
            for dh in range(2):
                if dl or dc or dh:
                    peers.append({"yl": lax.rem(yl + dl, 2), "c": lax.rem(c + dc, 2), "yh": lax.rem(yh + dh, 2)})
    for peer in peers:
        pl.semaphore_signal(barrier, inc=1, device_id=peer, device_id_type=MESH)
    sm_parts[...] = jnp.zeros_like(sm_parts)
    sm_parts[0:2, 0:64] = gain_ref[...].astype(F32)
    sm_parts[2:6, 0:64] = off_ref[...].astype(F32)
    sm_parts[22:23, 0:32] = hid_ref[...].astype(F32)
    sm_parts[39:40, 0:8] = head_ref[0:1].astype(F32)
    sm_parts[40:41, 0:8] = head_ref[1:2].astype(F32)
    placed = pltpu.roll(sm_parts[0:16], c * 64, 1) + pltpu.roll(sm_parts[16:32], lax.rem(dp, 4) * 32, 1)
    sm_own[...] = (placed + pltpu.roll(sm_parts[32:48], dp * 8, 1)).astype(BF16)
    for load in loads:
        load.wait()
    pl.semaphore_wait(barrier, len(peers))

    w_sm = WeightGather(ring_x, me, sm, 16, sm_own)
    w_kv = WeightGather(ring_x, me, wi.at[:, pl.ds(128, 256)], 64, wi_own.at[:, pl.ds(128, 256)])
    w_q = WeightGatherAlongX(ring_x, me, wq_all, wq_line)
    w_o = WeightGather(ring_x, me, wo, 64, wo_ref)
    w_e = WeightGather(ring_x, me, we, 64, we_ref)
    w_c = WeightGather(ring_x, me, wc, 64, wc_ref)
    w_sm.start()
    w_kv.start()
    wq_line[x] = wi_own[:, 0:128]
    w_q.gather.start()
    gather_x = RingGather(ring_z, xg, block, 64, partner, block_partner)
    gather_x.start()
    w_o.start()
    w_sm.start_x()
    w_e.start()
    w_c.start()
    w_kv.start_x()
    w_q.gather.forward()
    w_o.start_x()
    gather_x.forward()
    w_q.start_y()
    w_sm.gather.forward()
    w_kv.gather.forward()
    gather_x.done()
    gather_c = RingGather(ring_z, cotg, block, 64, partner, block_partner)
    gather_c.start()
    w_sm.gather.done()

    tiles = [sm[pl.ds(16 * k, 16)].astype(F32) for k in range(16)]
    pairs = [tiles[2 * k] + tiles[2 * k + 1] for k in range(8)]
    vectors = jnp.concatenate(pairs, axis=1)
    gains, offs = vectors[0:2], vectors[2:6]
    fours = [pairs[2 * k] + pairs[2 * k + 1] for k in range(4)]
    hidden_bias = jnp.concatenate([f[6:7] for f in fours], axis=1)
    every = fours[0] + fours[1] + fours[2] + fours[3]
    qkv_bias = jnp.concatenate([every[7:8], jnp.zeros((1, 128), F32), every[8:9]], axis=1)
    gain1, gain2 = gains[0:1], gains[1:2]
    off0, off1, off2, off3 = (offs[k : k + 1] for k in range(4))

    @pl.loop(0, 4)
    def _(i):
        r = rows(i * 256, 256)
        normed, _ = norm_rows(xg[r].astype(F32))
        h1[r] = (normed * gain1 + off0).astype(BF16)

    links.settle()
    w_kv.gather.done()
    w_o.gather.forward()

    kv_slots = links.slots(2)
    kv_copies = []
    for s in range(2):
        part = pl.ds(s * 512, 512)
        kv_copies.append(links.make(qkv.at[part, pl.ds(128, 256)], kvr.at[part], kv_slots + s, {"yh": 1}))
        links.keep(kv_copies[s], yh == 0)

    @pl.loop(0, 4)
    def _(i):
        r = rows(i * 256, 256)
        qkv[r, 128:384] = (nn(h1[r], wi[:, 128:384]) + qkv_bias[:, 128:384]).astype(BF16)
        for s in range(2):
            pl.when((i == 2 * s + 1) & (yh == 0))(kv_copies[s].start)

    w_q.done()
    wi[:, 0:128] = wq_all[...].reshape(1024, 128)

    @pl.loop(0, 4)
    def _(i):
        r = rows(i * 256, 256)
        qkv[r, 0:128] = (nn(h1[r], wi[:, 0:128]) + qkv_bias[:, 0:128]).astype(BF16)

    w_o.gather.done()
    w_e.start_x()
    w_c.start_x()
    rank = c * 4 + z
    wo_all[:, rows(rank * 128, 128)] = wo[...]
    gather_o = ColumnGather(ring_z, c, wo_all, partner)
    gather_c.forward()
    gather_o.start()

    lane = lax.broadcasted_iota(jnp.int32, (1, 128), 1)
    head_lanes = [lane < 64, lane >= 64]

    def causal(scores, first):
        r = lax.broadcasted_iota(jnp.int32, scores.shape, 0) + first
        return jnp.where(r >= lax.broadcasted_iota(jnp.int32, scores.shape, 1), scores, MASKED)

    def masked(value, h):
        return jnp.where(head_lanes[h], value, jnp.zeros_like(value))

    def attend():
        @pl.loop(0, 2)
        def _(s):
            for qb in range(2):
                nk = 256 * (qb + 1)
                r = rows(s * 512 + qb * 256, 256)
                keys = rows(s * 512, nk, 512)
                q, k, v = qkv[r, 0:128], qkv[keys, 128:256], qkv[keys, 256:384]
                outs = []
                for h in range(2):
                    near = causal(nt(masked(q, h), k) * SCALE, qb * 256)
                    peak = jnp.max(near, axis=-1, keepdims=True)
                    near = jnp.exp(near - peak)
                    top[h, r] = peak
                    low_sum[h, r] = jnp.sum(near, axis=-1, keepdims=True)
                    outs.append(nn(near.astype(BF16), v))
                att_f[r] = jnp.where(head_lanes[0], outs[0], outs[1])

    def finish(remote):
        @pl.loop(0, 4)
        def _(i):
            r = rows(i * 256, 256)
            keys = rows((i // 2) * 512, 512)
            outs = []
            for h in range(2):
                peak, total, o = top[h, r], low_sum[h, r], att_f[r]
                if remote:
                    far = nt(masked(qkv[r, 0:128], h), kvr[keys, 0:128]) * SCALE
                    higher = jnp.maximum(peak, jnp.max(far, axis=-1, keepdims=True))
                    far = jnp.exp(far - higher)
                    shrink = jnp.exp(peak - higher)
                    total = total * shrink + jnp.sum(far, axis=-1, keepdims=True)
                    o = o * shrink + nn(far.astype(BF16), kvr[keys, 128:256])
                    peak = higher
                outs.append(o * (1.0 / total))
                lse[h, r] = peak + jnp.log(total)
            o = jnp.where(head_lanes[0], outs[0], outs[1])
            att_f[r] = o
            att[r] = o.astype(BF16)

    attend()
    gather_o.forward()
    links.settle()
    pl.when(yh == 0)(functools.partial(finish, False))

    @pl.when(yh == 1)
    def _():
        for s in range(2):
            links.wait(kv_slots + s, kvr.at[pl.ds(s * 512, 512)], {"yh": 0})
        finish(True)

    swap_a = Swap(ring_z, c, 128)
    swap_a.start(att, att_in)
    x_own = xg[own].astype(F32)
    cot_own = cotg[own].astype(F32)
    w_e.gather.forward()
    w_c.gather.forward()
    links.settle()
    gather_c.done()
    gather_o.done()
    swap_a.done(att_in)
    joined = jnp.concatenate([att_in[128 * k : 128 * k + 128] for k in range(8)], axis=1)
    resid[...] = x_own + nt(joined, wo_all[...]) + off1
    normed2, inverse2 = norm_rows(resid[...])
    h2[own] = (normed2 * gain2 + off2).astype(BF16)
    gather_h = RingGather(ring_z, h2, block, 64, partner, block_partner)
    gather_h.start()
    links.settle()
    w_e.gather.done()
    w_c.gather.done()
    vec_t[...] = jnp.transpose(vectors)
    gather_h.forward()

    hb_sum[...] = jnp.zeros_like(hb_sum)

    def mlp_tile(pos):
        near_rows, next_rows = rows(pos * 128, 128), rows(512 + pos * 128, 128)

        def load(ref):
            return jnp.concatenate([ref[near_rows], ref[next_rows]], axis=0)

        def store(ref, value):
            ref[near_rows] = value[0:128]
            ref[next_rows] = value[128:256]

        p = nn(load(h2), we[...]) + hidden_bias
        square = p * p
        t = jnp.tanh(GELU_COEF * (p + CUBIC * p * square))
        store(hid, (0.5 * p * (1.0 + t)).astype(BF16))
        slope = 0.5 * (1.0 + t) + 0.5 * p * (1.0 - t * t) * (GELU_COEF * (1.0 + 3.0 * CUBIC * square))
        g = (nn(load(cotg), wc[...]) * slope).astype(BF16)
        store(gp, g)
        hb_sum[...] += jnp.sum(g.astype(F32), axis=0, keepdims=True)
        store(part_2, nt(g, we[...]).astype(BF16))

    sum_2 = GroupSum(ring_z, c, part_2, core_2, near_2)
    sum_2.run_by_chip(mlp_tile, gather_h)

    def weight_grad(out, left, right):
        @pl.loop(0, 4)
        def _(i):
            r = rows(i * 256, 256)
            out[r] = tn(left[:, r], right[...]).astype(BF16)

    g_e = WeightSum(ring_x, me, ge, 64, land_e, landy_e)
    g_c = WeightSum(ring_x, me, gc, 64, land_c, landy_c)
    weight_grad(ge, h2, gp)
    g_e.start()
    links.settle()
    sum_2.middle()
    weight_grad(gc, cotg, hid)
    g_c.start()

    links.settle()
    grad2 = sum_2.total()
    gres[...] = cot_own + norm_back(grad2, normed2, inverse2, gain2)
    grad_branch = gres[...].astype(BF16)
    gbg[own] = grad_branch
    for k in range(4):
        g = nn(grad_branch, wo_all[:, 256 * k : 256 * k + 256]).astype(BF16)
        gatt_out[256 * k : 256 * k + 128] = g[:, 0:128]
        gatt_out[256 * k + 128 : 256 * k + 256] = g[:, 128:256]
    swap_g = Swap(ring_z, c, 128)
    swap_g.start(gatt_out, gatt)
    gather_b = RingGather(ring_z, gbg, block, 64, partner, block_partner)
    gather_b.start()
    vec[1:2] = jnp.sum(grad2 * normed2, axis=0, keepdims=True)
    vec[3:4] = jnp.sum(grad_branch.astype(F32), axis=0, keepdims=True)
    vec[4:5] = jnp.sum(grad2, axis=0, keepdims=True)
    vec[5:6] = jnp.sum(cot_own, axis=0, keepdims=True)

    def out_tile(r):
        part_o[r] = nt(hid[r], wc[...]).astype(BF16)

    sum_o = GroupSum(ring_z, c, part_o, core_o, near_o)
    sum_o.run(out_tile)
    g_e.middle()
    links.settle()
    swap_g.done(gatt)

    @pl.loop(0, 4)
    def _(i):
        r = rows(i * 256, 256)
        product = gatt[r].astype(F32) * att_f[r]
        for h in range(2):
            delta[h, r] = jnp.sum(masked(product, h), axis=-1, keepdims=True)

    gkv_slots = links.slots(2)
    gkv_copies = []
    for s in range(2):
        part = pl.ds(s * 512, 512)
        gkv_copies.append(links.make(gkv_out.at[part], gkv_in.at[part], gkv_slots + s, {"yh": 0}))
        links.keep(gkv_copies[s], yh == 1)

    def attend_far():
        @pl.loop(0, 2)
        def _(s):
            seq = rows(s * 512, 512)
            k, v = kvr[seq, 0:128], kvr[seq, 128:256]
            dk0_acc[...] = jnp.zeros_like(dk0_acc)
            dv0_acc[...] = jnp.zeros_like(dv0_acc)

            @pl.loop(0, 2)
            def _(qb):
                r = rows(s * 512 + qb * 256, 256)
                q, g = qkv[r, 0:128], gatt[r]
                outs = []
                for h in range(2):
                    qm, gm = masked(q, h), masked(g, h)
                    far = jnp.exp(nt(qm, k) * SCALE - lse[h, r])
                    far_s = (far * (nt(gm, v) - delta[h, r])).astype(BF16)
                    dk0_acc[...] += tn(far_s, qm)
                    dv0_acc[...] += tn(far.astype(BF16), gm)
                    outs.append(nn(far_s, k))
                gq_f[r] = jnp.where(head_lanes[0], outs[0], outs[1])

            gkv_out[seq, 0:128] = (dk0_acc[...] * SCALE).astype(BF16)
            gkv_out[seq, 128:256] = dv0_acc[...].astype(BF16)
            for k in range(2):
                pl.when(s == k)(gkv_copies[k].start)

    def attend_back():
        @pl.loop(0, 2)
        def _(s):
            dk_acc[...] = jnp.zeros_like(dk_acc)
            dv_acc[...] = jnp.zeros_like(dv_acc)
            seq = rows(s * 512, 512)
            for qb in range(2):
                nk = 256 * (qb + 1)
                r = rows(s * 512 + qb * 256, 256)
                keys = rows(s * 512, nk, 512)
                q, k, v, g = qkv[r, 0:128], qkv[keys, 128:256], qkv[keys, 256:384], gatt[r]
                outs = []
                for h in range(2):
                    qm, gm = masked(q, h), masked(g, h)
                    near = jnp.exp(causal(nt(qm, k) * SCALE, qb * 256) - lse[h, r])
                    near_s = (near * (nt(gm, v) - delta[h, r])).astype(BF16)
                    dk_acc[0:nk] += tn(near_s, qm)
                    dv_acc[0:nk] += tn(near.astype(BF16), gm)
                    outs.append(nn(near_s, k))
                total = gq_f[r] + jnp.where(head_lanes[0], outs[0], outs[1])
                gqkv[r, 0:128] = (total * SCALE).astype(BF16)
            gqkv[seq, 128:256] = (dk_acc[...] * SCALE).astype(BF16)
            gqkv[seq, 256:384] = dv_acc[...].astype(BF16)

    @pl.when(yh == 0)
    def _():
        gq_f[...] = jnp.zeros_like(gq_f)

    pl.when(yh == 1)(attend_far)
    gather_b.forward()
    g_c.middle()
    g_e.start_y()
    sum_o.start()
    gather_b.done()
    attend_back()
    sum_o.middle()
    weight_grad(go, gbg, att)
    g_o = WeightSum(ring_x, me, go, 64, land_o, landy_o)
    g_o.start()

    links.settle()
    @pl.when(yh == 0)
    def _():
        for s in range(2):
            links.wait(gkv_slots + s, gkv_in.at[pl.ds(s * 512, 512)], {"yh": 1})

            @pl.loop(0, 2)
            def _(k):
                r = rows(s * 512 + k * 256, 256)
                gqkv[r, 128:384] = (gqkv[r, 128:384].astype(F32) + gkv_in[r].astype(F32)).astype(BF16)

    head_sums = jnp.sum(gqkv[...].astype(F32), axis=0, keepdims=True)

    @pl.loop(0, 4)
    def _(i):
        r = rows(i * 256, 256)
        g = tn(h1[:, r], gqkv[...])
        gi[r] = g.astype(BF16)
        weight = wi[r].astype(F32)
        off_grad = jnp.sum(weight * head_sums, axis=-1, keepdims=True)
        mixed = jnp.sum(weight * g, axis=-1, keepdims=True)
        gain_grad = (mixed - vec_t[r, 2:3] * off_grad) / vec_t[r, 0:1]
        columns[r] = jnp.where(lane == 0, gain_grad, jnp.where(lane == 2, off_grad, 0.0))

    g_i = WeightSum(ring_x, me, gi, 64, land_i, landy_i)
    g_i.start()
    def grad1_tile(r):
        part_1[r] = nt(gqkv[r], wi[...]).astype(BF16)

    sum_1 = GroupSum(ring_z, c, part_1, core_1, near_1)
    sum_1.run(grad1_tile)
    sum_1.start()
    g_c.start_y()
    turned = jnp.transpose(columns[...])
    vec[0:1] = turned[0:1]
    vec[2:3] = turned[2:3]
    hb = hb_sum[...]
    vec[6:7] = jnp.concatenate([hb[:, 128 * (k // 2) : 128 * (k // 2) + 128] for k in range(8)], axis=1)
    vec[7:8] = jnp.concatenate([head_sums[:, 0:128]] * 8, axis=1)
    vec[8:9] = jnp.concatenate([head_sums[:, 256:384]] * 8, axis=1)
    vec[9:16] = jnp.zeros((7, 1024), F32)
    for k in range(16):
        gs[pl.ds(16 * k, 16)] = vec[:, 128 * (k // 2) : 128 * (k // 2) + 128].astype(BF16)
    g_s = SmallSum(ring_x, me, gs, 16, land_s, landy_s)
    g_s.start()
    links.settle()
    g_i.middle()
    g_o.middle()
    sum_1.middle()
    g_s.start_y()
    g_i.start_y()
    g_o.start_y()
    normed1, inverse1 = norm_rows(x_own)
    gtok_ref[...] = gres[...] + norm_back(sum_1.total(), normed1, inverse1, gain1)
    links.settle()
    tile = g_s.finish()
    slot = yh * 4 + z
    tens[rows(slot * 16, 16)] = tile
    mine = tens.at[rows(slot * 16, 16)]
    t_ids = links.slots(8)
    others = [(dh, dz) for dh in range(2) for dz in range(4) if dh or dz]
    for dh, dz in others:
        links.send(mine, mine, t_ids + slot, {"yh": lax.rem(yh + dh, 2), "z": lax.rem(z + dz, 4)})
    out_ref[...] = (resid[...] + sum_o.total() + off3).astype(BF16)
    gwe_ref[...] = g_e.finish()
    gwc_ref[...] = g_c.finish()
    gwo_ref[...] = g_o.finish()
    for dh, dz in others:
        theirs = lax.rem(yh + dh, 2) * 4 + lax.rem(z + dz, 4)
        ref = tens.at[rows(theirs * 16, 16)]
        links.wait(t_ids + theirs, ref, {"yh": lax.rem(yh + dh, 2), "z": lax.rem(z + dz, 4)})
    total = tens[0:16]
    for k in range(1, 8):
        total = total + tens[16 * k : 16 * k + 16]
    gsm_ref[0:6] = total[0:6]
    gsm_ref[6:16] = tile[6:16]
    gwi_ref[...] = g_i.finish()
    links.drain(len(links.open))


def final_kernel(
    out_k, gtok_k, gwi, gwo, gwe, gwc, gsm,
    out_ref, gtok_ref, gi_ref, go_ref, ge_ref, gc_ref, head_ref, hid_ref, gain_ref, off_ref,
):
    c = lax.axis_index("c")
    dp = lax.axis_index("x") * 4 + lax.axis_index("yl") * 2 + c
    out_ref[...] = out_k[...]
    gtok_ref[...] = gtok_k[...]
    for k in range(3):
        gi_ref[k] = gwi[:, 128 * k : 128 * k + 128]
    go_ref[...] = gwo[...]
    ge_ref[...] = gwe[...]
    gc_ref[...] = gwc[...]
    small = gsm[...]
    mine = pltpu.roll(small, lax.rem(128 - c * 64, 128), 1)
    gain_ref[...] = mine[0:2, 0:64]
    off_ref[...] = mine[2:6, 0:64]
    hid_ref[...] = pltpu.roll(small, lax.rem(128 - lax.rem(dp, 4) * 32, 128), 1)[6:7, 0:32]
    heads = pltpu.roll(small, lax.rem(128 - dp * 8, 128), 1)
    head_ref[0] = heads[7:8, 0:8]
    head_ref[1] = heads[8:9, 0:8]


def per_device(tokens, input_proj, output_proj, expand_proj, contract_proj, head_bias, hidden_bias, norm_gains, offsets, cotangent):
    vmem = pl.BlockSpec(memory_space=pltpu.VMEM)
    shape = jax.ShapeDtypeStruct
    widths = (384, 128, 512, 512)

    def buf(r, n, t=BF16):
        return pltpu.VMEM((r, n), t)

    scratch = [buf(1024, 1024) for _ in range(5)]
    scratch += [buf(1024, n) for n in widths] + [buf(256, 128)]
    scratch += [buf(1024, n) for n in widths] + [buf(256, 128)]
    scratch += [buf(768, n) for n in widths] + [buf(256, 128)]
    scratch += [buf(256, n) for n in widths] + [buf(64, 128)]
    scratch += [buf(1024, 1024) for _ in range(3)] + [buf(512, 1024) for _ in range(3)]
    scratch += [buf(384, 1024) for _ in range(3)]
    scratch += [buf(1024, 1024), buf(1024, 128), buf(1024, 128)]
    scratch += [buf(1024, 384), buf(1024, 384), buf(1024, 256), buf(1024, 256), buf(1024, 256)]
    scratch += [buf(1024, 128), buf(1024, 128), buf(1024, 512), buf(1024, 512)]
    scratch += [pltpu.VMEM((2, 1024, 1), F32)] + [buf(512, 128, F32) for _ in range(4)]
    scratch += [buf(128, 1024, F32), buf(128, 1024, F32), buf(16, 1024, F32), buf(128, 128, F32)]
    scratch += [buf(1, 512, F32), buf(64, 384), buf(16, 128), buf(48, 128, F32)]
    scratch += [pltpu.VMEM((2, 1024, 1), F32), pltpu.VMEM((2, 1024, 1), F32)]
    scratch += [buf(1024, 128, F32), buf(1024, 128, F32), pltpu.VMEM((2, 1024, 1), F32)]
    scratch += [buf(1024, 128, F32), buf(1024, 16, F32)]
    scratch += [pltpu.VMEM((4, 4, 64, 128), BF16), pltpu.VMEM((4, 64, 128), BF16)]
    scratch += [pltpu.SemaphoreType.DMA((SENDS,)), pltpu.SemaphoreType.DMA((RECEIVES,))]
    scratch += [pltpu.SemaphoreType.DMA((5,))]
    out, gtok, gwi, gwo, gwe, gwc, gsm = pl.pallas_call(
        layer_kernel,
        out_shape=(
            shape((128, 1024), BF16),
            shape((128, 1024), F32),
            *(shape((64, n), F32) for n in widths),
            shape((16, 128), F32),
        ),
        in_specs=[pl.BlockSpec(memory_space=pl.ANY)] * 6 + [vmem] * 4,
        out_specs=[vmem] * 7,
        scratch_shapes=scratch,
        compiler_params=pltpu.CompilerParams(
            collective_id=0, has_side_effects=True, vmem_limit_bytes=58 * 1024 * 1024
        ),
    )(
        tokens, cotangent, input_proj, output_proj.T, expand_proj, contract_proj.T,
        norm_gains, offsets, hidden_bias, head_bias.reshape(2, 8),
    )
    outs = pl.pallas_call(
        final_kernel,
        out_shape=(
            shape((128, 1024), BF16),
            shape((128, 1024), F32),
            shape((3, 64, 128), F32),
            shape((64, 128), F32),
            shape((64, 512), F32),
            shape((64, 512), F32),
            shape((2, 1, 8), F32),
            shape((1, 32), F32),
            shape((2, 64), F32),
            shape((4, 64), F32),
        ),
        in_specs=[vmem] * 7,
        out_specs=[vmem] * 10,
    )(out, gtok, gwi, gwo, gwe, gwc, gsm)
    return (*outs[:3], outs[3].T, outs[4], outs[5].T, *outs[6:])


def solution(mesh):
    split = Mesh(mesh.devices.reshape(4, 2, 2, 2, 4), ("x", "yl", "c", "yh", "z"))
    token_rows = P(DP + TENSOR, None)
    weights = (
        P(None, DP, TENSOR),
        P(TENSOR, DP),
        P(DP, TENSOR),
        P(TENSOR, DP),
        P(None, TENSOR, DP),
        P(TENSOR, DP),
        P(None, DP),
        P(None, DP),
    )
    return jax.shard_map(
        per_device,
        mesh=split,
        in_specs=(token_rows, *weights, token_rows),
        out_specs=(token_rows, token_rows, *weights),
        check_vma=False,
    )
```

```python
import functools

import jax
import jax.numpy as jnp
from jax import lax
from jax.experimental import pallas as pl
from jax.experimental.pallas import tpu as pltpu
from jax.sharding import Mesh
from jax.sharding import PartitionSpec as P

F32, BF16 = jnp.float32, jnp.bfloat16
MESH = pl.DeviceIdType.MESH
DP = ("x", "yl", "c")
TENSOR = ("yh", "z")
EPSILON = 1e-05
MASKED = -1000000000.0
GELU_COEF = 0.7978845608028654
CUBIC = 0.044715
SCALE = 64 ** (-0.5)
SENDS = 104
RECEIVES = 236


def nn(a, b):
    return lax.dot_general(a, b, (((1,), (0,)), ((), ())), preferred_element_type=F32)


def nt(a, b):
    return lax.dot_general(a, b, (((1,), (1,)), ((), ())), preferred_element_type=F32)


def tn(a, b):
    return lax.dot_general(a, b, (((0,), (0,)), ((), ())), preferred_element_type=F32)


def rows(start, size, by=None):
    if isinstance(start, int):
        return pl.ds(start, size)
    return pl.ds(pl.multiple_of(start, by or size), size)


def norm_rows(v):
    shifted = v - jnp.mean(v, axis=-1, keepdims=True)
    inverse = lax.rsqrt(jnp.mean(shifted * shifted, axis=-1, keepdims=True) + EPSILON)
    return shifted * inverse, inverse


def norm_back(grad, normed, inverse, gain):
    scaled = grad * gain
    first = jnp.mean(scaled, axis=-1, keepdims=True)
    second = jnp.mean(scaled * normed, axis=-1, keepdims=True)
    return inverse * (scaled - first - normed * second)


class Links:
    def __init__(self, send_sems, recv_sems):
        self.send_sems, self.recv_sems = send_sems, recv_sems
        self.sent, self.received, self.open, self.free, self.mark = 0, 0, [], [], 0

    def outgoing(self, count):
        first = self.sent
        self.sent += count
        assert self.sent <= SENDS, self.sent
        return first

    def slots(self, count):
        first = self.received
        self.received += count
        assert self.received <= RECEIVES, self.received
        return first

    def make(self, src, dst, recv, to):
        self.last = self.free.pop(0) if self.free else self.outgoing(1)
        return pltpu.make_async_remote_copy(
            src_ref=src,
            dst_ref=dst,
            send_sem=self.send_sems.at[self.last],
            recv_sem=self.recv_sems.at[recv],
            device_id=to,
            device_id_type=MESH,
        )

    def keep(self, copy, cond=None):
        self.open.append((self.last, cond, copy))

    def send(self, src, dst, recv, to, like=None):
        copy = self.make(src, dst, recv, to)
        copy.start()
        if like is not None:
            copy = like
        self.keep(copy)

    def send_if(self, cond, src, dst, recv, to):
        copy = self.make(src, dst, recv, to)
        pl.when(cond)(copy.start)
        self.keep(copy, cond)

    def local_if(self, cond, src, dst, recv):
        copy = pltpu.make_async_copy(src, dst, self.recv_sems.at[recv])
        pl.when(cond)(copy.start)

    def wait(self, recv, ref, to):
        pltpu.make_async_remote_copy(
            src_ref=ref,
            dst_ref=ref,
            send_sem=self.send_sems.at[0],
            recv_sem=self.recv_sems.at[recv],
            device_id=to,
            device_id_type=MESH,
        ).wait_recv()

    def drain(self, count):
        for sem, cond, copy in self.open[:count]:
            if not hasattr(copy, "wait_send"):
                copy = pltpu.make_async_remote_copy(
                    src_ref=copy,
                    dst_ref=copy,
                    send_sem=self.send_sems.at[sem],
                    recv_sem=self.recv_sems.at[0],
                    device_id={"c": 0},
                    device_id_type=MESH,
                )
            if cond is None:
                copy.wait_send()
            else:
                pl.when(cond)(copy.wait_send)
            if sem is not None:
                self.free.append(sem)
        self.open = self.open[count:]

    def settle(self):
        self.drain(self.mark)
        self.mark = len(self.open)


class Ring:
    def __init__(self, links, axis, pos):
        self.links, self.axis = links, axis
        self.pos = pos
        self.right, self.left, self.far = (lax.rem(pos + k, 4) for k in (1, 3, 2))
        self.to_right, self.to_left = {axis: self.right}, {axis: self.left}


class RingGather:
    def __init__(self, ring, buf, offset, half, partner=None, offset_partner=None):
        self.ring, self.buf, self.offset, self.half = ring, buf, offset, half
        self.partner, self.offset_partner = partner, offset_partner
        self.ids = ring.links.slots(6)
        if partner is not None:
            self.pids = ring.links.slots(8)

    def at(self, pos, part, offset=None):
        return self.buf.at[rows((offset or self.offset)(pos) + part * self.half, self.half)]

    def like(self):
        return self.buf.at[pl.ds(0, self.half)]

    def relay(self, pos, part, slot):
        if self.partner is not None:
            ref = self.at(pos, part)
            self.ring.links.send(ref, ref, self.pids + slot, self.partner, self.like())

    def start(self):
        r, s = self.ring, self.ring.links.send
        a, b = self.at(r.pos, 0), self.at(r.pos, 1)
        s(a, a, self.ids + 0, r.to_right)
        s(b, b, self.ids + 3, r.to_left)
        s(b, b, self.ids + 1, r.to_right)
        s(a, a, self.ids + 2, r.to_left)
        self.relay(r.pos, 0, 0)
        self.relay(r.pos, 1, 1)

    def forward(self):
        r, s, w = self.ring, self.ring.links.send, self.ring.links.wait
        ref = self.at(r.left, 0)
        w(self.ids + 0, ref, r.to_left)
        s(ref, ref, self.ids + 4, r.to_right)
        ref = self.at(r.right, 1)
        w(self.ids + 3, ref, r.to_right)
        s(ref, ref, self.ids + 5, r.to_left)
        self.relay(r.left, 0, 2)
        self.relay(r.right, 1, 5)

    def done(self):
        self.near()
        self.far()
        self.own()

    def near(self):
        r, w = self.ring, self.ring.links.wait
        w(self.ids + 1, self.at(r.left, 1), r.to_left)
        self.relay(r.left, 1, 3)
        w(self.ids + 2, self.at(r.right, 0), r.to_right)
        self.relay(r.right, 0, 4)
        self.relayed(2, ((r.left, 0), (r.left, 1), (r.right, 0), (r.right, 1)))

    def far(self):
        r, w = self.ring, self.ring.links.wait
        w(self.ids + 4, self.at(r.far, 0), r.to_left)
        self.relay(r.far, 0, 6)
        w(self.ids + 5, self.at(r.far, 1), r.to_right)
        self.relay(r.far, 1, 7)
        self.relayed(6, ((r.far, 0), (r.far, 1)))

    def own(self):
        r = self.ring
        self.relayed(0, ((r.pos, 0), (r.pos, 1)))

    def relayed(self, first, blocks):
        if self.partner is not None:
            for k, (pos, part) in enumerate(blocks):
                self.ring.links.wait(self.pids + first + k, self.at(pos, part, self.offset_partner), self.partner)


class ColumnGather(RingGather):
    def __init__(self, ring, c, buf, partner):
        super().__init__(ring, buf, c, buf.shape[0] // 2, partner, 1 - c)

    def at(self, pos, part, core=None):
        rank = (self.offset if core is None else core) * 4 + pos
        return self.buf.at[pl.ds(part * self.half, self.half), rows(rank * 128, 128)]

    def like(self):
        return self.buf.at[pl.ds(0, self.half), pl.ds(0, 128)]


class FirstGather(RingGather):
    def at(self, pos, part, offset=None):
        return self.buf.at[pos, pl.ds(part * self.half, self.half)]

    def like(self):
        return self.buf.at[0, pl.ds(0, self.half)]


class WeightGatherAlongX:
    def __init__(self, ring, me, buf, line):
        self.ring, self.me, self.buf, self.line = ring, me, buf, line
        self.gather = FirstGather(ring, line, None, line.shape[1] // 2)
        self.ids = ring.links.slots(4)

    def start_y(self):
        x, yl, c, yh, z = self.me
        links = self.ring.links
        self.gather.done()
        slot = yl * 2 + c
        dst = self.buf.at[:, slot]
        for dl, dh in ((1, 0), (0, 1), (1, 1)):
            to = {"yl": lax.rem(yl + dl, 2), "yh": lax.rem(yh + dh, 2), "c": yh}
            links.send(self.line, dst, self.ids + slot, to)
        links.local_if(c == yh, self.line, dst, self.ids + slot)
        links.send_if(c != yh, self.line, dst, self.ids + slot, {"c": yh})

    def done(self):
        for k in range(4):
            self.ring.links.wait(self.ids + k, self.buf.at[:, k], {"c": 1 - self.me[2]})


class Swap:
    def __init__(self, ring, c, size):
        self.ring, self.c, self.size = ring, c, size
        self.rank = c * 4 + ring.pos
        self.ids = ring.links.slots(8)
        self.others = [(dc, dz) for dz in (2, 1, 3, 0) for dc in (0, 1) if dc or dz]

    def peer(self, dc, dz):
        return lax.rem(self.c + dc, 2), lax.rem(self.ring.pos + dz, 4)

    def tile(self, buf, rank):
        return buf.at[rows(rank * self.size, self.size)]

    def start(self, src, dst):
        for dc, dz in self.others:
            to_c, to_z = self.peer(dc, dz)
            to = {"c": to_c, "z": to_z}
            self.ring.links.send(self.tile(src, to_c * 4 + to_z), self.tile(dst, self.rank), self.ids + self.rank, to)
        self.tile(dst, self.rank)[...] = self.tile(src, self.rank)[...]

    def done(self, dst):
        for dc, dz in self.others:
            of_c, of_z = self.peer(dc, dz)
            theirs = of_c * 4 + of_z
            self.ring.links.wait(self.ids + theirs, self.tile(dst, theirs), {"c": of_c, "z": of_z})


class RingSum:
    def __init__(self, ring, buf, offset, half, land):
        self.ring, self.buf, self.offset, self.half, self.land = ring, buf, offset, half, land
        self.ids = ring.links.slots(6)

    def at(self, pos, part, count=1):
        return self.buf.at[rows(self.offset(pos) + part * self.half, self.half * count, self.half)]

    def landing(self, slot):
        return self.land.at[pl.ds(slot * self.half, self.half)]

    def send(self, src, slot, to):
        like = self.buf.at[pl.ds(0, self.half)]
        self.ring.links.send(src, self.landing(slot), self.ids + slot, to, like)

    def wait(self, slot, to):
        self.ring.links.wait(self.ids + slot, self.landing(slot), to)

    def add(self, pos, part, slot):
        ref = self.at(pos, part)
        ref[...] = (ref[...].astype(F32) + self.landing(slot)[...].astype(F32)).astype(BF16)

    def send_far(self):
        r = self.ring
        self.send(self.at(r.far, 0), 0, r.to_right)
        self.send(self.at(r.far, 1), 1, r.to_left)

    def send_near(self):
        r = self.ring
        self.send(self.at(r.right, 1), 3, r.to_right)
        self.send(self.at(r.left, 0), 4, r.to_left)

    def middle(self):
        r = self.ring
        self.wait(0, r.to_left)
        self.add(r.right, 0, 0)
        self.send(self.at(r.right, 0), 2, r.to_right)
        self.wait(1, r.to_right)
        self.add(r.left, 1, 1)
        self.send(self.at(r.left, 1), 5, r.to_left)

    def total(self):
        r = self.ring
        self.wait(3, r.to_left)
        self.wait(4, r.to_right)
        self.wait(2, r.to_left)
        self.wait(5, r.to_right)
        own = self.at(r.pos, 0, 2)[...].astype(F32)
        left = self.land[pl.ds(2 * self.half, 2 * self.half)].astype(F32)
        right = self.land[pl.ds(4 * self.half, 2 * self.half)].astype(F32)
        return own + left + right


class GroupSum:
    def __init__(self, ring, c, buf, from_core, land):
        self.links, self.c, self.buf, self.from_core = ring.links, c, buf, from_core
        self.partner = {"c": 1 - c}
        self.order = (ring.far, ring.right, ring.left, ring.pos)
        self.ids, self.out_ids = ring.links.slots(4), ring.links.outgoing(4)
        self.sum = RingSum(ring, buf, lambda p: c * 512 + p * 128, 64, land)

    def core_copy(self, pos):
        return pltpu.make_async_remote_copy(
            src_ref=self.buf.at[rows((1 - self.c) * 512 + pos * 128, 128)],
            dst_ref=self.from_core.at[rows(pos * 128, 128)],
            send_sem=self.links.send_sems.at[self.out_ids + pos],
            recv_sem=self.links.recv_sems.at[self.ids + pos],
            device_id=self.partner,
            device_id_type=MESH,
        )

    def run(self, body):
        first = self.order[0] // 2

        @pl.loop(0, 4)
        def _(i):
            tile = lax.rem(first + i, 2)
            body(rows(lax.rem(1 - self.c + i // 2, 2) * 512 + tile * 256, 256))

            @pl.when(i < 2)
            def _():
                self.core_copy(tile * 2).start()
                self.core_copy(tile * 2 + 1).start()

        for pos in range(4):
            self.links.open.append((None, None, self.core_copy(pos)))

    def run_by_chip(self, body, gather):
        z = self.order[3]

        @pl.loop(0, 4)
        def _(i):
            pl.when(i == 0)(gather.own)
            pl.when(i == 1)(gather.near)

            @pl.when(i == 3)
            def _():
                gather.far()
                self.core_add(1)
                self.core_add(2)
                self.sum.send_near()

            pos = lax.rem(z + jnp.where(i == 2, 3, jnp.where(i == 3, 2, i)), 4)
            body(pos)
            self.core_copy(pos).start()

        for pos in range(4):
            self.links.open.append((None, None, self.core_copy(pos)))
        self.core_add(0)
        self.sum.send_far()

    def core_add(self, k):
        got = self.from_core.at[rows(self.order[k] * 128, 128)]
        self.links.wait(self.ids + self.order[k], got, self.partner)
        ref = self.buf.at[rows(self.c * 512 + self.order[k] * 128, 128)]
        ref[...] = (ref[...].astype(F32) + got[...].astype(F32)).astype(BF16)

    def start(self):
        self.core_add(0)
        self.sum.send_far()
        self.core_add(1)
        self.core_add(2)
        self.sum.send_near()

    def middle(self):
        self.sum.middle()
        self.core_add(3)

    def total(self):
        return self.sum.total()


class WeightGather:
    def __init__(self, ring, me, buf, size, shard):
        self.ring, self.me, self.buf, self.size, self.shard = ring, me, buf, size, shard
        self.ids = ring.links.slots(4)
        self.gather = RingGather(ring, buf, lambda p: p * 4 * size, 2 * size)

    def start(self):
        x, yl, c, yh, z = self.me
        links = self.ring.links
        own = self.buf.at[rows((x * 4 + yl * 2 + c) * self.size, self.size)]
        slot = self.ids + yl * 2 + c
        for dl, dh in ((1, 0), (0, 1), (1, 1)):
            to = {"yl": lax.rem(yl + dl, 2), "yh": lax.rem(yh + dh, 2), "c": yh}
            links.send(self.shard, own, slot, to)
        links.local_if(c == yh, self.shard, own, slot)
        links.send_if(c != yh, self.shard, own, slot, {"c": yh})

    def start_x(self):
        x, yl, c, yh, z = self.me
        for k in range(4):
            ref = self.buf.at[rows((x * 4 + k) * self.size, self.size)]
            self.ring.links.wait(self.ids + k, ref, {"c": 1 - c})
        self.gather.start()


class WeightSum:
    def __init__(self, ring, me, buf, size, land, land_y):
        self.ring, self.me, self.buf, self.size = ring, me, buf, size
        self.land_y = land_y
        self.sum = RingSum(ring, buf, lambda p: p * 4 * size, 2 * size, land)
        self.ids = ring.links.slots(4)

    def start(self):
        self.sum.send_far()
        self.sum.send_near()

    def middle(self):
        self.sum.middle()

    def x_total(self):
        return self.sum.total()

    def start_y(self):
        x, yl, c, yh, z = self.me
        links, size = self.ring.links, self.size
        total = self.x_total()
        self.buf[rows(x * 4 * size, 4 * size)] = total.astype(BF16)
        slot = yh * 2 + yl
        dst = self.land_y.at[rows(slot * size, size)]
        for dl, dc in ((1, 0), (0, 1), (1, 1), (0, 0)):
            to_l, to_c = lax.rem(yl + dl, 2), lax.rem(c + dc, 2)
            src = self.buf.at[rows((x * 4 + to_l * 2 + to_c) * size, size)]
            if dl or dc:
                links.send(src, dst, self.ids + slot, {"yl": to_l, "c": to_c, "yh": c})
            else:
                links.local_if(c == yh, src, dst, self.ids + slot)
                links.send_if(c != yh, src, dst, self.ids + slot, {"yh": c})

    def finish(self):
        c = self.me[2]
        total = 0.0
        for k in range(4):
            ref = self.land_y.at[pl.ds(k * self.size, self.size)]
            self.ring.links.wait(self.ids + k, ref, {"c": 1 - c})
            total = total + ref[...].astype(F32)
        return total


class SmallSum(WeightSum):
    def __init__(self, ring, me, buf, size, land, land_y):
        self.ring, self.me, self.buf, self.size = ring, me, buf, size
        self.land, self.land_y = land, land_y
        self.x_ids = ring.links.slots(4)
        self.ids = ring.links.slots(4)

    def start(self):
        x = self.me[0]
        for d in (2, 1, 3):
            to = lax.rem(x + d, 4)
            src = self.buf.at[rows(to * 4 * self.size, 4 * self.size)]
            dst = self.land.at[pl.ds(d * 4 * self.size, 4 * self.size)]
            self.ring.links.send(src, dst, self.x_ids + d, {"x": to})

    def x_total(self):
        x = self.me[0]
        total = self.buf[rows(x * 4 * self.size, 4 * self.size)].astype(F32)
        for d in (1, 3, 2):
            ref = self.land.at[pl.ds(d * 4 * self.size, 4 * self.size)]
            self.ring.links.wait(self.x_ids + d, ref, {"x": lax.rem(x + 4 - d, 4)})
            total = total + ref[...].astype(F32)
        return total


def layer_kernel(
    tok_ref, cot_ref, wi_ref, wo_ref, we_ref, wc_ref, gain_ref, off_ref, hid_ref, head_ref,
    out_ref, gtok_ref, gwi_ref, gwo_ref, gwe_ref, gwc_ref, gsm_ref,
    xg, cotg, h1, h2, gbg, wi, wo, we, wc, sm, gi, go, ge, gc, gs,
    land_i, land_o, land_e, land_c, land_s, landy_i, landy_o, landy_e, landy_c, landy_s,
    part_o, part_2, part_1, core_o, core_2, core_1, near_o, near_2, near_1, wo_all, att_in, gatt_out,
    qkv, gqkv, kvr, gkv_out, gkv_in, att, gatt, hid, gp, lse, dk_acc, dv_acc, dk0_acc, dv0_acc,
    resid, gres, vec, tens, hb_sum, wi_own, sm_own, sm_parts, top, low_sum, att_f, gq_f, delta, columns,
    vec_t, wq_all, wq_line, send_sems, recv_sems, local_sems,
):
    x, yl, c, yh, z = me = tuple(lax.axis_index(a) for a in ("x", "yl", "c", "yh", "z"))
    dp = x * 4 + yl * 2 + c
    links = Links(send_sems, recv_sems)
    ring_z, ring_x = Ring(links, "z", z), Ring(links, "x", x)
    partner = {"c": 1 - c}

    def block(p):
        return c * 512 + p * 128

    def block_partner(p):
        return (1 - c) * 512 + p * 128

    own = rows(block(z), 128)
    loads = [pltpu.make_async_copy(tok_ref, xg.at[own], local_sems.at[0])]
    loads.append(pltpu.make_async_copy(cot_ref, cotg.at[own], local_sems.at[1]))
    for k in range(3):
        loads.append(pltpu.make_async_copy(wi_ref.at[k], wi_own.at[:, pl.ds(128 * k, 128)], local_sems.at[2 + k]))
    for load in loads:
        load.start()

    barrier = pltpu.get_barrier_semaphore()
    peers = [{"x": ring_x.right}, {"x": ring_x.left}, {"z": ring_z.right}, {"z": ring_z.left}]
    for dl in range(2):
        for dc in range(2):
            for dh in range(2):
                if dl or dc or dh:
                    peers.append({"yl": lax.rem(yl + dl, 2), "c": lax.rem(c + dc, 2), "yh": lax.rem(yh + dh, 2)})
    for peer in peers:
        pl.semaphore_signal(barrier, inc=1, device_id=peer, device_id_type=MESH)
    sm_parts[...] = jnp.zeros_like(sm_parts)
    sm_parts[0:2, 0:64] = gain_ref[...].astype(F32)
    sm_parts[2:6, 0:64] = off_ref[...].astype(F32)
    sm_parts[22:23, 0:32] = hid_ref[...].astype(F32)
    sm_parts[39:40, 0:8] = head_ref[0:1].astype(F32)
    sm_parts[40:41, 0:8] = head_ref[1:2].astype(F32)
    placed = pltpu.roll(sm_parts[0:16], c * 64, 1) + pltpu.roll(sm_parts[16:32], lax.rem(dp, 4) * 32, 1)
    sm_own[...] = (placed + pltpu.roll(sm_parts[32:48], dp * 8, 1)).astype(BF16)
    for load in loads:
        load.wait()
    pl.semaphore_wait(barrier, len(peers))

    w_sm = WeightGather(ring_x, me, sm, 16, sm_own)
    w_kv = WeightGather(ring_x, me, wi.at[:, pl.ds(128, 256)], 64, wi_own.at[:, pl.ds(128, 256)])
    w_q = WeightGatherAlongX(ring_x, me, wq_all, wq_line)
    w_o = WeightGather(ring_x, me, wo, 64, wo_ref)
    w_e = WeightGather(ring_x, me, we, 64, we_ref)
    w_c = WeightGather(ring_x, me, wc, 64, wc_ref)
    w_sm.start()
    w_kv.start()
    wq_line[x] = wi_own[:, 0:128]
    w_q.gather.start()
    gather_x = RingGather(ring_z, xg, block, 64, partner, block_partner)
    gather_x.start()
    w_o.start()
    w_sm.start_x()
    w_e.start()
    w_c.start()
    w_kv.start_x()
    w_q.gather.forward()
    w_o.start_x()
    gather_x.forward()
    w_q.start_y()
    w_sm.gather.forward()
    w_kv.gather.forward()
    gather_x.done()
    gather_c = RingGather(ring_z, cotg, block, 64, partner, block_partner)
    gather_c.start()
    w_sm.gather.done()

    tiles = [sm[pl.ds(16 * k, 16)].astype(F32) for k in range(16)]
    pairs = [tiles[2 * k] + tiles[2 * k + 1] for k in range(8)]
    vectors = jnp.concatenate(pairs, axis=1)
    gains, offs = vectors[0:2], vectors[2:6]
    fours = [pairs[2 * k] + pairs[2 * k + 1] for k in range(4)]
    hidden_bias = jnp.concatenate([f[6:7] for f in fours], axis=1)
    every = fours[0] + fours[1] + fours[2] + fours[3]
    qkv_bias = jnp.concatenate([every[7:8], jnp.zeros((1, 128), F32), every[8:9]], axis=1)
    gain1, gain2 = gains[0:1], gains[1:2]
    off0, off1, off2, off3 = (offs[k : k + 1] for k in range(4))

    @pl.loop(0, 4)
    def _(i):
        r = rows(i * 256, 256)
        normed, _ = norm_rows(xg[r].astype(F32))
        h1[r] = (normed * gain1 + off0).astype(BF16)

    links.settle()
    w_kv.gather.done()
    w_o.gather.forward()

    kv_slots = links.slots(2)
    kv_copies = []
    for s in range(2):
        part = pl.ds(s * 512, 512)
        kv_copies.append(links.make(qkv.at[part, pl.ds(128, 256)], kvr.at[part], kv_slots + s, {"yh": 1}))
        links.keep(kv_copies[s], yh == 0)

    @pl.loop(0, 4)
    def _(i):
        r = rows(i * 256, 256)
        qkv[r, 128:384] = (nn(h1[r], wi[:, 128:384]) + qkv_bias[:, 128:384]).astype(BF16)
        for s in range(2):
            pl.when((i == 2 * s + 1) & (yh == 0))(kv_copies[s].start)

    w_q.done()
    wi[:, 0:128] = wq_all[...].reshape(1024, 128)

    @pl.loop(0, 4)
    def _(i):
        r = rows(i * 256, 256)
        qkv[r, 0:128] = (nn(h1[r], wi[:, 0:128]) + qkv_bias[:, 0:128]).astype(BF16)

    w_o.gather.done()
    w_e.start_x()
    w_c.start_x()
    rank = c * 4 + z
    wo_all[:, rows(rank * 128, 128)] = wo[...]
    gather_o = ColumnGather(ring_z, c, wo_all, partner)
    gather_c.forward()
    gather_o.start()

    lane = lax.broadcasted_iota(jnp.int32, (1, 128), 1)
    head_lanes = [lane < 64, lane >= 64]

    def causal(scores, first):
        r = lax.broadcasted_iota(jnp.int32, scores.shape, 0) + first
        return jnp.where(r >= lax.broadcasted_iota(jnp.int32, scores.shape, 1), scores, MASKED)

    def masked(value, h):
        return jnp.where(head_lanes[h], value, jnp.zeros_like(value))

    def attend():
        @pl.loop(0, 2)
        def _(s):
            for qb in range(2):
                nk = 256 * (qb + 1)
                r = rows(s * 512 + qb * 256, 256)
                keys = rows(s * 512, nk, 512)
                q, k, v = qkv[r, 0:128], qkv[keys, 128:256], qkv[keys, 256:384]
                outs = []
                for h in range(2):
                    near = causal(nt(masked(q, h), k) * SCALE, qb * 256)
                    peak = jnp.max(near, axis=-1, keepdims=True)
                    near = jnp.exp(near - peak)
                    top[h, r] = peak
                    low_sum[h, r] = jnp.sum(near, axis=-1, keepdims=True)
                    outs.append(nn(near.astype(BF16), v))
                att_f[r] = jnp.where(head_lanes[0], outs[0], outs[1])

    def finish(remote):
        @pl.loop(0, 4)
        def _(i):
            r = rows(i * 256, 256)
            keys = rows((i // 2) * 512, 512)
            outs = []
            for h in range(2):
                peak, total, o = top[h, r], low_sum[h, r], att_f[r]
                if remote:
                    far = nt(masked(qkv[r, 0:128], h), kvr[keys, 0:128]) * SCALE
                    higher = jnp.maximum(peak, jnp.max(far, axis=-1, keepdims=True))
                    far = jnp.exp(far - higher)
                    shrink = jnp.exp(peak - higher)
                    total = total * shrink + jnp.sum(far, axis=-1, keepdims=True)
                    o = o * shrink + nn(far.astype(BF16), kvr[keys, 128:256])
                    peak = higher
                outs.append(o * (1.0 / total))
                lse[h, r] = peak + jnp.log(total)
            o = jnp.where(head_lanes[0], outs[0], outs[1])
            att_f[r] = o
            att[r] = o.astype(BF16)

    attend()
    gather_o.forward()
    links.settle()
    pl.when(yh == 0)(functools.partial(finish, False))

    @pl.when(yh == 1)
    def _():
        for s in range(2):
            links.wait(kv_slots + s, kvr.at[pl.ds(s * 512, 512)], {"yh": 0})
        finish(True)

    swap_a = Swap(ring_z, c, 128)
    swap_a.start(att, att_in)
    x_own = xg[own].astype(F32)
    cot_own = cotg[own].astype(F32)
    w_e.gather.forward()
    w_c.gather.forward()
    links.settle()
    gather_o.done()
    swap_a.done(att_in)
    joined = jnp.concatenate([att_in[128 * k : 128 * k + 128] for k in range(8)], axis=1)
    resid[...] = x_own + nt(joined, wo_all[...]) + off1
    normed2, inverse2 = norm_rows(resid[...])
    h2[own] = (normed2 * gain2 + off2).astype(BF16)
    gather_h = RingGather(ring_z, h2, block, 64, partner, block_partner)
    gather_h.start()
    gather_c.done()
    links.settle()
    w_e.gather.done()
    w_c.gather.done()
    vec_t[...] = jnp.transpose(vectors)
    gather_h.forward()

    hb_sum[...] = jnp.zeros_like(hb_sum)

    def mlp_tile(pos):
        near_rows, next_rows = rows(pos * 128, 128), rows(512 + pos * 128, 128)

        def load(ref):
            return jnp.concatenate([ref[near_rows], ref[next_rows]], axis=0)

        def store(ref, value):
            ref[near_rows] = value[0:128]
            ref[next_rows] = value[128:256]

        p = nn(load(h2), we[...]) + hidden_bias
        square = p * p
        t = jnp.tanh(GELU_COEF * (p + CUBIC * p * square))
        store(hid, (0.5 * p * (1.0 + t)).astype(BF16))
        slope = 0.5 * (1.0 + t) + 0.5 * p * (1.0 - t * t) * (GELU_COEF * (1.0 + 3.0 * CUBIC * square))
        g = (nn(load(cotg), wc[...]) * slope).astype(BF16)
        store(gp, g)
        hb_sum[...] += jnp.sum(g.astype(F32), axis=0, keepdims=True)
        store(part_2, nt(g, we[...]).astype(BF16))

    sum_2 = GroupSum(ring_z, c, part_2, core_2, near_2)
    sum_2.run_by_chip(mlp_tile, gather_h)

    def weight_grad(out, left, right):
        @pl.loop(0, 4)
        def _(i):
            r = rows(i * 256, 256)
            out[r] = tn(left[:, r], right[...]).astype(BF16)

    g_e = WeightSum(ring_x, me, ge, 64, land_e, landy_e)
    g_c = WeightSum(ring_x, me, gc, 64, land_c, landy_c)
    weight_grad(ge, h2, gp)
    g_e.start()
    links.settle()
    sum_2.middle()
    weight_grad(gc, cotg, hid)
    g_c.start()

    links.settle()
    grad2 = sum_2.total()
    gres[...] = cot_own + norm_back(grad2, normed2, inverse2, gain2)
    grad_branch = gres[...].astype(BF16)
    gbg[own] = grad_branch
    for k in range(4):
        g = nn(grad_branch, wo_all[:, 256 * k : 256 * k + 256]).astype(BF16)
        gatt_out[256 * k : 256 * k + 128] = g[:, 0:128]
        gatt_out[256 * k + 128 : 256 * k + 256] = g[:, 128:256]
    swap_g = Swap(ring_z, c, 128)
    swap_g.start(gatt_out, gatt)
    gather_b = RingGather(ring_z, gbg, block, 64, partner, block_partner)
    gather_b.start()
    vec[1:2] = jnp.sum(grad2 * normed2, axis=0, keepdims=True)
    vec[3:4] = jnp.sum(grad_branch.astype(F32), axis=0, keepdims=True)
    vec[4:5] = jnp.sum(grad2, axis=0, keepdims=True)
    vec[5:6] = jnp.sum(cot_own, axis=0, keepdims=True)

    def out_tile(r):
        part_o[r] = nt(hid[r], wc[...]).astype(BF16)

    sum_o = GroupSum(ring_z, c, part_o, core_o, near_o)
    sum_o.run(out_tile)
    g_e.middle()
    links.settle()
    swap_g.done(gatt)

    @pl.loop(0, 4)
    def _(i):
        r = rows(i * 256, 256)
        product = gatt[r].astype(F32) * att_f[r]
        for h in range(2):
            delta[h, r] = jnp.sum(masked(product, h), axis=-1, keepdims=True)

    gkv_slots = links.slots(2)
    gkv_copies = []
    for s in range(2):
        part = pl.ds(s * 512, 512)
        gkv_copies.append(links.make(gkv_out.at[part], gkv_in.at[part], gkv_slots + s, {"yh": 0}))
        links.keep(gkv_copies[s], yh == 1)

    def attend_far():
        @pl.loop(0, 2)
        def _(s):
            seq = rows(s * 512, 512)
            k, v = kvr[seq, 0:128], kvr[seq, 128:256]
            dk0_acc[...] = jnp.zeros_like(dk0_acc)
            dv0_acc[...] = jnp.zeros_like(dv0_acc)

            @pl.loop(0, 2)
            def _(qb):
                r = rows(s * 512 + qb * 256, 256)
                q, g = qkv[r, 0:128], gatt[r]
                outs = []
                for h in range(2):
                    qm, gm = masked(q, h), masked(g, h)
                    far = jnp.exp(nt(qm, k) * SCALE - lse[h, r])
                    far_s = (far * (nt(gm, v) - delta[h, r])).astype(BF16)
                    dk0_acc[...] += tn(far_s, qm)
                    dv0_acc[...] += tn(far.astype(BF16), gm)
                    outs.append(nn(far_s, k))
                gq_f[r] = jnp.where(head_lanes[0], outs[0], outs[1])

            gkv_out[seq, 0:128] = (dk0_acc[...] * SCALE).astype(BF16)
            gkv_out[seq, 128:256] = dv0_acc[...].astype(BF16)
            for k in range(2):
                pl.when(s == k)(gkv_copies[k].start)

    def attend_back():
        @pl.loop(0, 2)
        def _(s):
            dk_acc[...] = jnp.zeros_like(dk_acc)
            dv_acc[...] = jnp.zeros_like(dv_acc)
            seq = rows(s * 512, 512)
            for qb in range(2):
                nk = 256 * (qb + 1)
                r = rows(s * 512 + qb * 256, 256)
                keys = rows(s * 512, nk, 512)
                q, k, v, g = qkv[r, 0:128], qkv[keys, 128:256], qkv[keys, 256:384], gatt[r]
                outs = []
                for h in range(2):
                    qm, gm = masked(q, h), masked(g, h)
                    near = jnp.exp(causal(nt(qm, k) * SCALE, qb * 256) - lse[h, r])
                    near_s = (near * (nt(gm, v) - delta[h, r])).astype(BF16)
                    dk_acc[0:nk] += tn(near_s, qm)
                    dv_acc[0:nk] += tn(near.astype(BF16), gm)
                    outs.append(nn(near_s, k))
                total = gq_f[r] + jnp.where(head_lanes[0], outs[0], outs[1])
                gqkv[r, 0:128] = (total * SCALE).astype(BF16)
            gqkv[seq, 128:256] = (dk_acc[...] * SCALE).astype(BF16)
            gqkv[seq, 256:384] = dv_acc[...].astype(BF16)

    @pl.when(yh == 0)
    def _():
        gq_f[...] = jnp.zeros_like(gq_f)

    pl.when(yh == 1)(attend_far)
    gather_b.forward()
    g_c.middle()
    g_e.start_y()
    sum_o.start()
    gather_b.done()
    attend_back()
    sum_o.middle()
    weight_grad(go, gbg, att)
    g_o = WeightSum(ring_x, me, go, 64, land_o, landy_o)
    g_o.start()

    links.settle()
    @pl.when(yh == 0)
    def _():
        for s in range(2):
            links.wait(gkv_slots + s, gkv_in.at[pl.ds(s * 512, 512)], {"yh": 1})

            @pl.loop(0, 2)
            def _(k):
                r = rows(s * 512 + k * 256, 256)
                gqkv[r, 128:384] = (gqkv[r, 128:384].astype(F32) + gkv_in[r].astype(F32)).astype(BF16)

    head_sums = jnp.sum(gqkv[...].astype(F32), axis=0, keepdims=True)

    @pl.loop(0, 4)
    def _(i):
        r = rows(i * 256, 256)
        g = tn(h1[:, r], gqkv[...])
        gi[r] = g.astype(BF16)
        weight = wi[r].astype(F32)
        off_grad = jnp.sum(weight * head_sums, axis=-1, keepdims=True)
        mixed = jnp.sum(weight * g, axis=-1, keepdims=True)
        gain_grad = (mixed - vec_t[r, 2:3] * off_grad) / vec_t[r, 0:1]
        columns[r] = jnp.where(lane == 0, gain_grad, jnp.where(lane == 2, off_grad, 0.0))

    g_i = WeightSum(ring_x, me, gi, 64, land_i, landy_i)
    g_i.start()
    def grad1_tile(r):
        part_1[r] = nt(gqkv[r], wi[...]).astype(BF16)

    sum_1 = GroupSum(ring_z, c, part_1, core_1, near_1)
    sum_1.run(grad1_tile)
    sum_1.start()
    g_c.start_y()
    turned = jnp.transpose(columns[...])
    vec[0:1] = turned[0:1]
    vec[2:3] = turned[2:3]
    hb = hb_sum[...]
    vec[6:7] = jnp.concatenate([hb[:, 128 * (k // 2) : 128 * (k // 2) + 128] for k in range(8)], axis=1)
    vec[7:8] = jnp.concatenate([head_sums[:, 0:128]] * 8, axis=1)
    vec[8:9] = jnp.concatenate([head_sums[:, 256:384]] * 8, axis=1)
    vec[9:16] = jnp.zeros((7, 1024), F32)
    for k in range(16):
        gs[pl.ds(16 * k, 16)] = vec[:, 128 * (k // 2) : 128 * (k // 2) + 128].astype(BF16)
    g_s = SmallSum(ring_x, me, gs, 16, land_s, landy_s)
    g_s.start()
    links.settle()
    g_i.middle()
    g_o.middle()
    sum_1.middle()
    g_s.start_y()
    g_i.start_y()
    g_o.start_y()
    normed1, inverse1 = norm_rows(x_own)
    gtok_ref[...] = gres[...] + norm_back(sum_1.total(), normed1, inverse1, gain1)
    links.settle()
    tile = g_s.finish()
    slot = yh * 4 + z
    tens[rows(slot * 16, 16)] = tile
    mine = tens.at[rows(slot * 16, 16)]
    t_ids = links.slots(8)
    others = [(dh, dz) for dh in range(2) for dz in range(4) if dh or dz]
    for dh, dz in others:
        links.send(mine, mine, t_ids + slot, {"yh": lax.rem(yh + dh, 2), "z": lax.rem(z + dz, 4)})
    out_ref[...] = (resid[...] + sum_o.total() + off3).astype(BF16)
    gwe_ref[...] = g_e.finish()
    gwc_ref[...] = g_c.finish()
    gwo_ref[...] = g_o.finish()
    for dh, dz in others:
        theirs = lax.rem(yh + dh, 2) * 4 + lax.rem(z + dz, 4)
        ref = tens.at[rows(theirs * 16, 16)]
        links.wait(t_ids + theirs, ref, {"yh": lax.rem(yh + dh, 2), "z": lax.rem(z + dz, 4)})
    total = tens[0:16]
    for k in range(1, 8):
        total = total + tens[16 * k : 16 * k + 16]
    gsm_ref[0:6] = total[0:6]
    gsm_ref[6:16] = tile[6:16]
    gwi_ref[...] = g_i.finish()
    links.drain(len(links.open))


def final_kernel(
    out_k, gtok_k, gwi, gwo, gwe, gwc, gsm,
    out_ref, gtok_ref, gi_ref, go_ref, ge_ref, gc_ref, head_ref, hid_ref, gain_ref, off_ref,
):
    c = lax.axis_index("c")
    dp = lax.axis_index("x") * 4 + lax.axis_index("yl") * 2 + c
    out_ref[...] = out_k[...]
    gtok_ref[...] = gtok_k[...]
    for k in range(3):
        gi_ref[k] = gwi[:, 128 * k : 128 * k + 128]
    go_ref[...] = gwo[...]
    ge_ref[...] = gwe[...]
    gc_ref[...] = gwc[...]
    small = gsm[...]
    mine = pltpu.roll(small, lax.rem(128 - c * 64, 128), 1)
    gain_ref[...] = mine[0:2, 0:64]
    off_ref[...] = mine[2:6, 0:64]
    hid_ref[...] = pltpu.roll(small, lax.rem(128 - lax.rem(dp, 4) * 32, 128), 1)[6:7, 0:32]
    heads = pltpu.roll(small, lax.rem(128 - dp * 8, 128), 1)
    head_ref[0] = heads[7:8, 0:8]
    head_ref[1] = heads[8:9, 0:8]


def per_device(tokens, input_proj, output_proj, expand_proj, contract_proj, head_bias, hidden_bias, norm_gains, offsets, cotangent):
    vmem = pl.BlockSpec(memory_space=pltpu.VMEM)
    shape = jax.ShapeDtypeStruct
    widths = (384, 128, 512, 512)

    def buf(r, n, t=BF16):
        return pltpu.VMEM((r, n), t)

    scratch = [buf(1024, 1024) for _ in range(5)]
    scratch += [buf(1024, n) for n in widths] + [buf(256, 128)]
    scratch += [buf(1024, n) for n in widths] + [buf(256, 128)]
    scratch += [buf(768, n) for n in widths] + [buf(256, 128)]
    scratch += [buf(256, n) for n in widths] + [buf(64, 128)]
    scratch += [buf(1024, 1024) for _ in range(3)] + [buf(512, 1024) for _ in range(3)]
    scratch += [buf(384, 1024) for _ in range(3)]
    scratch += [buf(1024, 1024), buf(1024, 128), buf(1024, 128)]
    scratch += [buf(1024, 384), buf(1024, 384), buf(1024, 256), buf(1024, 256), buf(1024, 256)]
    scratch += [buf(1024, 128), buf(1024, 128), buf(1024, 512), buf(1024, 512)]
    scratch += [pltpu.VMEM((2, 1024, 1), F32)] + [buf(512, 128, F32) for _ in range(4)]
    scratch += [buf(128, 1024, F32), buf(128, 1024, F32), buf(16, 1024, F32), buf(128, 128, F32)]
    scratch += [buf(1, 512, F32), buf(64, 384), buf(16, 128), buf(48, 128, F32)]
    scratch += [pltpu.VMEM((2, 1024, 1), F32), pltpu.VMEM((2, 1024, 1), F32)]
    scratch += [buf(1024, 128, F32), buf(1024, 128, F32), pltpu.VMEM((2, 1024, 1), F32)]
    scratch += [buf(1024, 128, F32), buf(1024, 16, F32)]
    scratch += [pltpu.VMEM((4, 4, 64, 128), BF16), pltpu.VMEM((4, 64, 128), BF16)]
    scratch += [pltpu.SemaphoreType.DMA((SENDS,)), pltpu.SemaphoreType.DMA((RECEIVES,))]
    scratch += [pltpu.SemaphoreType.DMA((5,))]
    out, gtok, gwi, gwo, gwe, gwc, gsm = pl.pallas_call(
        layer_kernel,
        out_shape=(
            shape((128, 1024), BF16),
            shape((128, 1024), F32),
            *(shape((64, n), F32) for n in widths),
            shape((16, 128), F32),
        ),
        in_specs=[pl.BlockSpec(memory_space=pl.ANY)] * 6 + [vmem] * 4,
        out_specs=[vmem] * 7,
        scratch_shapes=scratch,
        compiler_params=pltpu.CompilerParams(
            collective_id=0, has_side_effects=True, vmem_limit_bytes=58 * 1024 * 1024
        ),
    )(
        tokens, cotangent, input_proj, output_proj.T, expand_proj, contract_proj.T,
        norm_gains, offsets, hidden_bias, head_bias.reshape(2, 8),
    )
    outs = pl.pallas_call(
        final_kernel,
        out_shape=(
            shape((128, 1024), BF16),
            shape((128, 1024), F32),
            shape((3, 64, 128), F32),
            shape((64, 128), F32),
            shape((64, 512), F32),
            shape((64, 512), F32),
            shape((2, 1, 8), F32),
            shape((1, 32), F32),
            shape((2, 64), F32),
            shape((4, 64), F32),
        ),
        in_specs=[vmem] * 7,
        out_specs=[vmem] * 10,
    )(out, gtok, gwi, gwo, gwe, gwc, gsm)
    return (*outs[:3], outs[3].T, outs[4], outs[5].T, *outs[6:])


def solution(mesh):
    split = Mesh(mesh.devices.reshape(4, 2, 2, 2, 4), ("x", "yl", "c", "yh", "z"))
    token_rows = P(DP + TENSOR, None)
    weights = (
        P(None, DP, TENSOR),
        P(TENSOR, DP),
        P(DP, TENSOR),
        P(TENSOR, DP),
        P(None, TENSOR, DP),
        P(TENSOR, DP),
        P(None, DP),
        P(None, DP),
    )
    return jax.shard_map(
        per_device,
        mesh=split,
        in_specs=(token_rows, *weights, token_rows),
        out_specs=(token_rows, token_rows, *weights),
        check_vma=False,
    )
```
